32 devices in a mesh: section: 2 (over x), dp: 8 (over z, y), tensor: 2 (over core).
Axes of the slice: x: 2, y: 2, z: 4, core: 2. Of those that a mesh axis runs over, the one named last changes fastest.
Arguments:
- text_stream: bfloat16 [2, 32, 92, 768], P('section', 'dp'), may hold values from -6 to 6
- image_stream: bfloat16 [2, 32, 100, 1024], P('section', 'dp'), may hold values from -6 to 6
- region_mask: int32 [32, 100], P('dp'), may hold values from 0 to 1, as said below
- co_text_in: bfloat16 [768, 3, 1024], P(None, None, 'tensor'), may hold values from -0.21875 to 0.21875
- co_text_out: bfloat16 [1024, 768], P('tensor'), may hold values from -0.75 to 0.75
- self_text_in: bfloat16 [768, 3, 768], P(None, None, 'tensor'), may hold values from -0.21875 to 0.21875
- self_text_out: bfloat16 [768, 768], P('tensor'), may hold values from -0.875 to 0.875
- image_attn_in: bfloat16 [2, 1024, 3, 1024], P('section', None, None, 'tensor'), may hold values from -0.1875 to 0.1875
- image_attn_out: bfloat16 [2, 1024, 1024], P('section', 'tensor'), may hold values from -0.75 to 0.75
- text_up: bfloat16 [2, 768, 3072], P('section', None, 'tensor'), may hold values from -0.21875 to 0.21875
- text_down: bfloat16 [2, 3072, 768], P('section', 'tensor'), may hold values from -0.15625 to 0.15625
- image_up: bfloat16 [2, 1024, 1024], P('section', None, 'tensor'), may hold values from -0.1875 to 0.1875
- image_down: bfloat16 [2, 1024, 1024], P('section', 'tensor'), may hold values from -0.25 to 0.25
- text_gain: float32 [2, 2, 768], P('section'), may hold values from 0.1 to 1.9
- text_shift: float32 [2, 2, 768], P('section'), may hold values from -1.5 to 1.5
- image_gain: float32 [2, 2, 1024], P('section'), may hold values from 0.1 to 1.9
- image_shift: float32 [2, 2, 1024], P('section'), may hold values from -1.5 to 1.5
Outputs:
- text_result: bfloat16 [2, 32, 92, 768], P('section', 'dp')
- image_result: bfloat16 [2, 32, 100, 1024], P('section', 'dp')
- co_text_in_grad: float32 [768, 3, 1024], P(None, None, 'tensor')
- co_text_out_grad: float32 [1024, 768], P('tensor')
- self_text_in_grad: float32 [768, 3, 768], P(None, None, 'tensor')
- self_text_out_grad: float32 [768, 768], P('tensor')
- image_attn_in_grad: float32 [2, 1024, 3, 1024], P('section', None, None, 'tensor')
- image_attn_out_grad: float32 [2, 1024, 1024], P('section', 'tensor')
- text_up_grad: float32 [2, 768, 3072], P('section', None, 'tensor')
- text_down_grad: float32 [2, 3072, 768], P('section', 'tensor')
- image_up_grad: float32 [2, 1024, 1024], P('section', None, 'tensor')
- image_down_grad: float32 [2, 1024, 1024], P('section', 'tensor')
- text_gain_grad: float32 [2, 2, 768], P('section')
- text_shift_grad: float32 [2, 2, 768], P('section')
- image_gain_grad: float32 [2, 2, 1024], P('section')
- image_shift_grad: float32 [2, 2, 1024], P('section')
The draws below stay inside these ranges and needn't reach their ends.
Inputs may be any that keep to these rules, and one draw needn't show every extreme that they name: `region_mask`: each row is 1 on a leading run of 10 to 100 region slots and 0 after it.
All inputs are finite; a program needn't handle non-finite values.
Results may differ from the reference program's by a relative error of at most 0.03.
Values may be sent and summed in bfloat16 or wider, within the bound.
No kernel may reach another device: no remote copies, remote signals or barrier semaphores. Data moves between devices by JAX's collectives and lax.ppermute only.
A program may use at most 192 MiB of HBM per device.

```python
import math
import jax
import jax.numpy as jnp
from jax import lax

D_TEXT = 768
HEADS_TEXT = 12
FF_TEXT = 3072
D_IMAGE = 1024
HEADS_IMAGE = 8
FF_IMAGE = 1024
D_CO = 1024
HEADS_CO = 8
TEXT_LEN = 92
REGIONS = 100
PAIRS = 32


def draw_region_mask(key, part):
    key = jax.random.fold_in(key, 11)
    first_key, second_key = jax.random.split(key)
    extent = REGIONS - 10
    breadth = jax.random.randint(first_key, (PAIRS,), 0, extent + 1)
    factor = jax.random.randint(second_key, (PAIRS,), 0, extent + 1)
    counts = 10 + breadth * factor // extent
    positions = jnp.arange(REGIONS, dtype=jnp.int32)
    return (positions[None, :] < counts[:, None]).astype(jnp.int32)


def block_levels(stream_key, shape, cuts, smallest, top_value):
    def one(dim, shards_of):
        draws = jax.random.uniform(jax.random.fold_in(jax.random.fold_in(stream_key, 6), dim), (shards_of,), jnp.float32, smallest / len(cuts), top_value / len(cuts))
        return jnp.repeat(jnp.exp(draws), shape[dim] // shards_of).reshape((-1,) + (1,) * (len(shape) - dim - 1))

    gain = one(*cuts[0])
    for cut in cuts[1:]:
        gain = gain * one(*cut)
    return gain


def bell_draw(stream_key, shape, width, most, pieces=(), kind=jnp.bfloat16):
    values = jax.random.normal(stream_key, shape, jnp.float32) * width
    if len(pieces) > 0:
        values = block_levels(stream_key, shape, pieces, -0.22, 0.18) * values
    return jnp.clip(values, min=-most, max=most).astype(kind)


def setup_inputs(seed: int = 0) -> dict:
    seeds = jax.random.split(jax.random.key(seed), 18)
    text_stream = bell_draw(seeds[0], (2, PAIRS, TEXT_LEN, D_TEXT), 1.0, 6.0, ((0, 2), (1, 8)))
    image_stream = bell_draw(seeds[1], (2, PAIRS, REGIONS, D_IMAGE), 1.0, 6.0, ((0, 2), (1, 8)))
    region_mask = draw_region_mask(jax.random.fold_in(seeds[17], 71), 0)
    co_text_in = bell_draw(seeds[3], (D_TEXT, 3, D_CO), D_TEXT ** -0.5, 0.21875, ((2, 2),))
    co_text_out = bell_draw(seeds[4], (D_CO, D_TEXT), (D_CO // 16) ** -0.5, 0.75, ((0, 2),))
    self_text_in = bell_draw(seeds[5], (D_TEXT, 3, D_TEXT), D_TEXT ** -0.5, 0.21875, ((2, 2),))
    self_text_out = bell_draw(seeds[6], (D_TEXT, D_TEXT), (D_TEXT // 16) ** -0.5, 0.875, ((0, 2),))
    image_attn_in = bell_draw(seeds[7], (2, D_IMAGE, 3, D_CO), D_IMAGE ** -0.5, 0.1875, ((0, 2), (3, 2)))
    image_attn_out = bell_draw(seeds[8], (2, D_CO, D_IMAGE), (D_CO // 16) ** -0.5, 0.75, ((0, 2), (1, 2)))
    text_up = bell_draw(seeds[9], (2, D_TEXT, FF_TEXT), D_TEXT ** -0.5, 0.21875, ((0, 2), (2, 2)))
    text_down = bell_draw(seeds[10], (2, FF_TEXT, D_TEXT), (FF_TEXT // 2) ** -0.5, 0.15625, ((0, 2), (1, 2)))
    image_up = bell_draw(seeds[11], (2, D_IMAGE, FF_IMAGE), D_IMAGE ** -0.5, 0.1875, ((0, 2), (2, 2)))
    image_down = bell_draw(seeds[12], (2, FF_IMAGE, D_IMAGE), (FF_IMAGE // 2) ** -0.5, 0.25, ((0, 2), (1, 2)))
    text_gain = jnp.clip(1.0 + 0.18 * jax.random.normal(seeds[13], (2, 2, D_TEXT), jnp.float32), 0.1, 1.9)
    text_shift = bell_draw(seeds[14], (2, 2, D_TEXT), 0.3, 1.5, ((0, 2),), jnp.float32)
    image_gain = jnp.clip(1.0 + 0.18 * jax.random.normal(seeds[15], (2, 2, D_IMAGE), jnp.float32), 0.1, 1.9)
    image_shift = bell_draw(seeds[16], (2, 2, D_IMAGE), 0.3, 1.5, ((0, 2),), jnp.float32)
    return {"text_stream": text_stream, "image_stream": image_stream, "region_mask": region_mask, "co_text_in": co_text_in, "co_text_out": co_text_out, "self_text_in": self_text_in, "self_text_out": self_text_out, "image_attn_in": image_attn_in, "image_attn_out": image_attn_out, "text_up": text_up, "text_down": text_down, "image_up": image_up, "image_down": image_down, "text_gain": text_gain, "text_shift": text_shift, "image_gain": image_gain, "image_shift": image_shift}


@jax.custom_vjp
def low(v):
    return lax.optimization_barrier(v.astype(jnp.bfloat16)).astype(jnp.float32)

@jax.custom_vjp
def low_back(v):
    return v

def low_keep(v):
    return (low(v), None)

def low_pass(kept, grad):
    return (grad,)

def back_keep(v):
    return (v, None)

def back_low(kept, grad):
    return (low(grad),)
low.defvjp(low_keep, low_pass)
low_back.defvjp(back_keep, back_low)

def project(values, weight):
    return jnp.einsum('pld,de->ple', values, weight, precision=lax.Precision.HIGHEST)

def project_three(values, weight):
    return jnp.einsum('pld,dce->plce', values, weight, precision=lax.Precision.HIGHEST)

def layer_norm(rows, scaling, offset):
    centre = rows - lax.optimization_barrier(jnp.mean(rows, axis=-1, keepdims=True))
    spread = lax.optimization_barrier(jnp.mean(centre * centre, axis=-1, keepdims=True))
    return centre * lax.rsqrt(spread + 1e-05) * scaling + offset

def gelu_tanh(inputs):
    return 0.5 * inputs * (1.0 + jnp.tanh(0.7978845608028654 * (inputs + 0.044715 * inputs * inputs * inputs)))

def attend(query, keys, values, keeping, head_size):
    pairs_here = query.shape[0]
    rows_here = query.shape[1]
    queries = query.reshape(pairs_here, rows_here, -1, head_size)
    keyed = keys.reshape(pairs_here, keys.shape[1], -1, head_size)
    valued = values.reshape(pairs_here, values.shape[1], -1, head_size)
    scores = jnp.einsum('pqhd,pkhd->phqk', queries, keyed, precision=lax.Precision.HIGHEST)
    scores = low_back(scores * (1.0 / math.sqrt(head_size)))
    scores = jnp.where(keeping[:, None, None, :], scores, -1000000000.0)
    highest = lax.optimization_barrier(jnp.max(scores, axis=-1, keepdims=True))
    raised = jnp.exp(scores - highest)
    attention = low(raised / lax.optimization_barrier(jnp.sum(raised, axis=-1, keepdims=True)))
    context = jnp.einsum('phqk,pkhd->pqhd', attention, valued, precision=lax.Precision.HIGHEST)
    return low_back(low(context.reshape(pairs_here, rows_here, -1)))

def stream_tail(residual, context, out_weight, scaling, offset, up_weight, down_weight):
    branch = low_back(project(context, out_weight))
    normed = layer_norm(residual + branch, scaling[0], offset[0])
    upward = low_back(project(low(normed), up_weight))
    mixture = low_back(project(low(gelu_tanh(upward)), down_weight))
    return layer_norm(normed + mixture, scaling[1], offset[1])

def co_block(text_values, image_values, keeping, params):
    cross_in, cross_out, single_in, single_out, attn_in, attn_out, up_text, down_text, up_image, down_image, gain_text, shift_text, gain_image, shift_image = params
    text_all = jnp.ones((text_values.shape[0], text_values.shape[1]), dtype=bool)
    text_proj = low_back(low(project_three(text_values, cross_in)))
    image_proj = low_back(low(project_three(image_values, attn_in[0])))
    text_context = attend(text_proj[:, :, 0], image_proj[:, :, 1], image_proj[:, :, 2], keeping, D_CO // HEADS_CO)
    image_context = attend(image_proj[:, :, 0], text_proj[:, :, 1], text_proj[:, :, 2], text_all, D_CO // HEADS_CO)
    text_after = stream_tail(text_values, text_context, cross_out, gain_text[0], shift_text[0], up_text[0], down_text[0])
    image_after = stream_tail(image_values, image_context, attn_out[0], gain_image[0], shift_image[0], up_image[0], down_image[0])
    return (text_after, image_after)

def self_block(text_values, image_values, keeping, params):
    cross_in, cross_out, single_in, single_out, attn_in, attn_out, up_text, down_text, up_image, down_image, gain_text, shift_text, gain_image, shift_image = params
    text_all = jnp.ones((text_values.shape[0], text_values.shape[1]), dtype=bool)
    text_proj = low_back(low(project_three(text_values, single_in)))
    image_proj = low_back(low(project_three(image_values, attn_in[1])))
    text_context = attend(text_proj[:, :, 0], text_proj[:, :, 1], text_proj[:, :, 2], text_all, D_TEXT // HEADS_TEXT)
    image_context = attend(image_proj[:, :, 0], image_proj[:, :, 1], image_proj[:, :, 2], keeping, D_IMAGE // HEADS_IMAGE)
    text_after = stream_tail(text_values, text_context, single_out, gain_text[1], shift_text[1], up_text[1], down_text[1])
    image_after = stream_tail(image_values, image_context, attn_out[1], gain_image[1], shift_image[1], up_image[1], down_image[1])
    return (text_after, image_after)

def reference(text_stream, image_stream, region_mask, co_text_in, co_text_out, self_text_in, self_text_out, image_attn_in, image_attn_out, text_up, text_down, image_up, image_down, text_gain, text_shift, image_gain, image_shift):
    keeping = region_mask > 0
    weights = tuple((argument.astype(jnp.float32) for argument in (co_text_in, co_text_out, self_text_in, self_text_out, image_attn_in, image_attn_out, text_up, text_down, image_up, image_down, text_gain, text_shift, image_gain, image_shift)))

    def forward(text_values, image_values, *params):
        first_text, first_image = co_block(text_values, image_values, keeping, params)
        return self_block(low_back(low(first_text)), low_back(low(first_image)), keeping, params)
    outputs, pullback = jax.vjp(forward, text_stream[0].astype(jnp.float32), image_stream[0].astype(jnp.float32), *weights)
    gradients = pullback((text_stream[1].astype(jnp.float32), image_stream[1].astype(jnp.float32)))
    text_result = jnp.stack([gradients[0], outputs[0]]).astype(jnp.bfloat16)
    image_result = jnp.stack([gradients[1], outputs[1]]).astype(jnp.bfloat16)
    return (text_result, image_result, gradients[2], gradients[3], gradients[4], gradients[5], gradients[6], gradients[7], gradients[8], gradients[9], gradients[10], gradients[11], gradients[12], gradients[13], gradients[14], gradients[15])
```

```python
import math

import jax
import jax.numpy as jnp
from jax import lax
from jax.sharding import PartitionSpec as P

D_TEXT = 768
HEADS_TEXT = 12
D_IMAGE = 1024
HEADS_IMAGE = 8
D_CO = 1024
HEADS_CO = 8

LOW = jnp.bfloat16
FULL = jnp.float32


def dot(spec, left, right):
    return jnp.einsum(spec, left, right, preferred_element_type=FULL)


def norm_parts(rows):
    centre = rows - jnp.mean(rows, axis=-1, keepdims=True)
    spread = jnp.mean(centre * centre, axis=-1, keepdims=True)
    inverse = lax.rsqrt(spread + 1e-05)
    return centre * inverse, inverse


def norm_back(unit, inverse, gain, grad):
    scaled = grad * gain
    first = jnp.mean(scaled, axis=-1, keepdims=True)
    second = jnp.mean(scaled * unit, axis=-1, keepdims=True)
    dgain = jnp.sum(grad * unit, axis=(0, 1))
    dshift = jnp.sum(grad, axis=(0, 1))
    return inverse * (scaled - first - unit * second), dgain, dshift


def gelu_both(inputs):
    rate = 0.7978845608028654
    bent = jnp.tanh(rate * (inputs + 0.044715 * inputs * inputs * inputs))
    value = 0.5 * inputs * (1.0 + bent)
    slope = 0.5 * (1.0 + bent) + 0.5 * inputs * (1.0 - bent * bent) * rate * (
        1.0 + 0.134145 * inputs * inputs
    )
    return value, slope


def heads_of(values, size):
    return values.reshape(values.shape[0], values.shape[1], values.shape[2] // size, size)


def attend(query, keys, values, keeping, size):
    scaling = 1.0 / math.sqrt(size)
    scores = dot("pqhd,pkhd->phqk", heads_of(query, size), heads_of(keys, size)) * scaling
    if keeping is not None:
        scores = jnp.where(keeping[:, None, None, :], scores, -1000000000.0)
    highest = jnp.max(scores, axis=-1, keepdims=True)
    raised = jnp.exp(scores - highest)
    weight = raised / jnp.sum(raised, axis=-1, keepdims=True)
    context = dot("phqk,pkhd->pqhd", weight.astype(LOW), heads_of(values, size))
    return context.reshape(query.shape).astype(LOW), weight


def attend_back(query, keys, values, weight, size, dcontext):
    scaling = 1.0 / math.sqrt(size)
    queries, keyed = heads_of(query, size), heads_of(keys, size)
    valued, dheads = heads_of(values, size), heads_of(dcontext, size)
    dvalues = dot("phqk,pqhd->pkhd", weight.astype(LOW), dheads)
    dweight = dot("pqhd,pkhd->phqk", dheads, valued)
    dscores = weight * (dweight - jnp.sum(dweight * weight, axis=-1, keepdims=True))
    dscores = dscores.astype(LOW)
    dquery = dot("phqk,pkhd->pqhd", dscores, keyed) * scaling
    dkeys = dot("phqk,pqhd->pkhd", dscores, queries) * scaling
    return (
        dquery.reshape(query.shape).astype(LOW),
        dkeys.reshape(keys.shape).astype(LOW),
        dvalues.reshape(values.shape).astype(LOW),
    )


def project(values, weights):
    return [dot("pld,dce->cple", values, half).astype(LOW) for half in weights]


def project_back(grads, weights):
    return sum(dot("cple,dce->pld", grad, half) for grad, half in zip(grads, weights))


def tail(residual, contexts, out_w, gain, shift, up_w, down_w):
    branch = sum(dot("ple,ed->pld", c, w) for c, w in zip(contexts, out_w))
    unit1, inv1 = norm_parts(residual.astype(FULL) + branch)
    normed = unit1 * gain[0] + shift[0]
    low_normed = normed.astype(LOW)
    uppers = [dot("pld,df->plf", low_normed, w) for w in up_w]
    both = [gelu_both(u) for u in uppers]
    hidden = [value.astype(LOW) for value, unused in both]
    mixed = sum(dot("plf,fd->pld", h, w) for h, w in zip(hidden, down_w))
    unit2, inv2 = norm_parts(normed + mixed)
    out = unit2 * gain[1] + shift[1]
    kept = (unit1, inv1, low_normed, [slope for unused, slope in both], hidden, unit2, inv2)
    return out, kept


def tail_back(kept, seed, out_w, gain, up_w, down_w):
    unit1, inv1, low_normed, slopes, hidden, unit2, inv2 = kept
    dsecond, dgain1, dshift1 = norm_back(unit2, inv2, gain[1], seed)
    dmixed = dsecond.astype(LOW)
    duppers = [
        (dot("pld,fd->plf", dmixed, w) * slope).astype(LOW) for w, slope in zip(down_w, slopes)
    ]
    dnormed = dsecond + sum(dot("plf,df->pld", du, w) for du, w in zip(duppers, up_w))
    dfirst, dgain0, dshift0 = norm_back(unit1, inv1, gain[0], dnormed)
    dbranch = dfirst.astype(LOW)
    dcontexts = [dot("pld,ed->ple", dbranch, w).astype(LOW) for w in out_w]
    gains = (jnp.stack([dgain0, dgain1]), jnp.stack([dshift0, dshift1]))
    return dfirst, dcontexts, (dmixed, duppers, dbranch), gains


def pair_up(weight, core_route):
    return [weight, lax.ppermute(weight, "tensor", core_route)]


def bit_route(axis, bit):
    return [(i, i ^ (1 << bit)) for i in range(lax.axis_size(axis))]


def scatter_sum(block, order):
    place = lax.axis_index("dp")
    for bit in order:
        high = (place >> bit) & 1
        halves = block.reshape((2, block.shape[0] // 2) + block.shape[1:])
        keep = lax.dynamic_index_in_dim(halves, high, 0, keepdims=False)
        give = lax.dynamic_index_in_dim(halves, 1 - high, 0, keepdims=False)
        got = lax.ppermute(give, "dp", bit_route("dp", bit))
        block = (keep.astype(FULL) + got.astype(FULL)).astype(LOW)
    return block


def gather_back(block, order):
    place = lax.axis_index("dp")
    for bit in reversed(order):
        high = ((place >> bit) & 1) == 1
        got = lax.ppermute(block, "dp", bit_route("dp", bit))
        block = jnp.concatenate([jnp.where(high, got, block), jnp.where(high, block, got)], axis=0)
    return block


def shards(
    text_stream,
    image_stream,
    region_mask,
    co_text_in,
    co_text_out,
    self_text_in,
    self_text_out,
    image_attn_in,
    image_attn_out,
    text_up,
    text_down,
    image_up,
    image_down,
    text_gain,
    text_shift,
    image_gain,
    image_shift,
):
    front = lax.axis_index("section") == 0
    core = lax.axis_index("tensor")
    core_route = [(0, 1), (1, 0)]
    pairs = text_stream.shape[1] // 2
    own = lambda values: lax.dynamic_slice_in_dim(values, core * pairs, pairs, 0)
    co_size = D_CO // HEADS_CO
    text_size = D_TEXT // HEADS_TEXT
    image_size = D_IMAGE // HEADS_IMAGE
    text_own = own(text_stream[0])
    image_own = own(image_stream[0])
    keeping = own(region_mask) > 0
    gain_t, shift_t, gain_i, shift_i = text_gain[0], text_shift[0], image_gain[0], image_shift[0]
    image_in = pair_up(image_attn_in[0], core_route)
    cross_in = pair_up(co_text_in, core_route)
    image_out = pair_up(image_attn_out[0], core_route)
    cross_out = pair_up(co_text_out, core_route)
    up_t = pair_up(text_up[0], core_route)
    down_t = pair_up(text_down[0], core_route)
    up_i = pair_up(image_up[0], core_route)
    down_i = pair_up(image_down[0], core_route)
    single_in = pair_up(self_text_in, core_route)
    single_out = pair_up(self_text_out, core_route)

    tp1 = project(text_own, cross_in)
    ip1 = project(image_own, image_in)
    ct1, wt1 = zip(*[attend(t[0], i[1], i[2], keeping, co_size) for t, i in zip(tp1, ip1)])
    ci1, wi1 = zip(*[attend(i[0], t[1], t[2], None, co_size) for t, i in zip(tp1, ip1)])
    out_t1, kept_t1 = tail(text_own, ct1, cross_out, gain_t, shift_t, up_t, down_t)
    out_i1, kept_i1 = tail(image_own, ci1, image_out, gain_i, shift_i, up_i, down_i)
    bt = lax.ppermute(out_t1.astype(LOW), "section", core_route)
    bi = lax.ppermute(out_i1.astype(LOW), "section", core_route)

    tp2 = project(bt, single_in)
    ip2 = project(bi, image_in)
    ct2, wt2 = zip(*[attend(t[0], t[1], t[2], None, text_size) for t in tp2])
    ci2, wi2 = zip(*[attend(i[0], i[1], i[2], keeping, image_size) for i in ip2])
    out_t2, kept_t2 = tail(bt, ct2, single_out, gain_t, shift_t, up_t, down_t)
    out_i2, kept_i2 = tail(bi, ci2, image_out, gain_i, shift_i, up_i, down_i)
    dres_t2, dct2, grads_t2, gains_t2 = tail_back(
        kept_t2, text_own.astype(FULL), single_out, gain_t, up_t, down_t
    )
    dres_i2, dci2, grads_i2, gains_i2 = tail_back(
        kept_i2, image_own.astype(FULL), image_out, gain_i, up_i, down_i
    )
    dtp2 = [
        jnp.stack(attend_back(t[0], t[1], t[2], w, text_size, dc))
        for t, w, dc in zip(tp2, wt2, dct2)
    ]
    dip2 = [
        jnp.stack(attend_back(i[0], i[1], i[2], w, image_size, dc))
        for i, w, dc in zip(ip2, wi2, dci2)
    ]
    dbt = (dres_t2 + project_back(dtp2, single_in)).astype(LOW)
    dbi = (dres_i2 + project_back(dip2, image_in)).astype(LOW)
    seed_t = lax.ppermute(dbt, "section", core_route).astype(FULL)
    seed_i = lax.ppermute(dbi, "section", core_route).astype(FULL)

    dres_t1, dct1, grads_t1, gains_t1 = tail_back(kept_t1, seed_t, cross_out, gain_t, up_t, down_t)
    dres_i1, dci1, grads_i1, gains_i1 = tail_back(kept_i1, seed_i, image_out, gain_i, up_i, down_i)
    dtp1, dip1 = [], []
    for half in range(2):
        t, i = tp1[half], ip1[half]
        tq, ik, iv = attend_back(t[0], i[1], i[2], wt1[half], co_size, dct1[half])
        iq, tk, tv = attend_back(i[0], t[1], t[2], wi1[half], co_size, dci1[half])
        dtp1.append(jnp.stack([tq, tk, tv]))
        dip1.append(jnp.stack([iq, ik, iv]))
    dxt = dres_t1 + project_back(dtp1, cross_in)
    dxi = dres_i1 + project_back(dip1, image_in)

    def choose(first, second):
        return jnp.where(front, first, second)

    def padded(values, like):
        grow = [(0, 0)] * (values.ndim - 1) + [(0, like.shape[-1] - values.shape[-1])]
        return jnp.pad(values, grow)

    def crossed(mine, given):
        return jnp.concatenate([mine, lax.ppermute(given, "tensor", core_route)], axis=-3)

    def split_factor(halves):
        return crossed(halves[0], halves[1])

    def whole_factor(values):
        return crossed(values, values)

    def select_halves(first, second):
        return [choose(a, padded(b, a)) for a, b in zip(first, second)]

    df_t, du_t, da_t = [
        select_halves(a, b) if isinstance(a, list) else choose(a, b)
        for a, b in zip(grads_t1, grads_t2)
    ]
    df_i, du_i, da_i = [
        select_halves(a, b) if isinstance(a, list) else choose(a, b)
        for a, b in zip(grads_i1, grads_i2)
    ]
    y_t, y_i = choose(kept_t1[2], kept_t2[2]), choose(kept_i1[2], kept_i2[2])
    hid_t = select_halves(kept_t1[4], kept_t2[4])
    hid_i = select_halves(kept_i1[4], kept_i2[4])
    c_t = select_halves(ct1, ct2)
    c_i = select_halves(ci1, ci2)
    dtp = select_halves(dtp1, dtp2)
    dip = select_halves(dip1, dip2)
    x_t, x_i = choose(text_own, bt), choose(image_own, bi)

    plain = "pla,plb->ab"
    y_order = tuple(range(lax.axis_size("dp").bit_length() - 1))
    z_order = y_order[1:] + y_order[:1]
    pieces = {}
    pieces["down_t"] = (dot(plain, split_factor(hid_t), whole_factor(df_t)), y_order)
    pieces["up_t"] = (dot(plain, whole_factor(y_t), split_factor(du_t)), y_order)
    pieces["down_i"] = (dot(plain, split_factor(hid_i), whole_factor(df_i)), y_order)
    pieces["up_i"] = (dot(plain, whole_factor(y_i), split_factor(du_i)), z_order)
    pieces["out_t"] = (dot(plain, split_factor(c_t), whole_factor(da_t)), y_order)
    pieces["out_i"] = (dot(plain, split_factor(c_i), whole_factor(da_i)), z_order)
    pieces["in_t"] = (dot("pla,cplb->acb", whole_factor(x_t), split_factor(dtp)), y_order)
    pieces["in_i"] = (dot("pla,cplb->acb", whole_factor(x_i), split_factor(dip)), y_order)
    sums = {
        name: scatter_sum(value.astype(LOW), order) for name, (value, order) in pieces.items()
    }
    wholes = {}
    for name in ("in_t", "out_t", "in_i", "out_i", "down_t", "up_t", "down_i", "up_i"):
        wholes[name] = gather_back(sums[name], pieces[name][1])
    in_t, out_t = wholes["in_t"], wholes["out_t"]
    other_in = lax.ppermute(in_t, "section", core_route)
    other_out = lax.ppermute(out_t, "section", core_route)
    single_width = self_text_in.shape[2]
    co_in_grad = choose(in_t, other_in).astype(FULL)
    co_out_grad = choose(out_t, other_out).astype(FULL)
    self_in_grad = choose(other_in, in_t)[:, :, :single_width].astype(FULL)
    self_out_grad = choose(other_out, out_t)[:single_width].astype(FULL)

    small = [choose(a, b) for a, b in zip(gains_t1 + gains_i1, gains_t2 + gains_i2)]
    widths = [value.shape[1] for value in small]
    flat = jnp.concatenate(small, axis=1)
    flat = flat + lax.ppermute(flat, "tensor", core_route)
    for bit in y_order:
        flat = flat + lax.ppermute(flat, "dp", bit_route("dp", bit))
    starts = [sum(widths[:n]) for n in range(4)]
    small = [flat[:, s : s + w] for s, w in zip(starts, widths)]

    def joined(values):
        values = values.astype(LOW)
        got = lax.ppermute(values, "tensor", core_route)
        low = core == 0
        return jnp.concatenate([jnp.where(low, values, got), jnp.where(low, got, values)], axis=0)

    text_result = joined(choose(dxt, out_t2))
    image_result = joined(choose(dxi, out_i2))
    return (
        text_result[None],
        image_result[None],
        co_in_grad,
        co_out_grad,
        self_in_grad,
        self_out_grad,
        wholes["in_i"].astype(FULL)[None],
        wholes["out_i"].astype(FULL)[None],
        wholes["up_t"].astype(FULL)[None],
        wholes["down_t"].astype(FULL)[None],
        wholes["up_i"].astype(FULL)[None],
        wholes["down_i"].astype(FULL)[None],
        small[0][None],
        small[1][None],
        small[2][None],
        small[3][None],
    )


def solution(mesh):
    in_specs = (
        P("section", "dp", None, None),
        P("section", "dp", None, None),
        P("dp", None),
        P(None, None, "tensor"),
        P("tensor", None),
        P(None, None, "tensor"),
        P("tensor", None),
        P("section", None, None, "tensor"),
        P("section", "tensor", None),
        P("section", None, "tensor"),
        P("section", "tensor", None),
        P("section", None, "tensor"),
        P("section", "tensor", None),
        P("section", None, None),
        P("section", None, None),
        P("section", None, None),
        P("section", None, None),
    )
    out_specs = (
        P("section", "dp", None, None),
        P("section", "dp", None, None),
        P(None, None, "tensor"),
        P("tensor", None),
        P(None, None, "tensor"),
        P("tensor", None),
        P("section", None, None, "tensor"),
        P("section", "tensor", None),
        P("section", None, "tensor"),
        P("section", "tensor", None),
        P("section", None, "tensor"),
        P("section", "tensor", None),
        P("section", None, None),
        P("section", None, None),
        P("section", None, None),
        P("section", None, None),
    )
    return jax.shard_map(shards, mesh=mesh, in_specs=in_specs, out_specs=out_specs, check_vma=False)
```

```python
import functools
import math

import jax
import jax.numpy as jnp
from jax import lax
from jax.experimental import pallas as pl
from jax.experimental.pallas import tpu as pltpu
from jax.sharding import PartitionSpec as P

D_TEXT = 768
HEADS_TEXT = 12
D_IMAGE = 1024
HEADS_IMAGE = 8
D_CO = 1024
HEADS_CO = 8

LOW = jnp.bfloat16
FULL = jnp.float32
TILE = 512
UNIT = 256
ROOM = 56 * 1024 * 1024


def times(left, right):
    return jnp.dot(left, right, preferred_element_type=FULL)


def times_back(left, right):
    return lax.dot_general(left, right, (((1,), (1,)), ((), ())), preferred_element_type=FULL)


def back_times(left, right):
    return lax.dot_general(left, right, (((0,), (0,)), ((), ())), preferred_element_type=FULL)


def norm_rows(rows):
    centre = rows - jnp.mean(rows, axis=-1, keepdims=True)
    spread = jnp.mean(centre * centre, axis=-1, keepdims=True)
    inverse = lax.rsqrt(spread + 1e-05)
    return centre * inverse, inverse


def norm_back(unit, inverse, gain, grad):
    scaled = grad * gain
    first = jnp.mean(scaled, axis=-1, keepdims=True)
    second = jnp.mean(scaled * unit, axis=-1, keepdims=True)
    dgain = jnp.sum(grad * unit, axis=0, keepdims=True)
    dshift = jnp.sum(grad, axis=0, keepdims=True)
    return inverse * (scaled - first - unit * second), dgain, dshift


def gelu_both(inputs):
    rate = 0.7978845608028654
    square = inputs * inputs
    bent = jnp.tanh(rate * inputs * (1.0 + 0.044715 * square))
    half = 0.5 * (1.0 + bent)
    slope = half + 0.5 * inputs * (1.0 - bent * bent) * rate * (1.0 + 0.134145 * square)
    return inputs * half, slope


def softmax_of(query, keys, allowed, size):
    scores = times_back(query, keys) * (1.0 / math.sqrt(size))
    scores = jnp.where(allowed, scores, -1000000000.0)
    raised = jnp.exp(scores - jnp.max(scores, axis=-1, keepdims=True))
    return raised / jnp.sum(raised, axis=-1, keepdims=True)


def attend(query, keys, values, allowed, size):
    if size == query.shape[1]:
        weight = softmax_of(query, keys, allowed, size)
        return times(weight.astype(LOW), values).astype(LOW)
    lower = lax.broadcasted_iota(jnp.int32, query.shape, 1) < size
    nothing = jnp.zeros_like(query)
    parts = []
    for mine in (jnp.where(lower, query, nothing), jnp.where(lower, nothing, query)):
        weight = softmax_of(mine, keys, allowed, size)
        parts.append(times(weight.astype(LOW), values))
    return jnp.where(lower, parts[0], parts[1]).astype(LOW)


def attend_back(query, keys, values, allowed, size, dcontext):
    scaling = 1.0 / math.sqrt(size)

    def one(masked_query, masked_dcontext):
        weight = softmax_of(masked_query, keys, allowed, size)
        dvalues = back_times(weight.astype(LOW), dcontext)
        dweight = times_back(masked_dcontext, values)
        dscores = weight * (dweight - jnp.sum(dweight * weight, axis=-1, keepdims=True))
        dscores = dscores.astype(LOW)
        return times(dscores, keys) * scaling, back_times(dscores, query) * scaling, dvalues

    if size == query.shape[1]:
        results = one(query, dcontext)
    else:
        results = []
        low_q = lax.broadcasted_iota(jnp.int32, query.shape, 1) < size
        low_k = lax.broadcasted_iota(jnp.int32, keys.shape, 1) < size
        zero_q = jnp.zeros_like(query)
        first = one(jnp.where(low_q, query, zero_q), jnp.where(low_q, dcontext, zero_q))
        second = one(jnp.where(low_q, zero_q, query), jnp.where(low_q, zero_q, dcontext))
        for lower, a, b in zip((low_q, low_k, low_k), first, second):
            results.append(jnp.where(lower, a, b))
    return [value.astype(LOW) for value in results]


def wide(column):
    return jnp.broadcast_to(column, (column.shape[0], 128))


def tail_forward(residual, contexts, out_w, gain, shift, up_w, down_w, kept, mixed):
    normed_ref, hidden, slopes, unit1, inv1, unit2, inv2 = kept
    branch = times(contexts[0], out_w[0][...]) + times(contexts[1], out_w[1][...])
    unit, inverse = norm_rows(residual.astype(FULL) + branch)
    unit1[...] = unit
    inv1[...] = wide(inverse)
    normed = unit * gain[0:1, :] + shift[0:1, :]
    normed_ref[...] = normed.astype(LOW)
    mixed[...] = normed
    for half in range(2):
        width = up_w[half].shape[1]
        for start in range(0, width, TILE):
            span = pl.ds(start, TILE)
            value, slope = gelu_both(times(normed_ref[...], up_w[half][:, span]))
            hidden[half][:, span] = value.astype(LOW)
            slopes[half][:, span] = slope
            mixed[...] += times(hidden[half][:, span], down_w[half][span, :])
    unit, inverse = norm_rows(mixed[...])
    unit2[...] = unit
    inv2[...] = wide(inverse)
    return unit * gain[1:2, :] + shift[1:2, :]


def tail_backward(seed, kept, out_w, gain, up_w, down_w, grads, total):
    slopes, unit1, inv1, unit2, inv2 = kept
    df, du, da, dgain, dshift = grads
    dsecond, dgain1, dshift1 = norm_back(unit2[...], inv2[:, 0:1], gain[1:2, :], seed)
    total[...] = dsecond
    df[...] = dsecond.astype(LOW)
    for half in range(2):
        width = up_w[half].shape[1]
        for start in range(0, width, TILE):
            span = pl.ds(start, TILE)
            dhidden = times_back(df[...], down_w[half][span, :])
            du[half][:, span] = (dhidden * slopes[half][:, span]).astype(LOW)
            total[...] += times_back(du[half][:, span], up_w[half][:, span])
    dfirst, dgain0, dshift0 = norm_back(unit1[...], inv1[:, 0:1], gain[0:1, :], total[...])
    dgain[...] = jnp.concatenate([dgain0, dgain1], axis=0)
    dshift[...] = jnp.concatenate([dshift0, dshift1], axis=0)
    total[...] = dfirst
    da[...] = dfirst.astype(LOW)
    return [times_back(da[...], w[...]).astype(LOW) for w in out_w]


def shape_of(rows, columns, kind=LOW):
    return jax.ShapeDtypeStruct((rows, columns), kind)


def launch(body, outputs, args, scratch=(), flag=None, work=0, name=None):
    whole = pl.BlockSpec(memory_space=pltpu.VMEM)
    moved = sum(math.prod(v.shape) * v.dtype.itemsize for v in tuple(args) + tuple(outputs))
    specs = [whole] * len(args)
    if flag is not None:
        specs = [pl.BlockSpec(memory_space=pltpu.SMEM)] + specs
        args = (flag,) + tuple(args)
    return pl.pallas_call(
        body,
        out_shape=tuple(outputs),
        in_specs=specs,
        out_specs=tuple([whole] * len(outputs)),
        scratch_shapes=list(scratch),
        compiler_params=pltpu.CompilerParams(vmem_limit_bytes=ROOM),
        cost_estimate=pl.CostEstimate(flops=work, bytes_accessed=moved, transcendentals=0),
        name=name,
    )(*args)


def rows_at(pair, rows):
    return pl.ds(pl.multiple_of(pair * rows, 16), rows)


def slab(index):
    return pl.ds(index * 128, 128)


def cross_forward(pairs, rows_t, rows_i, real_t, xt, xi, wt, wi, keep, tp, ip, ct, ci):
    width = ct.shape[1]
    for slot in range(3):
        span = pl.ds(slot * width, width)
        tp[:, span] = times(xt[...], wt[:, span]).astype(LOW)
        ip[:, span] = times(xi[...], wi[:, span]).astype(LOW)
    text_keys = lax.broadcasted_iota(jnp.int32, (1, rows_t), 1) < real_t
    slabs = width // 128

    def each(pair, carry):
        at_t, at_i = rows_at(pair, rows_t), rows_at(pair, rows_i)
        kept = keep[pair] > 0
        for n in range(slabs):
            ct[at_t, slab(n)] = attend(
                tp[at_t, slab(n)], ip[at_i, slab(slabs + n)], ip[at_i, slab(2 * slabs + n)], kept, 128
            )
            ci[at_i, slab(n)] = attend(
                ip[at_i, slab(n)],
                tp[at_t, slab(slabs + n)],
                tp[at_t, slab(2 * slabs + n)],
                text_keys,
                128,
            )
        return carry

    lax.fori_loop(0, pairs, each, 0)


def first_tail(x, c0, c1, o0, o1, gain, shift, u0, u1, d0, d1, out, y, h0, h1, s0, s1, n1, i1, n2, i2, mixed):
    kept = (y, (h0, h1), (s0, s1), n1, i1, n2, i2)
    out[...] = tail_forward(
        x[...], (c0[...], c1[...]), (o0, o1), gain, shift, (u0, u1), (d0, d1), kept, mixed
    ).astype(LOW)


def self_layer(
    pairs, rows, real, size, stride, front,
    x, w0, w1, keep, o0, o1, gain, shift, u0, u1, d0, d1, seed, y_in, h0_in, h1_in, c_in,
    out, dx, c0, c1, p0, p1, da, df, du0, du1, y, h0, h1, dgain, dshift,
    q0, q1, s0, s1, n1, i1, n2, i2, mixed, dc0, dc1,
):
    width = w0.shape[1] // 3

    @pl.when(front[0] == 1)
    def pass_on():
        y[...] = y_in[...]
        h0[...] = h0_in[...]
        h1[...] = h1_in[...]
        c0[...] = c_in[...]

    @pl.when(front[0] == 0)
    def work():
        slabs = width // 128
        if c0.shape[1] != width:
            rest = pl.ds(width, c0.shape[1] - width)
            c0[:, rest] = jnp.zeros((c0.shape[0], c0.shape[1] - width), LOW)
            c1[:, rest] = jnp.zeros((c0.shape[0], c0.shape[1] - width), LOW)
            for slot in range(3):
                rest = pl.ds(slot * stride + width, stride - width)
                p0[:, rest] = jnp.zeros((p0.shape[0], stride - width), LOW)
                p1[:, rest] = jnp.zeros((p0.shape[0], stride - width), LOW)
        for w, q in ((w0, q0), (w1, q1)):
            for slot in range(3):
                span = pl.ds(slot * width, width)
                q[:, span] = times(x[...], w[:, span]).astype(LOW)

        def allowed(pair):
            if keep is None:
                return lax.broadcasted_iota(jnp.int32, (1, rows), 1) < real
            return keep[pair] > 0

        def forward(pair, carry):
            at = rows_at(pair, rows)
            for q, c in ((q0, c0), (q1, c1)):
                for n in range(slabs):
                    c[at, slab(n)] = attend(
                        q[at, slab(n)],
                        q[at, slab(slabs + n)],
                        q[at, slab(2 * slabs + n)],
                        allowed(pair),
                        size,
                    )
            return carry

        lax.fori_loop(0, pairs, forward, 0)
        used = pl.ds(0, width)
        kept = (y, (h0, h1), (s0, s1), n1, i1, n2, i2)
        out[...] = tail_forward(
            x[...], (c0[:, used], c1[:, used]), (o0, o1), gain, shift, (u0, u1), (d0, d1), kept, mixed
        ).astype(LOW)
        dcs = tail_backward(
            seed[...].astype(FULL),
            ((s0, s1), n1, i1, n2, i2),
            (o0, o1),
            gain,
            (u0, u1),
            (d0, d1),
            (df, (du0, du1), da, dgain, dshift),
            mixed,
        )
        dc0[...] = dcs[0]
        dc1[...] = dcs[1]

        def backward(pair, carry):
            at = rows_at(pair, rows)
            for q, dc, p in ((q0, dc0, p0), (q1, dc1, p1)):
                for n in range(slabs):
                    grads = attend_back(
                        q[at, slab(n)],
                        q[at, slab(slabs + n)],
                        q[at, slab(2 * slabs + n)],
                        allowed(pair),
                        size,
                        dc[at, slab(n)],
                    )
                    for slot in range(3):
                        p[at, pl.ds(slot * stride + n * 128, 128)] = grads[slot]
            return carry

        lax.fori_loop(0, pairs, backward, 0)
        for w, p in ((w0, p0), (w1, p1)):
            for slot in range(3):
                mixed[...] += times_back(
                    p[:, pl.ds(slot * stride, width)], w[:, pl.ds(slot * width, width)]
                )
        dx[...] = mixed[...].astype(LOW)


def self_layer_open(pairs, rows, real, size, stride, front, x, w0, w1, *rest):
    self_layer(pairs, rows, real, size, stride, front, x, w0, w1, None, *rest)


def first_tail_back(
    front, seed, s0, s1, n1, i1, n2, i2, o0, o1, gain, u0, u1, d0, d1,
    df_in, du0_in, du1_in, da_in, dgain_in, dshift_in,
    df, du0, du1, da, dgain, dshift, dres, dc0, dc1,
):
    @pl.when(front[0] == 0)
    def pass_on():
        df[...] = df_in[...]
        du0[...] = du0_in[...]
        du1[...] = du1_in[...]
        da[...] = da_in[...]
        dgain[...] = dgain_in[...]
        dshift[...] = dshift_in[...]

    @pl.when(front[0] == 1)
    def work():
        dcs = tail_backward(
            seed[...].astype(FULL),
            ((s0, s1), n1, i1, n2, i2),
            (o0, o1),
            gain,
            (u0, u1),
            (d0, d1),
            (df, (du0, du1), da, dgain, dshift),
            dres,
        )
        dc0[...] = dcs[0]
        dc1[...] = dcs[1]


def cross_backward(
    pairs, rows_t, rows_i, real_t, front,
    tp, ip, dct, dci, keep, wt, wi, dtp0_in, dtp1_in, dip0_in, dip1_in,
    dtp, dip, dxt, dxi,
):
    width = dct.shape[1]
    slabs = width // 128
    half_t, half_i = dtp0_in.shape[0], dip0_in.shape[0]

    @pl.when(front[0] == 0)
    def pass_on():
        dtp[0:half_t, :] = dtp0_in[...]
        dtp[half_t:, :] = dtp1_in[...]
        dip[0:half_i, :] = dip0_in[...]
        dip[half_i:, :] = dip1_in[...]

    @pl.when(front[0] == 1)
    def work():
        text_keys = lax.broadcasted_iota(jnp.int32, (1, rows_t), 1) < real_t

        def each(pair, carry):
            at_t, at_i = rows_at(pair, rows_t), rows_at(pair, rows_i)
            kept = keep[pair] > 0
            for n in range(slabs):
                first, second, third = slab(n), slab(slabs + n), slab(2 * slabs + n)
                dq, dk, dv = attend_back(
                    tp[at_t, first], ip[at_i, second], ip[at_i, third], kept, 128, dct[at_t, first]
                )
                dtp[at_t, first] = dq
                dip[at_i, second] = dk
                dip[at_i, third] = dv
                dq, dk, dv = attend_back(
                    ip[at_i, first], tp[at_t, second], tp[at_t, third], text_keys, 128, dci[at_i, first]
                )
                dip[at_i, first] = dq
                dtp[at_t, second] = dk
                dtp[at_t, third] = dv
            return carry

        lax.fori_loop(0, pairs, each, 0)
        for dp, w, dx in ((dtp, wt, dxt), (dip, wi, dxi)):
            dx[...] = times_back(dp[:, pl.ds(0, width)], w[:, pl.ds(0, width)])
            for slot in range(1, 3):
                span = pl.ds(slot * width, width)
                dx[...] += times_back(dp[:, span], w[:, span])


def round_up(value, step):
    return -(-value // step) * step


def masks_of(order):
    count = len(order)
    return [
        sum(((place >> (count - 1 - n)) & 1) << bit for n, bit in enumerate(order))
        for place in range(1 << count)
    ]


def block_rows(weights, blocks):
    layout, start = [], 0
    for depth, width in weights:
        rows = round_up(depth // blocks, 16)
        layout.append((depth // blocks, rows, start))
        start += rows * (width // UNIT)
    return layout, start


def pack_body(shapes, order, me, *refs):
    count = len(order)
    blocks = 1 << count
    masks = masks_of(order)
    layout, size = block_rows(shapes, blocks)
    factors, rest = refs[: 4 * len(shapes)], refs[4 * len(shapes) :]
    outs, total = rest[: count + 1], rest[count + 1]
    for index, (depth, width) in enumerate(shapes):
        x0, x1, y0, y1 = factors[4 * index : 4 * index + 4]
        real, rows, start = layout[index]
        for column in range(0, width, TILE if width % TILE == 0 else UNIT):
            span = TILE if width % TILE == 0 else UNIT
            area = pl.ds(column, span)
            total[0:depth, 0:span] = back_times(x0[...], y0[:, area]) + back_times(
                x1[...], y1[:, area]
            )
            for place in range(blocks):
                level = place.bit_length()
                target = outs[count - level]
                inside = place - (1 << (level - 1)) if level else 0
                block = me[0] ^ masks[place]
                source = pl.ds(pl.multiple_of(block * real, 8), rows)
                for piece in range(0, span, UNIT):
                    row = inside * size + start + ((column + piece) // UNIT) * rows
                    target[row : row + rows, :] = total[source, piece : piece + UNIT].astype(LOW)


def pack(weights, order, me):
    shapes = [(w[0].shape[1], w[2].shape[1]) for w in weights]
    blocks = 1 << len(order)
    layout, size = block_rows(shapes, blocks)
    sizes = [size << (len(order) - 1 - n) for n in range(len(order))] + [size]
    deepest = max(depth for depth, unused in shapes) + 32
    work = sum(2 * (w[0].shape[0] + w[1].shape[0]) * s[0] * s[1] for w, s in zip(weights, shapes))
    return launch(
        functools.partial(pack_body, shapes, order),
        [shape_of(rows, UNIT) for rows in sizes],
        tuple(v for w in weights for v in w),
        scratch=[pltpu.VMEM((deepest, TILE), FULL)],
        flag=me,
        work=work,
        name="pack",
    )


def unpack_body(shapes, order, me, near, far, *outs):
    place = pl.program_id(0)
    blocks = 1 << len(order)
    layout, size = block_rows(shapes, blocks)

    def write(source):
        for (depth, width), (real, rows, start), out in zip(shapes, layout, outs):
            for column in range(0, width, UNIT):
                row = start + (column // UNIT) * rows
                values = source[row : row + rows, :].astype(FULL)
                out[:, column : column + UNIT] = values[0:real]

    @pl.when(place < blocks // 2)
    def first():
        write(near)

    @pl.when(place >= blocks // 2)
    def second():
        write(far)


def unpack(near, far, shapes, order, me):
    count = len(order)
    blocks = 1 << count
    layout, size = block_rows(shapes, blocks)

    def block_of(place, me):
        mask = 0
        for n, bit in enumerate(order):
            mask = mask | (((place >> (count - 1 - n)) & 1) << bit)
        return me[0] ^ mask

    grid_spec = pltpu.PrefetchScalarGridSpec(
        num_scalar_prefetch=1,
        grid=(blocks,),
        in_specs=[
            pl.BlockSpec((size, UNIT), lambda p, me: (jnp.minimum(p, blocks // 2 - 1), 0)),
            pl.BlockSpec((size, UNIT), lambda p, me: (jnp.maximum(p - blocks // 2, 0), 0)),
        ],
        out_specs=[
            pl.BlockSpec((real, width), lambda p, me: (block_of(p, me), 0))
            for (depth, width), (real, rows, start) in zip(shapes, layout)
        ],
    )
    return pl.pallas_call(
        functools.partial(unpack_body, shapes, order),
        out_shape=tuple(jax.ShapeDtypeStruct(shape, FULL) for shape in shapes),
        grid_spec=grid_spec,
        compiler_params=pltpu.CompilerParams(vmem_limit_bytes=ROOM),
        cost_estimate=pl.CostEstimate(
            flops=0, bytes_accessed=6 * sum(a * b for a, b in shapes), transcendentals=0
        ),
        name="unpack",
    )(me, near, far)


CORES = [(0, 1), (1, 0)]


def to_other_core(values):
    return lax.ppermute(values, "tensor", CORES)


def to_other_section(values):
    return lax.ppermute(values, "section", CORES)


def over_data(values, bit):
    route = [(place, place ^ (1 << bit)) for place in range(lax.axis_size("dp"))]
    return lax.ppermute(values, "dp", route)


def after(values, token):
    if token is None:
        return values
    return lax.optimization_barrier((values, token))[0]


def planned(chunks):
    free = {"low": 0.0, "near": 0.0, "far": 0.0}
    state = {name: [0, ready] for name, order, rows, ready, rank in chunks}
    events = []
    while True:
        best = None
        for name, order, rows, ready, rank in chunks:
            step, moment = state[name]
            count = len(order)
            if step == 2 * count:
                continue
            turn = step if step < count else 2 * count - 1 - step
            bit = order[turn]
            amount = rows << (count - 1 - turn)
            uses = {"low": amount}
            if bit == 1:
                uses = {"near": amount}
            elif bit > 1:
                uses = {"far": amount * bit, "near": amount * 0.5 * bit}
            begin = max([moment] + [free[link] for link in uses])
            key = (begin, rank)
            if best is None or key < best[0]:
                best = (key, name, step, uses, begin)
        if best is None:
            break
        unused, name, step, uses, begin = best
        end = begin + max(uses.values())
        for link, amount in uses.items():
            free[link] = max(free[link], begin + amount)
        state[name] = [step + 1, end + 50]
        events.append((begin, 1, name, step))
        events.append((end, 0, name, step))
    return sorted(events)


def summed(chunks, parts):
    sizes = {chunk[0]: chunk[2] for chunk in chunks}
    orders = {chunk[0]: chunk[1] for chunk in chunks}
    held = {name: list(values) for name, values in parts.items()}
    flying, pieces, token = {}, {name: [] for name in held}, None
    for unused, starting, name, step in planned(chunks):
        order, rows = orders[name], sizes[name]
        count = len(order)
        if starting:
            if step < count:
                given, bit = held[name][step], order[step]
            else:
                given, bit = held[name], order[2 * count - 1 - step]
            if step > 0:
                given = after(given, token)
            flying[name] = over_data(given, bit)
            continue
        got = after(flying.pop(name), token)
        token = got
        if step < count:
            mine = held[name]
            for later in range(step + 1, count):
                first = rows << (count - 1 - later)
                mine[later] = mine[later] + got[first : 2 * first]
            mine[count] = mine[count] + got[:rows]
            if step == count - 1:
                held[name] = mine[count]
                pieces[name].append(mine[count])
        else:
            pieces[name].append(got)
            if step < 2 * count - 1:
                held[name] = jnp.concatenate([held[name], got], axis=0)
    return {name: (held[name], pieces[name][-1]) for name in held}, pieces


def shards(
    text_stream,
    image_stream,
    region_mask,
    co_text_in,
    co_text_out,
    self_text_in,
    self_text_out,
    image_attn_in,
    image_attn_out,
    text_up,
    text_down,
    image_up,
    image_down,
    text_gain,
    text_shift,
    image_gain,
    image_shift,
):
    front = lax.axis_index("section") == 0
    core = lax.axis_index("tensor")
    flag = front.astype(jnp.int32).reshape(1)
    me = lax.axis_index("dp").astype(jnp.int32).reshape(1)
    pairs = text_stream.shape[1]
    half = pairs // 2
    real_t, real_i = text_stream.shape[2], image_stream.shape[2]
    rows_t, rows_i = round_up(real_t, 16), round_up(real_i, 16)
    wide_t, wide_i = text_stream.shape[3], image_stream.shape[3]
    text_size = D_TEXT // HEADS_TEXT
    image_size = D_IMAGE // HEADS_IMAGE

    def own_first(values):
        return jnp.where(core == 0, values, jnp.roll(values, half, axis=0))

    def flat_rows(values, rows):
        grown = jnp.pad(values, ((0, 0), (0, rows - values.shape[1]), (0, 0)))
        return grown.reshape(values.shape[0] * rows, values.shape[2])

    def fold(weight):
        return weight.reshape(weight.shape[0], -1)

    own_t, own_i = half * rows_t, half * rows_i
    all_t, all_i = pairs * rows_t, pairs * rows_i
    xt = flat_rows(own_first(text_stream[0]), rows_t)
    xi = flat_rows(own_first(image_stream[0]), rows_i)
    keep = own_first(jnp.pad(region_mask, ((0, 0), (0, rows_i - real_i)))).reshape(pairs, 1, rows_i)
    gain_t, shift_t, gain_i, shift_i = text_gain[0], text_shift[0], image_gain[0], image_shift[0]
    cross_in, image_in, single_in = fold(co_text_in), fold(image_attn_in[0]), fold(self_text_in)
    image_out, up_i, down_i = image_attn_out[0], image_up[0], image_down[0]
    up_t, down_t = text_up[0], text_down[0]
    image_out_2, cross_out_2 = to_other_core(image_out), to_other_core(co_text_out)
    up_i_2, down_i_2 = to_other_core(up_i), to_other_core(down_i)
    up_t_2, down_t_2 = to_other_core(up_t), to_other_core(down_t)
    image_in_2, single_in_2 = to_other_core(image_in), to_other_core(single_in)
    single_out_2 = to_other_core(self_text_out)
    cross = cross_in.shape[1] // 3
    single = single_in.shape[1] // 3
    ff_t, ff_i = up_t.shape[1], up_i.shape[1]
    tail_t = (up_t, up_t_2, down_t, down_t_2)
    tail_i = (up_i, up_i_2, down_i, down_i_2)

    tp, ip, ct, ci = launch(
        functools.partial(cross_forward, pairs, rows_t, rows_i, real_t),
        [shape_of(all_t, 3 * cross), shape_of(all_i, 3 * cross), shape_of(all_t, cross), shape_of(all_i, cross)],
        (xt, xi, cross_in, image_in, keep),
        work=6 * cross * (all_t * wide_t + all_i * wide_i),
        name="cross_forward",
    )
    ci_2 = to_other_core(ci[own_i:])
    ct_2 = to_other_core(ct[own_t:])

    def tail_shapes(rows, width, hidden):
        return [
            shape_of(rows, width),
            shape_of(rows, width),
            shape_of(rows, hidden),
            shape_of(rows, hidden),
            shape_of(rows, hidden, FULL),
            shape_of(rows, hidden, FULL),
            shape_of(rows, width, FULL),
            shape_of(rows, 128, FULL),
            shape_of(rows, width, FULL),
            shape_of(rows, 128, FULL),
        ]

    def run_first_tail(x, c0, c1, o0, o1, gain, shift, ff, rows, width, hidden, name):
        return launch(
            first_tail,
            tail_shapes(rows, width, hidden),
            (x, c0, c1, o0, o1, gain, shift) + ff,
            scratch=[pltpu.VMEM((rows, width), FULL)],
            work=4 * rows * width * (o0.shape[0] + 2 * hidden),
            name=name,
        )

    bi, yi, hi0, hi1, si0, si1, ni1, ii1, ni2, ii2 = run_first_tail(
        xi[:own_i], ci[:own_i], ci_2, image_out, image_out_2, gain_i, shift_i, tail_i, own_i, wide_i, ff_i, "tail_i"
    )
    bi = to_other_section(bi)
    bt, yt, ht0, ht1, st0, st1, nt1, it1, nt2, it2 = run_first_tail(
        xt[:own_t], ct[:own_t], ct_2, co_text_out, cross_out_2, gain_t, shift_t, tail_t, own_t, wide_t, ff_t, "tail_t"
    )
    bt = to_other_section(bt)

    def run_self(rows, real, size, width, hidden, x, w0, w1, masked, o0, o1, gain, shift, ff, seed, y, h0, h1, c, name):
        count = half * rows
        inner = w0.shape[1] // 3
        body = functools.partial(self_layer if masked else self_layer_open, half, rows, real, size, cross)
        low_w, low_h = shape_of(count, width), shape_of(count, hidden)
        grads = [shape_of(2, width, FULL)] * 2
        outputs = [low_w, low_w] + [shape_of(count, cross)] * 2 + [shape_of(count, 3 * cross)] * 2
        outputs += [low_w, low_w, low_h, low_h, low_w, low_h, low_h] + grads
        scratch = [pltpu.VMEM((count, 3 * inner), LOW)] * 2
        scratch += [pltpu.VMEM((count, hidden), FULL)] * 2
        scratch += [pltpu.VMEM((count, width), FULL), pltpu.VMEM((count, 128), FULL)] * 2
        scratch += [pltpu.VMEM((count, width), FULL)] + [pltpu.VMEM((count, inner), LOW)] * 2
        return launch(
            body,
            outputs,
            (x, w0, w1) + ((keep,) if masked else ()) + (o0, o1, gain, shift) + ff + (seed, y, h0, h1, c),
            scratch=scratch,
            flag=flag,
            work=8 * count * width * (4 * inner + 2 * hidden),
            name=name,
        )

    i2 = run_self(
        rows_i, real_i, image_size, wide_i, ff_i, bi, image_in, image_in_2, True, image_out, image_out_2,
        gain_i, shift_i, tail_i, xi[:own_i], yi, hi0, hi1, ci[:own_i], "self_i",
    )
    seed_i = to_other_section(i2[1])
    t2 = run_self(
        rows_t, real_t, text_size, wide_t, ff_t, bt, single_in, single_in_2, False, self_text_out, single_out_2,
        gain_t, shift_t, tail_t, xt[:own_t], yt, ht0, ht1, ct[:own_t], "self_t",
    )
    seed_t = to_other_section(t2[1])
    (oi, unused, ci_own, ci_give, pi0, pi1, dai, dfi, dui0, dui1, yi, hi0, hi1, dgi, dsi) = i2
    (ot, unused, ct_own, ct_give, pt0, pt1, dat, dft, dut0, dut1, yt, ht0, ht1, dgt, dst) = t2

    def run_tail_back(seed, kept, o0, o1, gain, ff, given, rows, width, hidden, name):
        low_w, low_h = shape_of(rows, width), shape_of(rows, hidden)
        grads = [shape_of(2, width, FULL)] * 2
        outputs = [low_w, low_h, low_h, low_w] + grads + [shape_of(rows, width, FULL)]
        return launch(
            first_tail_back,
            outputs + [shape_of(rows, cross)] * 2,
            (seed,) + kept + (o0, o1, gain) + ff + given,
            flag=flag,
            work=4 * rows * width * (cross + 2 * hidden),
            name=name,
        )

    dfi, dui0, dui1, dai, dgi, dsi, dri, dci_own, dci_give = run_tail_back(
        seed_i, (si0, si1, ni1, ii1, ni2, ii2), image_out, image_out_2, gain_i, tail_i,
        (dfi, dui0, dui1, dai, dgi, dsi), own_i, wide_i, ff_i, "tail_back_i",
    )
    dft, dut0, dut1, dat, dgt, dst, drt, dct_own, dct_give = run_tail_back(
        seed_t, (st0, st1, nt1, it1, nt2, it2), co_text_out, cross_out_2, gain_t, tail_t,
        (dft, dut0, dut1, dat, dgt, dst), own_t, wide_t, ff_t, "tail_back_t",
    )
    dci_2, dct_2 = to_other_core(dci_give), to_other_core(dct_give)
    dtp, dip, dxt, dxi = launch(
        functools.partial(cross_backward, pairs, rows_t, rows_i, real_t),
        [
            shape_of(all_t, 3 * cross),
            shape_of(all_i, 3 * cross),
            shape_of(all_t, wide_t, FULL),
            shape_of(all_i, wide_i, FULL),
        ],
        (
            tp,
            ip,
            jnp.concatenate([dct_own, dct_2], axis=0),
            jnp.concatenate([dci_own, dci_2], axis=0),
            keep,
            cross_in,
            image_in,
            pt0,
            to_other_core(pt1),
            pi0,
            to_other_core(pi1),
        ),
        flag=flag,
        work=6 * cross * (all_t * wide_t + all_i * wide_i),
        name="cross_backward",
    )

    low_bits = tuple(range(lax.axis_size("dp").bit_length() - 1))
    turned = low_bits[1:] + low_bits[:1]

    def choose(first, second):
        return jnp.where(front, first, second)

    ct_other = choose(ct[own_t:], to_other_core(ct_give))
    ci_other = choose(ci[own_i:], to_other_core(ci_give))
    xt_own, xt_other = choose(xt[:own_t], bt), choose(xt[own_t:], to_other_core(bt))
    xi_own, xi_other = choose(xi[:own_i], bi), choose(xi[own_i:], to_other_core(bi))
    up_i_factors = (yi, to_other_core(yi), dui0, to_other_core(dui1))
    down_i_factors = (hi0, to_other_core(hi1), dfi, to_other_core(dfi))
    up_t_factors = (yt, to_other_core(yt), dut0, to_other_core(dut1))
    down_t_factors = (ht0, to_other_core(ht1), dft, to_other_core(dft))
    out_i_factors = (ci_own, ci_other, dai, to_other_core(dai))
    out_t_factors = (ct_own, ct_other, dat, to_other_core(dat))
    in_t_factors = (xt_own, xt_other, dtp[:own_t], dtp[own_t:])
    in_i_factors = (xi_own, xi_other, dip[:own_i], dip[own_i:])
    groups = {
        "ff_i": ((up_i_factors, down_i_factors), turned, 0, 2),
        "up_t": ((up_t_factors,), low_bits, 0, 3),
        "down_t": ((down_t_factors,), low_bits, 0, 4),
        "outs": ((out_i_factors, out_t_factors), low_bits, 150, 0),
        "in_t": ((in_t_factors,), low_bits, 500, 1),
        "in_i": ((in_i_factors,), low_bits, 500, 5),
    }
    parts = {name: pack(group[0], group[1], me) for name, group in groups.items()}
    chunks = [
        (name, group[1], parts[name][-1].shape[0], group[2], group[3]) for name, group in groups.items()
    ]
    sums, pieces = summed(chunks, parts)
    wholes = {}
    for name, (weights, order, unused, unused) in groups.items():
        shapes = [(w[0].shape[1], w[2].shape[1]) for w in weights]
        wholes[name] = unpack(sums[name][0], sums[name][1], shapes, order, me)

    def from_other_section(name):
        got = [to_other_section(piece) for piece in pieces[name]]
        weights, order = groups[name][0], groups[name][1]
        shapes = [(w[0].shape[1], w[2].shape[1]) for w in weights]
        return unpack(jnp.concatenate(got[:-1], axis=0), got[-1], shapes, order, me)

    out_t, in_t = wholes["outs"][1], wholes["in_t"][0]
    other_out, other_in = from_other_section("outs")[1], from_other_section("in_t")[0]

    def slots(values):
        return values.reshape(values.shape[0], 3, cross)

    co_in_grad = slots(choose(in_t, other_in))
    co_out_grad = choose(out_t, other_out)
    self_in_grad = slots(choose(other_in, in_t))[:, :, :single]
    self_out_grad = choose(other_out, out_t)[:single]

    flat = jnp.concatenate([dgt, dst, dgi, dsi], axis=1)
    flat = flat + to_other_core(flat)
    for bit in low_bits:
        flat = flat + over_data(flat, bit)
    ends = [wide_t, 2 * wide_t, 2 * wide_t + wide_i]
    small = jnp.split(flat, ends, axis=1)

    def result(rest, partial, output, count, rows, real):
        mine = choose(rest + partial[:count] + to_other_core(partial[count:]), output.astype(FULL))
        mine = mine.astype(LOW).reshape(half, rows, -1)[:, :real]
        got = to_other_core(mine)
        return jnp.concatenate(
            [jnp.where(core == 0, mine, got), jnp.where(core == 0, got, mine)], axis=0
        )[None]

    return (
        result(drt, dxt, ot, own_t, rows_t, real_t),
        result(dri, dxi, oi, own_i, rows_i, real_i),
        co_in_grad,
        co_out_grad,
        self_in_grad,
        self_out_grad,
        slots(wholes["in_i"][0])[None],
        wholes["outs"][0][None],
        wholes["up_t"][0][None],
        wholes["down_t"][0][None],
        wholes["ff_i"][0][None],
        wholes["ff_i"][1][None],
        small[0][None],
        small[1][None],
        small[2][None],
        small[3][None],
    )


def solution(mesh):
    in_specs = (
        P("section", "dp", None, None),
        P("section", "dp", None, None),
        P("dp", None),
        P(None, None, "tensor"),
        P("tensor", None),
        P(None, None, "tensor"),
        P("tensor", None),
        P("section", None, None, "tensor"),
        P("section", "tensor", None),
        P("section", None, "tensor"),
        P("section", "tensor", None),
        P("section", None, "tensor"),
        P("section", "tensor", None),
        P("section", None, None),
        P("section", None, None),
        P("section", None, None),
        P("section", None, None),
    )
    out_specs = (
        P("section", "dp", None, None),
        P("section", "dp", None, None),
        P(None, None, "tensor"),
        P("tensor", None),
        P(None, None, "tensor"),
        P("tensor", None),
        P("section", None, None, "tensor"),
        P("section", "tensor", None),
        P("section", None, "tensor"),
        P("section", "tensor", None),
        P("section", None, "tensor"),
        P("section", "tensor", None),
        P("section", None, None),
        P("section", None, None),
        P("section", None, None),
        P("section", None, None),
    )
    return jax.shard_map(shards, mesh=mesh, in_specs=in_specs, out_specs=out_specs, check_vma=False)
```

```python
import functools
import math

import jax
import jax.numpy as jnp
from jax import lax
from jax.experimental import pallas as pl
from jax.experimental.pallas import tpu as pltpu
from jax.sharding import PartitionSpec as P

D_TEXT = 768
HEADS_TEXT = 12
D_IMAGE = 1024
HEADS_IMAGE = 8
D_CO = 1024
HEADS_CO = 8

LOW = jnp.bfloat16
FULL = jnp.float32
TILE = 512
UNIT = 256
ROOM = 56 * 1024 * 1024


def times(left, right):
    return jnp.dot(left, right, preferred_element_type=FULL)


def times_back(left, right):
    return lax.dot_general(left, right, (((1,), (1,)), ((), ())), preferred_element_type=FULL)


def back_times(left, right):
    return lax.dot_general(left, right, (((0,), (0,)), ((), ())), preferred_element_type=FULL)


def norm_rows(rows):
    centre = rows - jnp.mean(rows, axis=-1, keepdims=True)
    spread = jnp.mean(centre * centre, axis=-1, keepdims=True)
    inverse = lax.rsqrt(spread + 1e-05)
    return centre * inverse, inverse


def norm_back(unit, inverse, gain, grad):
    scaled = grad * gain
    first = jnp.mean(scaled, axis=-1, keepdims=True)
    second = jnp.mean(scaled * unit, axis=-1, keepdims=True)
    dgain = jnp.sum(grad * unit, axis=0, keepdims=True)
    dshift = jnp.sum(grad, axis=0, keepdims=True)
    return inverse * (scaled - first - unit * second), dgain, dshift


def gelu_both(inputs):
    rate = 0.7978845608028654
    square = inputs * inputs
    bent = jnp.tanh(rate * inputs * (1.0 + 0.044715 * square))
    half = 0.5 * (1.0 + bent)
    slope = half + 0.5 * inputs * (1.0 - bent * bent) * rate * (1.0 + 0.134145 * square)
    return inputs * half, slope


def heads_of(query, size):
    if size == query.shape[1]:
        return [query]
    lower = lax.broadcasted_iota(jnp.int32, (1, query.shape[1]), 1) < size
    low = lower.astype(FULL).astype(LOW)
    return [query * low, query * (1 - low)]


def merged(parts, size):
    if len(parts) == 1:
        return parts[0]
    return jnp.where(lax.broadcasted_iota(jnp.int32, parts[0].shape, 1) < size, parts[0], parts[1])


def softmax_all(pairs, alloweds, size):
    scores = [times_back(query, keys) for query, keys in pairs]
    scores = [
        jnp.where(allowed, score * (1.0 / math.sqrt(size)), -1000000000.0)
        for score, allowed in zip(scores, alloweds)
    ]
    tops = [jnp.max(score, axis=-1, keepdims=True) for score in scores]
    raised = [jnp.exp(score - top) for score, top in zip(scores, tops)]
    shares = [1.0 / jnp.sum(value, axis=-1, keepdims=True) for value in raised]
    return [value * share for value, share in zip(raised, shares)]


def attend_all(units, size):
    singles = [(q, k, v, a) for query, k, v, a in units for q in heads_of(query, size)]
    weights = softmax_all([one[:2] for one in singles], [one[3] for one in singles], size)
    contexts = [times(w.astype(LOW), one[2]) for w, one in zip(weights, singles)]
    heads = len(singles) // len(units)
    return [merged(contexts[n * heads : (n + 1) * heads], size).astype(LOW) for n in range(len(units))]


def attend_back_all(units, size):
    scaling = 1.0 / math.sqrt(size)
    singles = [
        (q, k, v, a, d, query, dcontext)
        for query, k, v, a, dcontext in units
        for q, d in zip(heads_of(query, size), heads_of(dcontext, size))
    ]
    weights = softmax_all([one[:2] for one in singles], [one[3] for one in singles], size)
    dweights = [times_back(one[4], one[2]) for one in singles]
    dvalues = [back_times(w.astype(LOW), one[6]) for w, one in zip(weights, singles)]
    sums = [jnp.sum(dw * w, axis=-1, keepdims=True) for dw, w in zip(dweights, weights)]
    dscores = [(w * (dw - s)).astype(LOW) for w, dw, s in zip(weights, dweights, sums)]
    dqueries = [times(ds, one[1]) * scaling for ds, one in zip(dscores, singles)]
    dkeys = [back_times(ds, one[5]) * scaling for ds, one in zip(dscores, singles)]
    heads = len(singles) // len(units)
    return [
        [merged(grads[n * heads : (n + 1) * heads], size).astype(LOW) for grads in (dqueries, dkeys, dvalues)]
        for n in range(len(units))
    ]


def wide(column):
    return jnp.broadcast_to(column, (column.shape[0], 128))


class Late:
    def __init__(self, source, target, signal):
        self.target = target
        self.copy = pltpu.make_async_copy(source, target, signal)
        self.copy.start()
        self.here = False

    def get(self):
        if not self.here:
            self.copy.wait()
            self.here = True
        return self.target


class Here:
    def __init__(self, target):
        self.target = target

    def get(self):
        return self.target


def fetch(sources, targets, signals):
    return [Late(s, t, signals.at[n]) for n, (s, t) in enumerate(zip(sources, targets))]


def pass_through(sources, targets, signals):
    copies = [
        pltpu.make_async_copy(s, t, signals.at[n]) for n, (s, t) in enumerate(zip(sources, targets))
    ]
    for copy in copies:
        copy.start()
    for copy in copies:
        copy.wait()


def tail_forward(residual, contexts, out_w, gain, shift, up_w, down_w, kept, mixed):
    normed_ref, hidden, slopes, unit1, inv1, unit2, inv2 = kept
    branch = times(contexts[0], out_w[0].get()[...]) + times(contexts[1], out_w[1].get()[...])
    unit, inverse = norm_rows(residual.astype(FULL) + branch)
    unit1[...] = unit
    inv1[...] = wide(inverse)
    normed = unit * gain[0:1, :] + shift[0:1, :]
    normed_ref[...] = normed.astype(LOW)
    mixed[...] = normed
    for half in range(2):
        up, down = up_w[half].get(), down_w[half].get()
        for start in range(0, up.shape[1], TILE):
            span = pl.ds(start, TILE)
            value, slope = gelu_both(times(normed_ref[...], up[:, span]))
            hidden[half][:, span] = value.astype(LOW)
            slopes[half][:, span] = slope
            mixed[...] += times(hidden[half][:, span], down[span, :])
    unit, inverse = norm_rows(mixed[...])
    unit2[...] = unit
    inv2[...] = wide(inverse)
    return unit * gain[1:2, :] + shift[1:2, :]


def tail_backward(seed, kept, out_w, gain, up_w, down_w, grads, total):
    slopes, unit1, inv1, unit2, inv2 = kept
    df, du, da, dgain, dshift = grads
    dsecond, dgain1, dshift1 = norm_back(
        unit2.get()[...], inv2.get()[:, 0:1], gain[1:2, :], seed
    )
    total[...] = dsecond
    df[...] = dsecond.astype(LOW)
    for half in range(2):
        up, down, slope = up_w[half].get(), down_w[half].get(), slopes[half].get()
        for start in range(0, up.shape[1], TILE):
            span = pl.ds(start, TILE)
            dhidden = times_back(df[...], down[span, :])
            du[half][:, span] = (dhidden * slope[:, span]).astype(LOW)
            total[...] += times_back(du[half][:, span], up[:, span])
    dfirst, dgain0, dshift0 = norm_back(
        unit1.get()[...], inv1.get()[:, 0:1], gain[0:1, :], total[...]
    )
    dgain[...] = jnp.concatenate([dgain0, dgain1], axis=0)
    dshift[...] = jnp.concatenate([dshift0, dshift1], axis=0)
    total[...] = dfirst
    da[...] = dfirst.astype(LOW)
    return [times_back(da[...], w.get()[...]).astype(LOW) for w in out_w]


def shape_of(rows, columns, kind=LOW):
    return jax.ShapeDtypeStruct((rows, columns), kind)


def launch(body, outputs, args, far=(), scratch=(), flag=None, work=0, name=None):
    whole = pl.BlockSpec(memory_space=pltpu.VMEM)
    moved = sum(
        math.prod(v.shape) * v.dtype.itemsize for v in tuple(args) + tuple(far) + tuple(outputs)
    )
    specs = [pl.BlockSpec(memory_space=pltpu.SMEM)] + [whole] * len(args)
    specs += [pl.BlockSpec(memory_space=pl.ANY)] * len(far)
    return pl.pallas_call(
        body,
        out_shape=tuple(outputs),
        in_specs=specs,
        out_specs=tuple([whole] * len(outputs)),
        scratch_shapes=list(scratch),
        compiler_params=pltpu.CompilerParams(vmem_limit_bytes=ROOM),
        cost_estimate=pl.CostEstimate(flops=work, bytes_accessed=moved, transcendentals=0),
        name=name,
    )(flag, *args, *far)


def buffers_for(far):
    return [pltpu.VMEM(v.shape, v.dtype) for v in far] + [pltpu.SemaphoreType.DMA((len(far),))]


def rows_at(pair, rows):
    return pl.ds(pl.multiple_of(pair * rows, 16), rows)


def slab(index):
    return pl.ds(index * 128, 128)


def cross_forward(
    pairs, rows_t, rows_i, real_t, info, x_t, x_i, keep, far_t, far_i,
    xt_own, xt_other, xi_own, xi_other, tp, ip, ct_own, ct_other, ci_own, ci_other, xt, xi, wt, wi, signals,
):
    half = pairs // 2
    for place in range(pairs):
        pair = lax.rem(place + half * info[1], pairs)
        text, image = x_t[rows_at(pair, rows_t), :], x_i[rows_at(pair, rows_i), :]
        xt[place * rows_t : (place + 1) * rows_t, :] = text
        xi[place * rows_i : (place + 1) * rows_i, :] = image
        inside = place % half
        (xt_own, xt_other)[place // half][inside * rows_t : (inside + 1) * rows_t, :] = text
        (xi_own, xi_other)[place // half][inside * rows_i : (inside + 1) * rows_i, :] = image

    @pl.when(info[0] == 1)
    def work():
        width = ct_own.shape[1]
        weights = fetch((far_t, far_i), (wt, wi), signals)
        for late, x, p in ((weights[0], xt, tp), (weights[1], xi, ip)):
            for slot in range(3):
                p[:, pl.ds(slot * width, width)] = times(x[...], late.get()[slot]).astype(LOW)
        text_keys = lax.broadcasted_iota(jnp.int32, (1, rows_t), 1) < real_t
        slabs = width // 128

        def each(pair, carry):
            at_t, at_i = rows_at(pair, rows_t), rows_at(pair, rows_i)
            for group, ct, ci in ((0, ct_own, ci_own), (half, ct_other, ci_other)):
                from_t, from_i = rows_at(pair + group, rows_t), rows_at(pair + group, rows_i)
                kept = keep[lax.rem(pair + group + half * info[1], pairs)] > 0
                texts, images = [], []
                for n in range(slabs):
                    first, second, third = slab(n), slab(slabs + n), slab(2 * slabs + n)
                    texts.append((tp[from_t, first], ip[from_i, second], ip[from_i, third], kept))
                    images.append((ip[from_i, first], tp[from_t, second], tp[from_t, third], text_keys))
                results = zip(attend_all(texts, 128), attend_all(images, 128))
                for n, (text, image) in enumerate(results):
                    ct[at_t, slab(n)] = text
                    ci[at_i, slab(n)] = image
            return carry

        lax.fori_loop(0, half, each, 0)


def first_tail(
    info, x, c0, c1, gain, shift, *refs
):
    far, refs = refs[:6], refs[6:]
    out, y, h0, h1, s0, s1, n1, i1, n2, i2, mixed = refs[:11]
    near, signals = refs[11:17], refs[17]

    @pl.when(info[0] == 1)
    def work():
        o0, o1, u0, d0, u1, d1 = fetch(far, near, signals)
        kept = (y, (h0, h1), (s0, s1), n1, i1, n2, i2)
        out[...] = tail_forward(
            x[...], (c0[...], c1[...]), (o0, o1), gain, shift, (u0, u1), (d0, d1), kept, mixed
        ).astype(LOW)


def self_layer(
    masked, half, rows, real, size, stride, info, x, seed, gain, shift, keep, *refs
):
    far, refs = refs[:12], refs[12:]
    (out, dx, c0, p0, da, df, du0, du1, y, h0, dgain, dshift, give) = refs[:13]
    (q0, q1, s0, s1, n1, i1, n2, i2, mixed, dc0, dc1, h1, c1, p1) = refs[13:27]
    near, signals = refs[27:35], refs[35]
    width = q0.shape[1] // 3
    wide_x, wide_h, wide_c = x.shape[1], h1.shape[1], c1.shape[1]
    spans = []
    for columns in (wide_x, wide_h, wide_c, p1.shape[1], wide_x):
        spans.append(pl.ds(sum(span.size for span in spans), columns))

    @pl.when(info[0] == 1)
    def pass_on():
        targets = (y, h0, c0, give.at[:, spans[0]], give.at[:, spans[1]])
        pass_through((far[8], far[9], far[11], far[8], far[10]), targets, signals)

    @pl.when(info[0] == 0)
    def work():
        w0, w1, o0, o1, u0, d0, u1, d1 = fetch(far[:8], near, signals)
        slabs = width // 128
        if c0.shape[1] != width:
            rest = pl.ds(width, c0.shape[1] - width)
            c0[:, rest] = jnp.zeros((c0.shape[0], c0.shape[1] - width), LOW)
            c1[:, rest] = jnp.zeros((c0.shape[0], c0.shape[1] - width), LOW)
            for slot in range(3):
                rest = pl.ds(slot * stride + width, stride - width)
                p0[:, rest] = jnp.zeros((p0.shape[0], stride - width), LOW)
                p1[:, rest] = jnp.zeros((p0.shape[0], stride - width), LOW)
        for w, q in ((w0, q0), (w1, q1)):
            for slot in range(3):
                q[:, pl.ds(slot * width, width)] = times(x[...], w.get()[slot]).astype(LOW)

        def allowed(pair):
            if not masked:
                return lax.broadcasted_iota(jnp.int32, (1, rows), 1) < real
            return keep[pair + half * info[1]] > 0

        def forward(pair, carry):
            at = rows_at(pair, rows)
            kept = allowed(pair)
            units = [
                (q[at, slab(n)], q[at, slab(slabs + n)], q[at, slab(2 * slabs + n)], kept)
                for q in (q0, q1)
                for n in range(slabs)
            ]
            results = attend_all(units, size)
            for n, value in enumerate(results):
                (c0, c1)[n // slabs][at, slab(n % slabs)] = value
            return carry

        lax.fori_loop(0, half, forward, 0)
        used = pl.ds(0, width)
        kept = (y, (h0, h1), (s0, s1), n1, i1, n2, i2)
        out[...] = tail_forward(
            x[...], (c0[:, used], c1[:, used]), (o0, o1), gain, shift, (u0, u1), (d0, d1), kept, mixed
        ).astype(LOW)
        held = ((Here(s0), Here(s1)), Here(n1), Here(i1), Here(n2), Here(i2))
        dcs = tail_backward(
            seed[...].astype(FULL),
            held,
            (o0, o1),
            gain,
            (u0, u1),
            (d0, d1),
            (df, (du0, du1), da, dgain, dshift),
            mixed,
        )
        dc0[...] = dcs[0]
        dc1[...] = dcs[1]

        def backward(pair, carry):
            at = rows_at(pair, rows)
            kept = allowed(pair)
            units = [
                (q[at, slab(n)], q[at, slab(slabs + n)], q[at, slab(2 * slabs + n)], kept, dc[at, slab(n)])
                for q, dc in ((q0, dc0), (q1, dc1))
                for n in range(slabs)
            ]
            results = attend_back_all(units, size)
            for n, grads in enumerate(results):
                for slot in range(3):
                    column = slot * stride + (n % slabs) * 128
                    (p0, p1)[n // slabs][at, pl.ds(column, 128)] = grads[slot]
            return carry

        lax.fori_loop(0, half, backward, 0)
        for w, p in ((w0, p0), (w1, p1)):
            for slot in range(3):
                mixed[...] += times_back(p[:, pl.ds(slot * stride, width)], w.get()[slot])
        dx[...] = mixed[...].astype(LOW)
        for span, value in zip(spans, (y, h1, c1, p1, x)):
            give[:, span] = value[...]


def first_tail_back(info, seed, gain, *refs):
    far, refs = refs[:18], refs[18:]
    df, du0, da, dgain, dshift, dres, dc0, give = refs[:8]
    du1, near, signals = refs[8], refs[9:21], refs[21]
    spans = []
    for columns in (df.shape[1], du1.shape[1], da.shape[1], dc0.shape[1]):
        spans.append(pl.ds(sum(span.size for span in spans), columns))

    @pl.when(info[0] == 0)
    def pass_on():
        df_in, du0_in, du1_in, da_in, dgain_in, dshift_in = far[12:]
        pass_through(
            (df_in, du0_in, da_in, dgain_in, dshift_in, df_in, du1_in, da_in),
            (df, du0, da, dgain, dshift) + tuple(give.at[:, span] for span in spans[:3]),
            signals,
        )

    @pl.when(info[0] == 1)
    def work():
        n2, i2, d0, s0, u0, d1, s1, u1, n1, i1, o0, o1 = fetch(far[:12], near, signals)
        dcs = tail_backward(
            seed[...].astype(FULL),
            ((s0, s1), n1, i1, n2, i2),
            (o0, o1),
            gain,
            (u0, u1),
            (d0, d1),
            (df, (du0, du1), da, dgain, dshift),
            dres,
        )
        dc0[...] = dcs[0]
        for span, value in zip(spans, (df[...], du1[...], da[...], dcs[1])):
            give[:, span] = value


def cross_backward(
    wides, pairs, rows_t, rows_i, real_t, info,
    tp, ip, dct_own, dci_own, keep, *refs
):
    far, refs = refs[:8], refs[8:]
    dtp_own, dtp_other, dip_own, dip_other, dxt_own, dxt_other, dxi_own, dxi_other = refs[:8]
    wt, wi, dct_other, dci_other, signals = refs[8:]
    width = dct_own.shape[1]
    slabs = width // 128
    half = pairs // 2

    @pl.when(info[0] == 0)
    def pass_on():
        sources = []
        for mine, got in ((far[4], far[5]), (far[6], far[7])):
            start = got.shape[1] - wides[len(sources) // 2] - mine.shape[1]
            sources += [mine, got.at[:, pl.ds(start, mine.shape[1])]]
        pass_through(sources, (dtp_own, dtp_other, dip_own, dip_other), signals)

    @pl.when(info[0] == 1)
    def work():
        got = [far[n].at[:, pl.ds(far[n].shape[1] - width, width)] for n in (2, 3)]
        weights = fetch(
            (got[0], got[1], far[0], far[1]), (dct_other, dci_other, wt, wi), signals
        )
        weights[0].get()
        weights[1].get()
        weights = weights[2:]
        text_keys = lax.broadcasted_iota(jnp.int32, (1, rows_t), 1) < real_t

        def each(pair, carry):
            at_t, at_i = rows_at(pair, rows_t), rows_at(pair, rows_i)
            for group, dct, dci, dtp, dip in (
                (0, dct_own, dci_own, dtp_own, dip_own),
                (half, dct_other, dci_other, dtp_other, dip_other),
            ):
                from_t, from_i = rows_at(pair + group, rows_t), rows_at(pair + group, rows_i)
                kept = keep[lax.rem(pair + group + half * info[1], pairs)] > 0
                texts, images = [], []
                for n in range(slabs):
                    first, second, third = slab(n), slab(slabs + n), slab(2 * slabs + n)
                    texts.append((tp[from_t, first], ip[from_i, second], ip[from_i, third], kept, dct[at_t, first]))
                    images.append((ip[from_i, first], tp[from_t, second], tp[from_t, third], text_keys, dci[at_i, first]))
                results = zip(attend_back_all(texts, 128), attend_back_all(images, 128))
                for n, (text, image) in enumerate(results):
                    first, second, third = slab(n), slab(slabs + n), slab(2 * slabs + n)
                    dtp[at_t, first], dip[at_i, second], dip[at_i, third] = text
                    dip[at_i, first], dtp[at_t, second], dtp[at_t, third] = image
            return carry

        lax.fori_loop(0, half, each, 0)
        for late, triples in (
            (weights[0], ((dtp_own, dxt_own), (dtp_other, dxt_other))),
            (weights[1], ((dip_own, dxi_own), (dip_other, dxi_other))),
        ):
            for dp, dx in triples:
                total = times_back(dp[:, pl.ds(0, width)], late.get()[0])
                for slot in range(1, 3):
                    total += times_back(dp[:, pl.ds(slot * width, width)], late.get()[slot])
                dx[...] = total


def round_up(value, step):
    return -(-value // step) * step


class Layout:
    def __init__(self, blocks, weights):
        self.blocks, self.weights = blocks, weights
        self.sizes = [0, 0]
        self.units = []
        self.after = {}
        for index, (name, depth, width) in enumerate(weights):
            real = depth // blocks
            for unit in range(width // UNIT):
                way = 0 if self.sizes[0] <= self.sizes[1] else 1
                self.units.append((index, unit, way, self.sizes[way], real))
                self.sizes[way] += round_up(real, 16)
            self.after[name] = list(self.sizes)


def pack_body(layout, chosen, kinds, later, info, *refs):
    blocks, weights = layout.blocks, layout.weights
    place = info[2]
    arrays = 1 + max(max(k[0], k[2] or 0) for k in kinds)
    sources, refs = refs[:arrays], refs[arrays + later :]
    targets, refs = refs[: 2 * blocks], refs[2 * blocks :]
    buffers, refs = refs[: len(kinds)], refs[len(kinds) :]
    outs, (total, signals, out_signals) = refs[: 2 * blocks], refs[2 * blocks :]
    waits = []
    for number, (first, column, second, other) in enumerate(kinds):
        buffer = buffers[number]

        def copy(source, start):
            view = sources[source].at[:, pl.ds(start, buffer.shape[1])]
            return pltpu.make_async_copy(view, buffer, signals.at[number])

        if second is None:
            copy(first, column).start()
        else:
            pl.when(info[0] == 1)(copy(first, column).start)
            pl.when(info[0] == 0)(copy(second, other).start)
        waits.append(copy(first, column))
    position, copies = 0, []
    for index, (name, depth, width) in enumerate(weights):
        if name not in chosen:
            continue
        mine = buffers[position : position + chosen[name]]
        for wait in waits[position : position + chosen[name]]:
            wait.wait()
        position += chosen[name]
        span = TILE if width % TILE == 0 else UNIT
        units = [unit for unit in layout.units if unit[0] == index]
        for column in range(0, width, span):
            area = pl.ds(column, span)
            if chosen[name] == 1:
                total[0:depth, 0:span] = mine[0][:, area]
            else:
                x0, x1, y0, y1 = mine
                total[0:depth, 0:span] = back_times(x0[...], y0[:, area]) + back_times(
                    x1[...], y1[:, area]
                )
            for unused, unit, way, row, real in units:
                inside = unit * UNIT - column
                if not 0 <= inside < span:
                    continue
                rows = round_up(real, 16)
                for hop in range(blocks):
                    block = lax.rem(place + (blocks - hop if way == 0 else hop), blocks)
                    source = pl.ds(pl.multiple_of(block * real, 8), rows)
                    outs[way * blocks + hop][row : row + rows, :] = total[
                        source, inside : inside + UNIT
                    ].astype(LOW)
        for way in range(2):
            rows = [(unit[3], unit[3] + round_up(unit[4], 16)) for unit in units if unit[2] == way]
            if not rows:
                continue
            part = pl.ds(rows[0][0], rows[-1][1] - rows[0][0])
            for hop in range(blocks):
                number = way * blocks + hop
                out = pltpu.make_async_copy(
                    outs[number].at[part], targets[number].at[part], out_signals.at[len(copies)]
                )
                out.start()
                copies.append(out)
    for out in copies:
        out.wait()


def pack(layout, factors, info, name, former=None):
    blocks = layout.blocks
    outputs = [shape_of(layout.sizes[way], UNIT) for way in range(2) for hop in range(blocks)]
    deepest = max(weight[1] for weight in layout.weights) + 32
    arrays, kinds, buffers, work = [], [], [], 0

    def number_of(array):
        for number, one in enumerate(arrays):
            if one is array:
                return number
        arrays.append(array)
        return len(arrays) - 1

    for weight in layout.weights:
        for first, second, columns in factors.get(weight[0], ()):
            if isinstance(first, tuple):
                kind = (number_of(first[0]), first[1], number_of(second[0]), second[1])
                array = first[0]
            else:
                kind = (number_of(first), second, None, None)
                array = first
            kinds.append(kind)
            buffers.append(pltpu.VMEM((array.shape[0], columns), array.dtype))
        if weight[0] in factors:
            work += 4 * factors[weight[0]][0][0].shape[0] * weight[1] * weight[2] if len(factors[weight[0]]) > 1 and not isinstance(factors[weight[0]][0][0], tuple) else 800 * weight[1] * weight[2]
    chosen = {name: len(value) for name, value in factors.items()}
    former = tuple(former[0]) + tuple(former[1]) if former else ()
    anywhere = pl.BlockSpec(memory_space=pl.ANY)
    moved = sum(math.prod(v.shape) * 2 for v in outputs) * 2
    outs = pl.pallas_call(
        functools.partial(pack_body, layout, chosen, kinds, len(former)),
        out_shape=tuple(outputs),
        in_specs=[pl.BlockSpec(memory_space=pltpu.SMEM)] + [anywhere] * (len(arrays) + len(former)),
        out_specs=tuple([anywhere] * len(outputs)),
        scratch_shapes=buffers
        + [pltpu.VMEM(v.shape, v.dtype) for v in outputs]
        + [
            pltpu.VMEM((deepest, TILE), FULL),
            pltpu.SemaphoreType.DMA((len(buffers),)),
            pltpu.SemaphoreType.DMA((2 * blocks * len(chosen),)),
        ],
        input_output_aliases={1 + len(arrays) + n: n for n in range(len(former))},
        compiler_params=pltpu.CompilerParams(vmem_limit_bytes=ROOM),
        cost_estimate=pl.CostEstimate(flops=work, bytes_accessed=moved, transcendentals=0),
        name=name,
    )(info, *arrays, *former)
    return [list(outs[:blocks]), list(outs[blocks:])]


def unpack_body(moves, shapes, blocks, later, info, *refs):
    sources = len(shapes)
    inputs, refs = refs[:sources], refs[sources:]
    if later:
        refs = refs[later:]
    count = len(refs) - sources - 1
    outs, wide_refs, signals = refs[:count], refs[count : count + sources], refs[-1]
    place = info[2]
    copies = []
    for source, wide_ref in zip(inputs, wide_refs):
        wide_ref[...] = source[...].astype(FULL)
    for number, (source, way, hop, row, real, target, slot, column, columns, mark) in enumerate(moves):
        block = lax.rem(place + (blocks - hop if way == 0 else hop), blocks)
        rows = pl.ds(pl.multiple_of(block * real, 8), real)
        area = pl.ds(column, columns)
        out = outs[target]
        view = out.at[rows, area] if slot is None else out.at[slot, rows, area]
        copy = pltpu.make_async_copy(
            wide_refs[source].at[pl.ds(row, real), pl.ds(0, columns)], view, signals.at[number]
        )
        wanted = None
        if mark:
            wanted = info[0] == (1 if mark == 1 else 0)
        depth = out.shape[-2]
        if depth < blocks * real:
            inside = block * real < depth
            wanted = inside if wanted is None else jnp.logical_and(wanted, inside)
        copies.append((copy, wanted))
    for step in ("start", "wait"):
        for copy, wanted in copies:
            if wanted is None:
                getattr(copy, step)()
            else:
                pl.when(wanted)(getattr(copy, step))


def unpack(moves, inputs, outputs, former, blocks, info):
    spec = pl.BlockSpec(memory_space=pl.ANY)
    whole = pl.BlockSpec(memory_space=pltpu.VMEM)
    former = tuple(former or ())
    inputs = tuple(inputs)
    rows = [value.shape[0] for value in inputs]
    return pl.pallas_call(
        functools.partial(unpack_body, moves, rows, blocks, len(former)),
        out_shape=tuple(jax.ShapeDtypeStruct(shape, FULL) for shape in outputs),
        in_specs=[pl.BlockSpec(memory_space=pltpu.SMEM)] + [whole] * len(inputs) + [spec] * len(former),
        out_specs=tuple([spec] * len(outputs)),
        scratch_shapes=[pltpu.VMEM((count, UNIT), FULL) for count in rows]
        + [pltpu.SemaphoreType.DMA((len(moves),))],
        input_output_aliases={1 + len(inputs) + n: n for n in range(len(former))},
        compiler_params=pltpu.CompilerParams(vmem_limit_bytes=ROOM),
        cost_estimate=pl.CostEstimate(flops=0, bytes_accessed=6 * sum(rows) * UNIT, transcendentals=0),
        name="unpack",
    )(info, *inputs, *former)


CORES = [(0, 1), (1, 0)]


def to_other_core(values):
    return lax.ppermute(values, "tensor", CORES)


def to_other_section(values):
    return lax.ppermute(values, "section", CORES)


def to_layer(values, layer):
    return lax.ppermute(values, "section", [(1 - layer, layer)])


def ring_order():
    places = list(range(lax.axis_size("dp")))
    return places[0::2] + places[1::2][::-1]


def ring_place():
    place, count = lax.axis_index("dp"), lax.axis_size("dp")
    return jnp.where(place % 2 == 0, place // 2, count - 1 - place // 2)


def to_next(values, way):
    order = ring_order()
    route = list(zip(order, order[1:] + order[:1]))
    if way == 1:
        route = [(there, here) for here, there in route]
    return lax.ppermute(values, "dp", route)


def after(values, token):
    if token is None:
        return values
    return lax.optimization_barrier((values, token))[0]


class Ring:
    def __init__(self, parts):
        self.parts = parts
        self.count = len(parts[0])
        self.pieces = [[None] * self.count, [None] * self.count]
        self.step = 0
        self.last = 2 * (self.count - 1)
        self.flying = [to_next(parts[way][1], way) for way in range(2)]

    def advance(self, token):
        got = [after(self.flying[0], token), after(self.flying[1], token)]
        turn, count = self.step, self.count
        self.step += 1
        if turn < count - 1:
            got = [got[way] + self.parts[way][(turn + 2) % count] for way in range(2)]
        hop = max(turn - (count - 2), 0)
        if turn >= count - 2:
            for way in range(2):
                self.pieces[way][hop] = got[way]
        if self.step < self.last:
            self.flying = [to_next(got[way], way) for way in range(2)]
        return tuple(got), (hop if turn >= count - 2 else None)


def shards(
    text_stream,
    image_stream,
    region_mask,
    co_text_in,
    co_text_out,
    self_text_in,
    self_text_out,
    image_attn_in,
    image_attn_out,
    text_up,
    text_down,
    image_up,
    image_down,
    text_gain,
    text_shift,
    image_gain,
    image_shift,
):
    front = lax.axis_index("section") == 0
    core = lax.axis_index("tensor")
    blocks = lax.axis_size("dp")
    in_ring = blocks == 8
    place = ring_place() if in_ring else 0 * core
    info = jnp.stack([front.astype(jnp.int32), core.astype(jnp.int32), place.astype(jnp.int32)])
    pairs = text_stream.shape[1]
    half = pairs // 2
    real_t, real_i = text_stream.shape[2], image_stream.shape[2]
    rows_t, rows_i = round_up(real_t, 16), round_up(real_i, 16)
    wide_t, wide_i = text_stream.shape[3], image_stream.shape[3]
    text_size = D_TEXT // HEADS_TEXT
    image_size = D_IMAGE // HEADS_IMAGE

    def flat_rows(values, rows):
        grown = jnp.pad(values, ((0, 0), (0, rows - values.shape[1]), (0, 0)))
        return grown.reshape(values.shape[0] * rows, values.shape[2])

    def by_slot(weight):
        return jnp.transpose(weight, (1, 0, 2))

    own_t, own_i = half * rows_t, half * rows_i
    all_t, all_i = pairs * rows_t, pairs * rows_i
    keep = jnp.pad(region_mask, ((0, 0), (0, rows_i - real_i))).reshape(pairs, 1, rows_i)
    gain_t, shift_t, gain_i, shift_i = text_gain[0], text_shift[0], image_gain[0], image_shift[0]
    cross_in, image_in, single_in = by_slot(co_text_in), by_slot(image_attn_in[0]), by_slot(self_text_in)
    image_out, up_i, down_i = image_attn_out[0], image_up[0], image_down[0]
    up_t, down_t = text_up[0], text_down[0]
    image_out_2, cross_out_2 = to_other_core(image_out), to_other_core(co_text_out)
    up_i_2, down_i_2 = to_other_core(up_i), to_other_core(down_i)
    up_t_2, down_t_2 = to_other_core(up_t), to_other_core(down_t)
    cross = cross_in.shape[2]
    single = single_in.shape[2]
    ff_t, ff_i = up_t.shape[1], up_i.shape[1]
    tail_t = (up_t, down_t, up_t_2, down_t_2)
    tail_i = (up_i, down_i, up_i_2, down_i_2)

    far = (cross_in, image_in)
    xt_own, xt_other, xi_own, xi_other, tp, ip, ct_own, ct_give, ci_own, ci_give = launch(
        functools.partial(cross_forward, pairs, rows_t, rows_i, real_t),
        [shape_of(own_t, wide_t)] * 2
        + [shape_of(own_i, wide_i)] * 2
        + [shape_of(all_t, 3 * cross), shape_of(all_i, 3 * cross)]
        + [shape_of(own_t, cross)] * 2
        + [shape_of(own_i, cross)] * 2,
        (flat_rows(text_stream[0], rows_t), flat_rows(image_stream[0], rows_i), keep),
        far=far,
        scratch=[pltpu.VMEM((all_t, wide_t), LOW), pltpu.VMEM((all_i, wide_i), LOW)] + buffers_for(far),
        flag=info,
        work=6 * cross * (all_t * wide_t + all_i * wide_i),
        name="cross_forward",
    )
    ct_other, ci_other = ct_give, ci_give
    ci_2 = to_other_core(ci_give)
    ct_2 = to_other_core(ct_give)

    def run_first_tail(x, c0, c1, o0, o1, gain, shift, ff, rows, width, hidden, name):
        low_w, low_h = shape_of(rows, width), shape_of(rows, hidden)
        far = (o0, o1) + ff
        return launch(
            first_tail,
            [low_w, low_w, low_h, low_h]
            + [shape_of(rows, hidden, FULL)] * 2
            + [shape_of(rows, width, FULL), shape_of(rows, 128, FULL)] * 2,
            (x, c0, c1, gain, shift),
            far=far,
            scratch=[pltpu.VMEM((rows, width), FULL)] + buffers_for(far),
            flag=info,
            work=4 * rows * width * (o0.shape[0] + 2 * hidden),
            name=name,
        )

    bi, yi, hi0, hi1, si0, si1, ni1, ii1, ni2, ii2 = run_first_tail(
        after(xi_own, (up_t_2, down_t_2, cross_out_2, ct_2)), ci_own, ci_2, image_out, image_out_2, gain_i, shift_i,
        tail_i, own_i, wide_i, ff_i, "tail_i"
    )
    image_in_2, single_in_2, single_out_2 = [
        to_other_core(after(value, bi)) for value in (image_in, single_in, self_text_out)
    ]
    bi_here, bi = bi, to_layer(bi, 1)
    bt, yt, ht0, ht1, st0, st1, nt1, it1, nt2, it2 = run_first_tail(
        after(xt_own, bi_here), ct_own, ct_2, co_text_out, cross_out_2, gain_t, shift_t, tail_t, own_t, wide_t, ff_t, "tail_t"
    )

    def run_self(rows, real, size, width, hidden, x, w0, w1, masked, o0, o1, gain, shift, ff, seed, y, h0, h1, c, name):
        count = half * rows
        inner = w0.shape[2]
        low_w, low_h = shape_of(count, width), shape_of(count, hidden)
        outputs = [low_w, low_w, shape_of(count, cross), shape_of(count, 3 * cross)]
        outputs += [low_w, low_w, low_h, low_h, low_w, low_h] + [shape_of(2, width, FULL)] * 2
        outputs += [shape_of(count, 2 * width + hidden + 4 * cross)]
        scratch = [pltpu.VMEM((count, 3 * inner), LOW)] * 2
        scratch += [pltpu.VMEM((count, hidden), FULL)] * 2
        scratch += [pltpu.VMEM((count, width), FULL), pltpu.VMEM((count, 128), FULL)] * 2
        scratch += [pltpu.VMEM((count, width), FULL)] + [pltpu.VMEM((count, inner), LOW)] * 2
        scratch += [pltpu.VMEM((count, columns), LOW) for columns in (hidden, cross, 3 * cross)]
        weights = (w0, w1, o0, o1) + ff
        return launch(
            functools.partial(self_layer, masked, half, rows, real, size, cross),
            outputs,
            (x, seed, gain, shift, keep),
            far=weights + (y, h0, h1, c),
            scratch=scratch + buffers_for(weights),
            flag=info,
            work=8 * count * width * (4 * inner + 2 * hidden),
            name=name,
        )

    i2 = run_self(
        rows_i, real_i, image_size, wide_i, ff_i, bi, image_in, image_in_2, True, image_out, image_out_2,
        gain_i, shift_i, tail_i, xi_own, yi, hi0, hi1, ci_own, "self_i",
    )
    seed_i = to_layer(i2[1], 0)
    bt = to_layer(bt, 1)
    t2 = run_self(
        rows_t, real_t, text_size, wide_t, ff_t, after(bt, i2[1]), single_in, single_in_2, False,
        self_text_out, single_out_2, gain_t, shift_t, tail_t, xt_own, yt, ht0, ht1, ct_own, "self_t",
    )
    seed_t = to_layer(t2[1], 0)
    (oi, unused, ci_own, pi_own, dai, dfi, dui0, dui1, yi, hi0, dgi, dsi, give_i) = i2
    (ot, unused, ct_own, pt_own, dat, dft, dut0, dut1, yt, ht0, dgt, dst, give_t) = t2
    left_t, left_i = to_other_core(give_t), to_other_core(give_i)

    def run_tail_back(seed, kept, o0, o1, gain, ff, given, rows, width, hidden, name):
        low_w, low_h = shape_of(rows, width), shape_of(rows, hidden)
        outputs = [low_w, low_h, low_w] + [shape_of(2, width, FULL)] * 2
        outputs += [shape_of(rows, width, FULL), shape_of(rows, cross)]
        outputs += [shape_of(rows, 2 * width + hidden + cross)]
        s0, s1, n1, i1, n2, i2 = kept
        u0, d0, u1, d1 = ff
        late = (n2, i2, d0, s0, u0, d1, s1, u1, n1, i1, o0, o1)
        return launch(
            first_tail_back,
            outputs,
            (seed, gain),
            far=late + given,
            scratch=[pltpu.VMEM((rows, hidden), LOW)] + buffers_for(late),
            flag=info,
            work=4 * rows * width * (cross + 2 * hidden),
            name=name,
        )


    def choose(first, second):
        return jnp.where(front, first, second)

    ff_layout = Layout(
        blocks,
        [
            ("down_t", ff_t, wide_t),
            ("up_t", wide_t, ff_t),
            ("up_i", wide_i, ff_i),
            ("down_i", ff_i, wide_i),
        ],
    )
    attn_layout = Layout(
        blocks,
        [
            ("in_t", wide_t, 3 * cross),
            ("out_t", cross, wide_t),
            ("in_i", wide_i, 3 * cross),
            ("out_i", cross, wide_i),
            ("small", blocks * 16, UNIT),
        ],
    )
    text_rows = attn_layout.after["out_t"]

    out = run_tail_back(
        seed_i, (si0, si1, ni1, ii1, ni2, ii2), image_out, image_out_2, gain_i, tail_i,
        (dfi, dui0, dui1, dai, dgi, dsi), own_i, wide_i, ff_i, "tail_back_i",
    )
    dfi, dui0, dai, dgi, dsi, dri, dci_own, give_i = out
    right_i = to_other_core(give_i)
    out = run_tail_back(
        after(seed_t, dci_own), (st0, st1, nt1, it1, nt2, it2), co_text_out, cross_out_2, gain_t, tail_t,
        (dft, dut0, dut1, dat, dgt, dst), own_t, wide_t, ff_t, "tail_back_t",
    )
    dft, dut0, dat, dgt, dst, drt, dct_own, give_t = out
    right_t = to_other_core(give_t)
    small = jnp.concatenate([dgt, dst, dgi, dsi], axis=1)
    small = small + to_other_core(small)
    small_rows = round_up(-(-small.size // UNIT), blocks) // blocks
    small = jnp.pad(small.reshape(-1), (0, blocks * small_rows * UNIT - small.size))
    small = small.reshape(blocks, small_rows, UNIT)
    small = jnp.pad(small, ((0, 0), (0, 16 - small_rows), (0, 0))).reshape(blocks * 16, UNIT)
    ff_parts = pack(
        ff_layout,
        {
            "down_t": ((ht0, 0, ff_t), (left_t, wide_t, ff_t), (after(dft, small), 0, wide_t), (right_t, 0, wide_t)),
            "up_t": ((yt, 0, wide_t), (left_t, 0, wide_t), (dut0, 0, ff_t), (right_t, wide_t, ff_t)),
            "up_i": ((yi, 0, wide_i), (left_i, 0, wide_i), (dui0, 0, ff_i), (right_i, wide_i, ff_i)),
            "down_i": ((hi0, 0, ff_i), (left_i, wide_i, ff_i), (dfi, 0, wide_i), (right_i, 0, wide_i)),
        },
        info,
        "pack_ff",
    )
    token = ff_parts[0][1]
    ff = Ring(ff_parts) if in_ring else None
    far = (cross_in, image_in)
    out = launch(
        functools.partial(cross_backward, (wide_t, wide_i), pairs, rows_t, rows_i, real_t),
        [shape_of(own_t, 3 * cross)] * 2
        + [shape_of(own_i, 3 * cross)] * 2
        + [shape_of(own_t, wide_t, FULL)] * 2
        + [shape_of(own_i, wide_i, FULL)] * 2,
        (after(tp, token), ip, dct_own, dci_own, keep),
        far=far + (right_t, right_i, pt_own, left_t, pi_own, left_i),
        scratch=[pltpu.VMEM(v.shape, v.dtype) for v in far]
        + [pltpu.VMEM((own_t, cross), LOW), pltpu.VMEM((own_i, cross), LOW), pltpu.SemaphoreType.DMA((4,))],
        flag=info,
        work=6 * cross * (all_t * wide_t + all_i * wide_i),
        name="cross_backward",
    )
    dtp_own, dtp_other, dip_own, dip_other, dxt_own, dxt_give, dxi_own, dxi_give = out
    token = dtp_own
    if in_ring:
        token, unused = ff.advance(token)

    def columns(part, wide, hidden):
        starts = {"c": wide + hidden, "x": wide + hidden + 4 * cross}
        return starts[part]

    ct_column, xt_column = columns("c", wide_t, ff_t), columns("x", wide_t, ff_t)
    ci_column, xi_column = columns("c", wide_i, ff_i), columns("x", wide_i, ff_i)
    attn_parts = pack(
        attn_layout,
        {
            "in_t": (
                ((xt_own, 0), (bt, 0), wide_t),
                ((xt_other, 0), (left_t, xt_column), wide_t),
                (after(dtp_own, token), 0, 3 * cross),
                (dtp_other, 0, 3 * cross),
            ),
            "out_t": (
                (ct_own, 0, cross),
                ((ct_give, 0), (left_t, ct_column), cross),
                (dat, 0, wide_t),
                (right_t, wide_t + ff_t, wide_t),
            ),
            "in_i": (
                ((xi_own, 0), (bi, 0), wide_i),
                ((xi_other, 0), (left_i, xi_column), wide_i),
                (dip_own, 0, 3 * cross),
                (dip_other, 0, 3 * cross),
            ),
            "out_i": (
                (ci_own, 0, cross),
                ((ci_give, 0), (left_i, ci_column), cross),
                (dai, 0, wide_i),
                (right_i, wide_i + ff_i, wide_i),
            ),
            "small": ((small, 0, UNIT),),
        },
        info,
        "pack_attention",
    )

    def choose(first, second):
        return jnp.where(front, first, second)

    def result(rest, partial, other, output, rows, real, token):
        mine = choose(rest + partial + to_other_core(after(other, token)), output.astype(FULL))
        mine = mine.astype(LOW).reshape(half, rows, -1)[:, :real]
        got = to_other_core(mine)
        return jnp.concatenate(
            [jnp.where(core == 0, mine, got), jnp.where(core == 0, got, mine)], axis=0
        )[None]

    main_shapes = [
        (ff_t, wide_t),
        (wide_t, ff_t),
        (wide_i, ff_i),
        (ff_i, wide_i),
        (3, wide_i, cross),
        (cross, wide_i),
        (blocks * 16, UNIT),
    ]
    text_shapes = [(3, wide_t, cross), (cross, wide_t), (3, wide_t, single), (self_text_out.shape[0], wide_t)]
    main_moves, text_moves = [], []

    def move(target, source, way, row, real, unit, output, shape, mark=0):
        slot, column, columns = None, unit * UNIT, UNIT
        if len(shape) == 3:
            slot, column = column // cross, column % cross
            columns = min(UNIT, shape[2] - column)
        if columns > 0:
            target.append((source, way, row, real, output, slot, column, columns, mark))

    for index, unit, way, row, real in ff_layout.units:
        move(main_moves, way, way, row, real, unit, index, main_shapes[index])
    for index, unit, way, row, real in attn_layout.units:
        if index >= 2:
            move(main_moves, 2 + way, way, row, real, unit, index + 2, main_shapes[index + 2])
        else:
            for mark in (1, 2):
                move(text_moves, way + 2 * (mark - 1), way, row, real, unit, index, text_shapes[index], mark)
                move(text_moves, way + 4 - 2 * mark, way, row, real, unit, index + 2, text_shapes[index + 2], mark)

    main, text = None, None

    def shifted(moves, hop, source_shift, row_shift):
        result = []
        for source, way, row, *rest in moves:
            result.append((source_shift(source), way, hop, row + row_shift(source), *rest))
        return result

    def spread_main(hops, ff, attn, main):
        inputs, moves = [], []
        for number, hop in enumerate(hops):
            inputs += [ff[0][hop], ff[1][hop], attn[0][hop], attn[1][hop]]
            moves += shifted(main_moves, hop, lambda source: source + 4 * number, lambda source: 0)
        return unpack(moves, inputs, main_shapes, main, blocks, info)

    def spread_text(hops, attn, crossed, text):
        inputs, moves, both = [], [], text_rows[0] + text_rows[1]
        for hop in hops:
            inputs += [attn[0][hop], attn[1][hop]]
        places = []
        for array in crossed:
            places += [(len(inputs), row) for row in range(0, array.shape[0], both)]
            inputs.append(array)
        for number, hop in enumerate(hops):
            moves += shifted(
                text_moves,
                hop,
                lambda source: source + 2 * number if source < 2 else places[number][0],
                lambda source: 0 if source < 2 else places[number][1] + (source - 2) * text_rows[0],
            )
        return unpack(moves, inputs, text_shapes, text, blocks, info)

    def cross_over(attn, hops):
        return to_other_section(
            jnp.concatenate([attn[way][hop][: text_rows[way]] for hop in hops for way in range(2)], axis=0)
        )

    if in_ring:
        attn = Ring(attn_parts)
        token = attn_parts[0][1]
        results = (
            result(drt, dxt_own, dxt_give, ot, rows_t, real_t, token),
            result(dri, dxi_own, dxi_give, oi, rows_i, real_i, token),
        )
        token = (token, results)
        groups = [(0, 1), (2, 3), (4, 5), (6,), (7,)]
        crossed = [None] * len(groups)
        while attn.step < attn.last:
            if ff.step < ff.last:
                token, unused = ff.advance(token)
            token, hop = attn.advance(token)
            if hop is None:
                continue
            if hop == 2:
                first = after(crossed[0], token)
                relay = [to_next(first[: text_rows[0]], 1), to_next(first[text_rows[0] : sum(text_rows)], 0)]
            if hop == 4:
                crossed[-1] = jnp.concatenate([after(value, token) for value in relay], axis=0)
                token = (token, crossed[-1])
            for number, group in enumerate(groups):
                if hop == group[-1]:
                    if number < len(groups) - 1:
                        crossed[number] = cross_over(attn.pieces, group)
                    main = spread_main(group, ff.pieces, attn.pieces, main)
                    token = (token, main)
                elif number and hop == group[0] and len(group) > 1:
                    text = spread_text(groups[number - 1], attn.pieces, [crossed[number - 1]], text)
                    token = (token, text)
        text = spread_text(groups[-3], attn.pieces, crossed[-3:-2], text)
        text = spread_text((6, 7), attn.pieces, crossed[-2:], text)
    else:
        results = (
            result(drt, dxt_own, dxt_give, ot, rows_t, real_t, token),
            result(dri, dxi_own, dxi_give, oi, rows_i, real_i, token),
        )
        ff, attn = lax.psum((ff_parts, attn_parts), "dp")
        for hop in range(0, blocks, 2):
            main = spread_main((hop, hop + 1), ff, attn, main)
            text = spread_text((hop, hop + 1), attn, [cross_over(attn, (hop, hop + 1))], text)
    down_t_grad, up_t_grad, up_i_grad, down_i_grad, in_i_grad, out_i_grad, small = main
    co_in_grad, co_out_grad, self_in_grad, self_out_grad = text
    small = small.reshape(blocks, 16, UNIT)[:, :small_rows].reshape(-1)[: 4 * (wide_t + wide_i)]
    small = small.reshape(2, 2 * (wide_t + wide_i))
    small = jnp.split(small, [wide_t, 2 * wide_t, 2 * wide_t + wide_i], axis=1)

    return (
        results[0],
        results[1],
        by_slot(co_in_grad),
        co_out_grad,
        by_slot(self_in_grad),
        self_out_grad,
        by_slot(in_i_grad)[None],
        out_i_grad[None],
        up_t_grad[None],
        down_t_grad[None],
        up_i_grad[None],
        down_i_grad[None],
        small[0][None],
        small[1][None],
        small[2][None],
        small[3][None],
    )


def solution(mesh):
    in_specs = (
        P("section", "dp", None, None),
        P("section", "dp", None, None),
        P("dp", None),
        P(None, None, "tensor"),
        P("tensor", None),
        P(None, None, "tensor"),
        P("tensor", None),
        P("section", None, None, "tensor"),
        P("section", "tensor", None),
        P("section", None, "tensor"),
        P("section", "tensor", None),
        P("section", None, "tensor"),
        P("section", "tensor", None),
        P("section", None, None),
        P("section", None, None),
        P("section", None, None),
        P("section", None, None),
    )
    out_specs = (
        P("section", "dp", None, None),
        P("section", "dp", None, None),
        P(None, None, "tensor"),
        P("tensor", None),
        P(None, None, "tensor"),
        P("tensor", None),
        P("section", None, None, "tensor"),
        P("section", "tensor", None),
        P("section", None, "tensor"),
        P("section", "tensor", None),
        P("section", None, "tensor"),
        P("section", "tensor", None),
        P("section", None, None),
        P("section", None, None),
        P("section", None, None),
        P("section", None, None),
    )
    return jax.shard_map(shards, mesh=mesh, in_specs=in_specs, out_specs=out_specs, check_vma=False)
```

```python
import functools
import math

import jax
import jax.numpy as jnp
from jax import lax
from jax.experimental import pallas as pl
from jax.experimental.pallas import tpu as pltpu
from jax.sharding import PartitionSpec as P

D_TEXT = 768
HEADS_TEXT = 12
D_IMAGE = 1024
HEADS_IMAGE = 8
D_CO = 1024
HEADS_CO = 8

LOW = jnp.bfloat16
FULL = jnp.float32
TILE = 512
UNIT = 256
ROOM = 56 * 1024 * 1024


def times(left, right):
    return jnp.dot(left, right, preferred_element_type=FULL)


def times_back(left, right):
    return lax.dot_general(left, right, (((1,), (1,)), ((), ())), preferred_element_type=FULL)


def back_times(left, right):
    return lax.dot_general(left, right, (((0,), (0,)), ((), ())), preferred_element_type=FULL)


def norm_rows(rows):
    centre = rows - jnp.mean(rows, axis=-1, keepdims=True)
    spread = jnp.mean(centre * centre, axis=-1, keepdims=True)
    inverse = lax.rsqrt(spread + 1e-05)
    return centre * inverse, inverse


def norm_back(unit, inverse, gain, grad):
    scaled = grad * gain
    first = jnp.mean(scaled, axis=-1, keepdims=True)
    second = jnp.mean(scaled * unit, axis=-1, keepdims=True)
    dgain = jnp.sum(grad * unit, axis=0, keepdims=True)
    dshift = jnp.sum(grad, axis=0, keepdims=True)
    return inverse * (scaled - first - unit * second), dgain, dshift


def gelu_both(inputs):
    rate = 0.7978845608028654
    square = inputs * inputs
    bent = jnp.tanh(rate * inputs * (1.0 + 0.044715 * square))
    half = 0.5 * (1.0 + bent)
    slope = half + 0.5 * inputs * (1.0 - bent * bent) * rate * (1.0 + 0.134145 * square)
    return inputs * half, slope


def heads_of(query, size):
    if size == query.shape[1]:
        return [query]
    lower = lax.broadcasted_iota(jnp.int32, (1, query.shape[1]), 1) < size
    low = lower.astype(FULL).astype(LOW)
    return [query * low, query * (1 - low)]


def merged(parts, size):
    if len(parts) == 1:
        return parts[0]
    return jnp.where(lax.broadcasted_iota(jnp.int32, parts[0].shape, 1) < size, parts[0], parts[1])


def softmax_all(pairs, alloweds, size):
    scores = [times_back(query, keys) for query, keys in pairs]
    scores = [
        jnp.where(allowed, score * (1.0 / math.sqrt(size)), -1000000000.0)
        for score, allowed in zip(scores, alloweds)
    ]
    tops = [jnp.max(score, axis=-1, keepdims=True) for score in scores]
    raised = [jnp.exp(score - top) for score, top in zip(scores, tops)]
    shares = [1.0 / jnp.sum(value, axis=-1, keepdims=True) for value in raised]
    return [value * share for value, share in zip(raised, shares)]


def attend_all(units, size):
    singles = [(q, k, v, a) for query, k, v, a in units for q in heads_of(query, size)]
    weights = softmax_all([one[:2] for one in singles], [one[3] for one in singles], size)
    contexts = [times(w.astype(LOW), one[2]) for w, one in zip(weights, singles)]
    heads = len(singles) // len(units)
    return [merged(contexts[n * heads : (n + 1) * heads], size).astype(LOW) for n in range(len(units))]


def attend_back_all(units, size):
    scaling = 1.0 / math.sqrt(size)
    singles = [
        (q, k, v, a, d, query, dcontext)
        for query, k, v, a, dcontext in units
        for q, d in zip(heads_of(query, size), heads_of(dcontext, size))
    ]
    weights = softmax_all([one[:2] for one in singles], [one[3] for one in singles], size)
    dweights = [times_back(one[4], one[2]) for one in singles]
    dvalues = [back_times(w.astype(LOW), one[6]) for w, one in zip(weights, singles)]
    sums = [jnp.sum(dw * w, axis=-1, keepdims=True) for dw, w in zip(dweights, weights)]
    dscores = [(w * (dw - s)).astype(LOW) for w, dw, s in zip(weights, dweights, sums)]
    dqueries = [times(ds, one[1]) * scaling for ds, one in zip(dscores, singles)]
    dkeys = [back_times(ds, one[5]) * scaling for ds, one in zip(dscores, singles)]
    heads = len(singles) // len(units)
    return [
        [merged(grads[n * heads : (n + 1) * heads], size).astype(LOW) for grads in (dqueries, dkeys, dvalues)]
        for n in range(len(units))
    ]


def wide(column):
    return jnp.broadcast_to(column, (column.shape[0], 128))


class Late:
    def __init__(self, source, target, signal):
        self.target = target
        self.copy = pltpu.make_async_copy(source, target, signal)
        self.copy.start()
        self.here = False

    def get(self):
        if not self.here:
            self.copy.wait()
            self.here = True
        return self.target


class Here:
    def __init__(self, target):
        self.target = target

    def get(self):
        return self.target


def fetch(sources, targets, signals):
    return [Late(s, t, signals.at[n]) for n, (s, t) in enumerate(zip(sources, targets))]


def pass_through(sources, targets, signals):
    copies = [
        pltpu.make_async_copy(s, t, signals.at[n]) for n, (s, t) in enumerate(zip(sources, targets))
    ]
    for copy in copies:
        copy.start()
    for copy in copies:
        copy.wait()


def tail_forward(residual, contexts, out_w, gain, shift, up_w, down_w, kept, mixed, leave=None):
    normed_ref, hidden, slopes, unit1, inv1, unit2, inv2 = kept
    branch = times(contexts[0], out_w[0].get()[...]) + times(contexts[1], out_w[1].get()[...])
    unit, inverse = norm_rows(residual.astype(FULL) + branch)
    unit1[...] = unit
    inv1[...] = wide(inverse)
    normed = unit * gain[0:1, :] + shift[0:1, :]
    normed_ref[...] = normed.astype(LOW)
    mixed[...] = normed
    if leave is not None:
        leave.go(normed_ref, unit1, inv1)
    for half in range(2):
        up, down = up_w[half].get(), down_w[half].get()
        for start in range(0, up.shape[1], TILE):
            span = pl.ds(start, TILE)
            value, slope = gelu_both(times(normed_ref[...], up[:, span]))
            hidden[half][:, span] = value.astype(LOW)
            slopes[half][:, span] = slope
            mixed[...] += times(hidden[half][:, span], down[span, :])
        if leave is not None:
            leave.go(hidden[half], slopes[half])
    unit, inverse = norm_rows(mixed[...])
    unit2[...] = unit
    inv2[...] = wide(inverse)
    return unit * gain[1:2, :] + shift[1:2, :]


def tail_backward(seed, kept, out_w, gain, up_w, down_w, grads, total, leave=None):
    slopes, unit1, inv1, unit2, inv2 = kept
    df, du, da, dgain, dshift = grads
    dsecond, dgain1, dshift1 = norm_back(
        unit2.get()[...], inv2.get()[:, 0:1], gain[1:2, :], seed
    )
    total[...] = dsecond
    df[...] = dsecond.astype(LOW)
    for half in range(2):
        up, down, slope = up_w[half].get(), down_w[half].get(), slopes[half].get()
        for start in range(0, up.shape[1], TILE):
            span = pl.ds(start, TILE)
            dhidden = times_back(df[...], down[span, :])
            du[half][:, span] = (dhidden * slope[:, span]).astype(LOW)
            total[...] += times_back(du[half][:, span], up[:, span])
    dfirst, dgain0, dshift0 = norm_back(
        unit1.get()[...], inv1.get()[:, 0:1], gain[0:1, :], total[...]
    )
    dgain[...] = jnp.concatenate([dgain0, dgain1], axis=0)
    dshift[...] = jnp.concatenate([dshift0, dshift1], axis=0)
    total[...] = dfirst
    da[...] = dfirst.astype(LOW)
    if leave is not None:
        leave.go(df, du[0], da, total)
    return [times_back(da[...], w.get()[...]).astype(LOW) for w in out_w]


def shape_of(rows, columns, kind=LOW):
    return jax.ShapeDtypeStruct((rows, columns), kind)


class Leave:
    def __init__(self, buffers, targets, signals):
        self.buffers, self.targets, self.signals = buffers, targets, signals
        self.begun = {}

    def go(self, *buffers):
        for buffer in buffers:
            number = [one is buffer for one in self.buffers].index(True)
            copy = pltpu.make_async_copy(buffer, self.targets[number], self.signals.at[number])
            copy.start()
            self.begun[number] = copy

    def finish(self):
        self.go(*[one for number, one in enumerate(self.buffers) if number not in self.begun])
        for copy in self.begun.values():
            copy.wait()
        self.begun = {}


def launch(body, outputs, args, far=(), scratch=(), flag=None, work=0, name=None):
    whole, anywhere = pl.BlockSpec(memory_space=pltpu.VMEM), pl.BlockSpec(memory_space=pl.ANY)
    moved = sum(
        math.prod(v.shape) * v.dtype.itemsize for v in tuple(args) + tuple(far) + tuple(outputs)
    )
    total, results = len(args) + len(far), len(outputs)

    def whole_body(info, *refs):
        targets, refs = refs[total : total + results], refs[:total] + refs[total + results :]
        outs, signals = refs[total : total + results], refs[total + results]
        body(Leave(outs, targets, signals), info, *refs[:total], *outs, *refs[total + results + 1 :])

    own = [pltpu.VMEM(v.shape, v.dtype) for v in outputs] + [pltpu.SemaphoreType.DMA((results,))]
    return pl.pallas_call(
        whole_body,
        out_shape=tuple(outputs),
        in_specs=[pl.BlockSpec(memory_space=pltpu.SMEM)] + [whole] * len(args) + [anywhere] * len(far),
        out_specs=tuple([anywhere] * results),
        scratch_shapes=own + list(scratch),
        compiler_params=pltpu.CompilerParams(vmem_limit_bytes=ROOM),
        cost_estimate=pl.CostEstimate(flops=work, bytes_accessed=moved, transcendentals=0),
        name=name,
    )(flag, *args, *far)


def buffers_for(far):
    return [pltpu.VMEM(v.shape, v.dtype) for v in far] + [pltpu.SemaphoreType.DMA((len(far),))]


def rows_at(pair, rows):
    return pl.ds(pl.multiple_of(pair * rows, 16), rows)


def slab(index):
    return pl.ds(index * 128, 128)


def cross_forward(
    pairs, rows_t, rows_i, real_t, leave, info, x_t, x_i, keep, far_t, far_i,
    xt_own, xt_other, xi_own, xi_other, tp, ip, ct_own, ct_other, ci_own, ci_other, xt, xi, wt, wi, signals,
):
    half = pairs // 2
    for place in range(pairs):
        pair = lax.rem(place + half * info[1], pairs)
        text, image = x_t[rows_at(pair, rows_t), :], x_i[rows_at(pair, rows_i), :]
        xt[place * rows_t : (place + 1) * rows_t, :] = text
        xi[place * rows_i : (place + 1) * rows_i, :] = image
        inside = place % half
        (xt_own, xt_other)[place // half][inside * rows_t : (inside + 1) * rows_t, :] = text
        (xi_own, xi_other)[place // half][inside * rows_i : (inside + 1) * rows_i, :] = image

    @pl.when(info[0] == 0)
    def idle():
        leave.finish()

    @pl.when(info[0] == 1)
    def work():
        width = ct_own.shape[1]
        weights = fetch((far_t, far_i), (wt, wi), signals)
        leave.go(xt_own, xt_other, xi_own, xi_other)
        for late, x, p in ((weights[0], xt, tp), (weights[1], xi, ip)):
            for slot in range(3):
                p[:, pl.ds(slot * width, width)] = times(x[...], late.get()[slot]).astype(LOW)
            leave.go(p)
        text_keys = lax.broadcasted_iota(jnp.int32, (1, rows_t), 1) < real_t
        slabs = width // 128

        def each(pair, carry):
            at_t, at_i = rows_at(pair, rows_t), rows_at(pair, rows_i)
            for group, ct, ci in ((0, ct_own, ci_own), (half, ct_other, ci_other)):
                from_t, from_i = rows_at(pair + group, rows_t), rows_at(pair + group, rows_i)
                kept = keep[lax.rem(pair + group + half * info[1], pairs)] > 0
                texts, images = [], []
                for n in range(slabs):
                    first, second, third = slab(n), slab(slabs + n), slab(2 * slabs + n)
                    texts.append((tp[from_t, first], ip[from_i, second], ip[from_i, third], kept))
                    images.append((ip[from_i, first], tp[from_t, second], tp[from_t, third], text_keys))
                results = zip(attend_all(texts, 128), attend_all(images, 128))
                for n, (text, image) in enumerate(results):
                    ct[at_t, slab(n)] = text
                    ci[at_i, slab(n)] = image
            return carry

        lax.fori_loop(0, half, each, 0, unroll=True)
        leave.finish()


def first_tail(
    leave, info, x, c0, c1, gain, shift, *refs
):
    far, refs = refs[:6], refs[6:]
    out, y, h0, h1, s0, s1, n1, i1, n2, i2, mixed = refs[:11]
    near, signals = refs[11:17], refs[17]

    @pl.when(info[0] == 1)
    def work():
        o0, o1, u0, d0, u1, d1 = fetch(far, near, signals)
        kept = (y, (h0, h1), (s0, s1), n1, i1, n2, i2)
        out[...] = tail_forward(
            x[...], (c0[...], c1[...]), (o0, o1), gain, shift, (u0, u1), (d0, d1), kept, mixed, leave
        ).astype(LOW)
        leave.finish()


def self_layer(
    masked, half, rows, real, size, stride, leave, info, x, seed, gain, shift, keep, *refs
):
    far, refs = refs[:12], refs[12:]
    (out, dx, c0, p0, da, df, du0, du1, y, h0, dgain, dshift, give) = refs[:13]
    (q0, q1, s0, s1, n1, i1, n2, i2, mixed, dc0, dc1, h1, c1, p1) = refs[13:27]
    near, signals = refs[27:35], refs[35]
    width = q0.shape[1] // 3
    wide_x, wide_h, wide_c = x.shape[1], h1.shape[1], c1.shape[1]
    spans = []
    for columns in (wide_x, wide_h, wide_c, p1.shape[1], wide_x):
        spans.append(pl.ds(sum(span.size for span in spans), columns))

    @pl.when(info[0] == 1)
    def pass_on():
        targets = (y, h0, c0, give.at[:, spans[0]], give.at[:, spans[1]])
        pass_through((far[8], far[9], far[11], far[8], far[10]), targets, signals)
        leave.go(y, h0, c0, give)
        for copy in leave.begun.values():
            copy.wait()
        leave.begun = {}

    @pl.when(info[0] == 0)
    def work():
        w0, w1, o0, o1, u0, d0, u1, d1 = fetch(far[:8], near, signals)
        slabs = width // 128
        if c0.shape[1] != width:
            rest = pl.ds(width, c0.shape[1] - width)
            c0[:, rest] = jnp.zeros((c0.shape[0], c0.shape[1] - width), LOW)
            c1[:, rest] = jnp.zeros((c0.shape[0], c0.shape[1] - width), LOW)
            for slot in range(3):
                rest = pl.ds(slot * stride + width, stride - width)
                p0[:, rest] = jnp.zeros((p0.shape[0], stride - width), LOW)
                p1[:, rest] = jnp.zeros((p0.shape[0], stride - width), LOW)
        for w, q in ((w0, q0), (w1, q1)):
            for slot in range(3):
                q[:, pl.ds(slot * width, width)] = times(x[...], w.get()[slot]).astype(LOW)

        def allowed(pair):
            if not masked:
                return lax.broadcasted_iota(jnp.int32, (1, rows), 1) < real
            return keep[pair + half * info[1]] > 0

        def forward(pair, carry):
            at = rows_at(pair, rows)
            kept = allowed(pair)
            units = [
                (q[at, slab(n)], q[at, slab(slabs + n)], q[at, slab(2 * slabs + n)], kept)
                for q in (q0, q1)
                for n in range(slabs)
            ]
            results = attend_all(units, size)
            for n, value in enumerate(results):
                (c0, c1)[n // slabs][at, slab(n % slabs)] = value
            return carry

        lax.fori_loop(0, half, forward, 0, unroll=True)
        leave.go(c0)
        used = pl.ds(0, width)
        kept = (y, (h0, h1), (s0, s1), n1, i1, n2, i2)
        out[...] = tail_forward(
            x[...], (c0[:, used], c1[:, used]), (o0, o1), gain, shift, (u0, u1), (d0, d1), kept, mixed
        ).astype(LOW)
        leave.go(out, y, h0)
        held = ((Here(s0), Here(s1)), Here(n1), Here(i1), Here(n2), Here(i2))
        dcs = tail_backward(
            seed[...].astype(FULL),
            held,
            (o0, o1),
            gain,
            (u0, u1),
            (d0, d1),
            (df, (du0, du1), da, dgain, dshift),
            mixed,
        )
        leave.go(da, df, du0, du1, dgain, dshift)
        dc0[...] = dcs[0]
        dc1[...] = dcs[1]

        def backward(pair, carry):
            at = rows_at(pair, rows)
            kept = allowed(pair)
            units = [
                (q[at, slab(n)], q[at, slab(slabs + n)], q[at, slab(2 * slabs + n)], kept, dc[at, slab(n)])
                for q, dc in ((q0, dc0), (q1, dc1))
                for n in range(slabs)
            ]
            results = attend_back_all(units, size)
            for n, grads in enumerate(results):
                for slot in range(3):
                    column = slot * stride + (n % slabs) * 128
                    (p0, p1)[n // slabs][at, pl.ds(column, 128)] = grads[slot]
            return carry

        lax.fori_loop(0, half, backward, 0, unroll=True)
        for span, value in zip(spans, (y, h1, c1, p1, x)):
            give[:, span] = value[...]
        leave.go(p0, give)
        for w, p in ((w0, p0), (w1, p1)):
            for slot in range(3):
                mixed[...] += times_back(p[:, pl.ds(slot * stride, width)], w.get()[slot])
        dx[...] = mixed[...].astype(LOW)
        leave.finish()


def first_tail_back(leave, info, seed, gain, *refs):
    far, refs = refs[:18], refs[18:]
    df, du0, da, dgain, dshift, dres, dc0, give = refs[:8]
    du1, near, signals = refs[8], refs[9:21], refs[21]
    spans = []
    for columns in (df.shape[1], du1.shape[1], da.shape[1], dc0.shape[1]):
        spans.append(pl.ds(sum(span.size for span in spans), columns))

    @pl.when(info[0] == 0)
    def pass_on():
        df_in, du0_in, du1_in, da_in, dgain_in, dshift_in = far[12:]
        pass_through(
            (df_in, du0_in, da_in, dgain_in, dshift_in, df_in, du1_in, da_in),
            (df, du0, da, dgain, dshift) + tuple(give.at[:, span] for span in spans[:3]),
            signals,
        )
        leave.finish()

    @pl.when(info[0] == 1)
    def work():
        n2, i2, d0, s0, u0, d1, s1, u1, n1, i1, o0, o1 = fetch(far[:12], near, signals)
        dcs = tail_backward(
            seed[...].astype(FULL),
            ((s0, s1), n1, i1, n2, i2),
            (o0, o1),
            gain,
            (u0, u1),
            (d0, d1),
            (df, (du0, du1), da, dgain, dshift),
            dres,
            leave,
        )
        dc0[...] = dcs[0]
        for span, value in zip(spans, (df[...], du1[...], da[...], dcs[1])):
            give[:, span] = value
        leave.finish()


def cross_backward(
    wides, pairs, rows_t, rows_i, real_t, leave, info,
    tp, ip, dct_own, dci_own, keep, *refs
):
    far, refs = refs[:8], refs[8:]
    dtp_own, dtp_other, dip_own, dip_other, dxt_own, dxt_other, dxi_own, dxi_other = refs[:8]
    wt, wi, dct_other, dci_other, signals = refs[8:]
    width = dct_own.shape[1]
    slabs = width // 128
    half = pairs // 2

    @pl.when(info[0] == 0)
    def pass_on():
        sources = []
        for mine, got in ((far[4], far[5]), (far[6], far[7])):
            start = got.shape[1] - wides[len(sources) // 2] - mine.shape[1]
            sources += [mine, got.at[:, pl.ds(start, mine.shape[1])]]
        pass_through(sources, (dtp_own, dtp_other, dip_own, dip_other), signals)
        leave.finish()

    @pl.when(info[0] == 1)
    def work():
        got = [far[n].at[:, pl.ds(far[n].shape[1] - width, width)] for n in (2, 3)]
        weights = fetch(
            (got[0], got[1], far[0], far[1]), (dct_other, dci_other, wt, wi), signals
        )
        weights[0].get()
        weights[1].get()
        weights = weights[2:]
        text_keys = lax.broadcasted_iota(jnp.int32, (1, rows_t), 1) < real_t

        def each(pair, carry):
            at_t, at_i = rows_at(pair, rows_t), rows_at(pair, rows_i)
            for group, dct, dci, dtp, dip in (
                (0, dct_own, dci_own, dtp_own, dip_own),
                (half, dct_other, dci_other, dtp_other, dip_other),
            ):
                from_t, from_i = rows_at(pair + group, rows_t), rows_at(pair + group, rows_i)
                kept = keep[lax.rem(pair + group + half * info[1], pairs)] > 0
                texts, images = [], []
                for n in range(slabs):
                    first, second, third = slab(n), slab(slabs + n), slab(2 * slabs + n)
                    texts.append((tp[from_t, first], ip[from_i, second], ip[from_i, third], kept, dct[at_t, first]))
                    images.append((ip[from_i, first], tp[from_t, second], tp[from_t, third], text_keys, dci[at_i, first]))
                results = zip(attend_back_all(texts, 128), attend_back_all(images, 128))
                for n, (text, image) in enumerate(results):
                    first, second, third = slab(n), slab(slabs + n), slab(2 * slabs + n)
                    dtp[at_t, first], dip[at_i, second], dip[at_i, third] = text
                    dip[at_i, first], dtp[at_t, second], dtp[at_t, third] = image
            return carry

        lax.fori_loop(0, half, each, 0, unroll=True)
        leave.go(dtp_own, dtp_other, dip_own, dip_other)
        for late, triples in (
            (weights[0], ((dtp_own, dxt_own), (dtp_other, dxt_other))),
            (weights[1], ((dip_own, dxi_own), (dip_other, dxi_other))),
        ):
            for dp, dx in triples:
                total = times_back(dp[:, pl.ds(0, width)], late.get()[0])
                for slot in range(1, 3):
                    total += times_back(dp[:, pl.ds(slot * width, width)], late.get()[slot])
                dx[...] = total
                leave.go(dx)
        leave.finish()


def round_up(value, step):
    return -(-value // step) * step


class Layout:
    def __init__(self, blocks, weights, firsts=None):
        self.blocks, self.weights = blocks, weights
        self.sizes = [0, 0]
        self.units = []
        self.after = {}
        for index, (name, depth, width) in enumerate(weights):
            real = depth // blocks
            for unit in range(width // UNIT):
                way = 0 if self.sizes[0] <= self.sizes[1] else 1
                if firsts:
                    way = 0 if unit < firsts[name] else 1
                self.units.append((index, unit, way, self.sizes[way], real))
                self.sizes[way] += round_up(real, 16)
            self.after[name] = list(self.sizes)


def pack_body(layout, chosen, kinds, later, info, *refs):
    blocks, weights = layout.blocks, layout.weights
    place = info[2]
    arrays = 1 + max(max(k[0], k[2] or 0) for k in kinds)
    sources, refs = refs[:arrays], refs[arrays + later :]
    targets, refs = refs[: 2 * blocks], refs[2 * blocks :]
    buffers, refs = refs[: len(kinds)], refs[len(kinds) :]
    outs, (total, signals, out_signals) = refs[: 2 * blocks], refs[2 * blocks :]
    waits = []
    for number, (first, column, second, other) in enumerate(kinds):
        buffer = buffers[number]

        def copy(source, start):
            view = sources[source].at[:, pl.ds(start, buffer.shape[1])]
            return pltpu.make_async_copy(view, buffer, signals.at[number])

        if second is None:
            copy(first, column).start()
        else:
            pl.when(info[0] == 1)(copy(first, column).start)
            pl.when(info[0] == 0)(copy(second, other).start)
        waits.append(copy(first, column))
    position, copies = 0, []
    for index, (name, depth, width) in enumerate(weights):
        if name not in chosen:
            continue
        mine = buffers[position : position + chosen[name]]
        for wait in waits[position : position + chosen[name]]:
            wait.wait()
        position += chosen[name]
        span = TILE if width % TILE == 0 else UNIT
        units = [unit for unit in layout.units if unit[0] == index]
        for column in range(0, width, span):
            area = pl.ds(column, span)
            if chosen[name] == 1:
                total[0:depth, 0:span] = mine[0][:, area]
            else:
                x0, x1, y0, y1 = mine
                total[0:depth, 0:span] = back_times(x0[...], y0[:, area]) + back_times(
                    x1[...], y1[:, area]
                )
            for unused, unit, way, row, real in units:
                inside = unit * UNIT - column
                if not 0 <= inside < span:
                    continue
                rows = round_up(real, 16)
                for hop in range(blocks):
                    block = lax.rem(place + (blocks - hop if way == 0 else hop), blocks)
                    source = pl.ds(pl.multiple_of(block * real, 8), rows)
                    outs[way * blocks + hop][row : row + rows, :] = total[
                        source, inside : inside + UNIT
                    ].astype(LOW)
        for way in range(2):
            rows = [(unit[3], unit[3] + round_up(unit[4], 16)) for unit in units if unit[2] == way]
            if not rows:
                continue
            part = pl.ds(rows[0][0], rows[-1][1] - rows[0][0])
            for hop in range(blocks):
                number = way * blocks + hop
                out = pltpu.make_async_copy(
                    outs[number].at[part], targets[number].at[part], out_signals.at[len(copies)]
                )
                out.start()
                copies.append(out)
    for out in copies:
        out.wait()


def pack(layout, factors, info, name, former=None):
    blocks = layout.blocks
    outputs = [shape_of(layout.sizes[way], UNIT) for way in range(2) for hop in range(blocks)]
    deepest = max(weight[1] for weight in layout.weights) + 32
    arrays, kinds, buffers, work = [], [], [], 0

    def number_of(array):
        for number, one in enumerate(arrays):
            if one is array:
                return number
        arrays.append(array)
        return len(arrays) - 1

    for weight in layout.weights:
        for first, second, columns in factors.get(weight[0], ()):
            if isinstance(first, tuple):
                kind = (number_of(first[0]), first[1], number_of(second[0]), second[1])
                array = first[0]
            else:
                kind = (number_of(first), second, None, None)
                array = first
            kinds.append(kind)
            buffers.append(pltpu.VMEM((array.shape[0], columns), array.dtype))
        if weight[0] in factors:
            work += 4 * factors[weight[0]][0][0].shape[0] * weight[1] * weight[2] if len(factors[weight[0]]) > 1 and not isinstance(factors[weight[0]][0][0], tuple) else 800 * weight[1] * weight[2]
    chosen = {name: len(value) for name, value in factors.items()}
    former = tuple(former[0]) + tuple(former[1]) if former else ()
    anywhere = pl.BlockSpec(memory_space=pl.ANY)
    moved = sum(math.prod(v.shape) * 2 for v in outputs) * 2
    outs = pl.pallas_call(
        functools.partial(pack_body, layout, chosen, kinds, len(former)),
        out_shape=tuple(outputs),
        in_specs=[pl.BlockSpec(memory_space=pltpu.SMEM)] + [anywhere] * (len(arrays) + len(former)),
        out_specs=tuple([anywhere] * len(outputs)),
        scratch_shapes=buffers
        + [pltpu.VMEM(v.shape, v.dtype) for v in outputs]
        + [
            pltpu.VMEM((deepest, TILE), FULL),
            pltpu.SemaphoreType.DMA((len(buffers),)),
            pltpu.SemaphoreType.DMA((2 * blocks * len(chosen),)),
        ],
        input_output_aliases={1 + len(arrays) + n: n for n in range(len(former))},
        compiler_params=pltpu.CompilerParams(vmem_limit_bytes=ROOM),
        cost_estimate=pl.CostEstimate(flops=work, bytes_accessed=moved, transcendentals=0),
        name=name,
    )(info, *arrays, *former)
    return [list(outs[:blocks]), list(outs[blocks:])]


def unpack_body(moves, shapes, blocks, later, info, *refs):
    sources = len(shapes)
    inputs, refs = refs[:sources], refs[sources:]
    if later:
        refs = refs[later:]
    count = len(refs) - sources - 1
    outs, wide_refs, signals = refs[:count], refs[count : count + sources], refs[-1]
    place = info[2]
    copies = []
    for source, wide_ref in zip(inputs, wide_refs):
        wide_ref[...] = source[...].astype(FULL)
    for number, (source, way, hop, row, real, target, slot, column, columns, mark) in enumerate(moves):
        block = lax.rem(place + (blocks - hop if way == 0 else hop), blocks)
        rows = pl.ds(pl.multiple_of(block * real, 8), real)
        area = pl.ds(column, columns)
        out = outs[target]
        view = out.at[rows, area] if slot is None else out.at[slot, rows, area]
        copy = pltpu.make_async_copy(
            wide_refs[source].at[pl.ds(row, real), pl.ds(0, columns)], view, signals.at[number]
        )
        wanted = None
        if mark:
            wanted = info[0] == (1 if mark == 1 else 0)
        depth = out.shape[-2]
        if depth < blocks * real:
            inside = block * real < depth
            wanted = inside if wanted is None else jnp.logical_and(wanted, inside)
        copies.append((copy, wanted))
    for step in ("start", "wait"):
        for copy, wanted in copies:
            if wanted is None:
                getattr(copy, step)()
            else:
                pl.when(wanted)(getattr(copy, step))


def unpack(moves, inputs, outputs, former, blocks, info):
    spec = pl.BlockSpec(memory_space=pl.ANY)
    whole = pl.BlockSpec(memory_space=pltpu.VMEM)
    former = tuple(former or ())
    inputs = tuple(inputs)
    rows = [value.shape[0] for value in inputs]
    return pl.pallas_call(
        functools.partial(unpack_body, moves, rows, blocks, len(former)),
        out_shape=tuple(jax.ShapeDtypeStruct(shape, FULL) for shape in outputs),
        in_specs=[pl.BlockSpec(memory_space=pltpu.SMEM)] + [whole] * len(inputs) + [spec] * len(former),
        out_specs=tuple([spec] * len(outputs)),
        scratch_shapes=[pltpu.VMEM((count, UNIT), FULL) for count in rows]
        + [pltpu.SemaphoreType.DMA((len(moves),))],
        input_output_aliases={1 + len(inputs) + n: n for n in range(len(former))},
        compiler_params=pltpu.CompilerParams(vmem_limit_bytes=ROOM),
        cost_estimate=pl.CostEstimate(flops=0, bytes_accessed=6 * sum(rows) * UNIT, transcendentals=0),
        name="unpack",
    )(info, *inputs, *former)


CORES = [(0, 1), (1, 0)]


def to_other_core(values):
    return lax.ppermute(values, "tensor", CORES)


def to_other_section(values):
    return lax.ppermute(values, "section", CORES)


def to_layer(values, layer):
    return lax.ppermute(values, "section", [(1 - layer, layer)])


def ring_order():
    places = list(range(lax.axis_size("dp")))
    return places[0::2] + places[1::2][::-1]


def ring_place():
    place, count = lax.axis_index("dp"), lax.axis_size("dp")
    return jnp.where(place % 2 == 0, place // 2, count - 1 - place // 2)


def to_next(values, way):
    order = ring_order()
    route = list(zip(order, order[1:] + order[:1]))
    if way == 1:
        route = [(there, here) for here, there in route]
    return lax.ppermute(values, "dp", route)


def after(values, token):
    if token is None:
        return values
    return lax.optimization_barrier((values, token))[0]


class Ring:
    def __init__(self, parts):
        self.parts = parts
        self.count = len(parts[0])
        self.pieces = [[None] * self.count, [None] * self.count]
        self.step = 0
        self.last = 2 * (self.count - 1)
        self.flying = [to_next(parts[way][1], way) for way in range(2)]

    def advance(self, token):
        got = [after(self.flying[0], token), after(self.flying[1], token)]
        turn, count = self.step, self.count
        self.step += 1
        if turn < count - 1:
            got = [got[way] + self.parts[way][(turn + 2) % count] for way in range(2)]
        hop = max(turn - (count - 2), 0)
        if turn >= count - 2:
            for way in range(2):
                self.pieces[way][hop] = got[way]
        if self.step < self.last:
            self.flying = [to_next(got[way], way) for way in range(2)]
        return tuple(got), (hop if turn >= count - 2 else None)


def shards(
    text_stream,
    image_stream,
    region_mask,
    co_text_in,
    co_text_out,
    self_text_in,
    self_text_out,
    image_attn_in,
    image_attn_out,
    text_up,
    text_down,
    image_up,
    image_down,
    text_gain,
    text_shift,
    image_gain,
    image_shift,
):
    front = lax.axis_index("section") == 0
    core = lax.axis_index("tensor")
    blocks = lax.axis_size("dp")
    in_ring = blocks == 8
    place = ring_place() if in_ring else 0 * core
    info = jnp.stack([front.astype(jnp.int32), core.astype(jnp.int32), place.astype(jnp.int32)])
    pairs = text_stream.shape[1]
    half = pairs // 2
    real_t, real_i = text_stream.shape[2], image_stream.shape[2]
    rows_t, rows_i = round_up(real_t, 16), round_up(real_i, 16)
    wide_t, wide_i = text_stream.shape[3], image_stream.shape[3]
    text_size = D_TEXT // HEADS_TEXT
    image_size = D_IMAGE // HEADS_IMAGE

    def flat_rows(values, rows):
        grown = jnp.pad(values, ((0, 0), (0, rows - values.shape[1]), (0, 0)))
        return grown.reshape(values.shape[0] * rows, values.shape[2])

    def by_slot(weight):
        return jnp.transpose(weight, (1, 0, 2))

    own_t, own_i = half * rows_t, half * rows_i
    all_t, all_i = pairs * rows_t, pairs * rows_i
    keep = jnp.pad(region_mask, ((0, 0), (0, rows_i - real_i))).reshape(pairs, 1, rows_i)
    gain_t, shift_t, gain_i, shift_i = text_gain[0], text_shift[0], image_gain[0], image_shift[0]
    cross_in, image_in, single_in = by_slot(co_text_in), by_slot(image_attn_in[0]), by_slot(self_text_in)
    image_out, up_i, down_i = image_attn_out[0], image_up[0], image_down[0]
    up_t, down_t = text_up[0], text_down[0]
    image_out_2, cross_out_2 = to_other_core(image_out), to_other_core(co_text_out)
    up_i_2, down_i_2 = to_other_core(up_i), to_other_core(down_i)
    up_t_2, down_t_2 = to_other_core(up_t), to_other_core(down_t)
    cross = cross_in.shape[2]
    single = single_in.shape[2]
    ff_t, ff_i = up_t.shape[1], up_i.shape[1]
    tail_t = (up_t, down_t, up_t_2, down_t_2)
    tail_i = (up_i, down_i, up_i_2, down_i_2)

    far = (cross_in, image_in)
    xt_own, xt_other, xi_own, xi_other, tp, ip, ct_own, ct_give, ci_own, ci_give = launch(
        functools.partial(cross_forward, pairs, rows_t, rows_i, real_t),
        [shape_of(own_t, wide_t)] * 2
        + [shape_of(own_i, wide_i)] * 2
        + [shape_of(all_t, 3 * cross), shape_of(all_i, 3 * cross)]
        + [shape_of(own_t, cross)] * 2
        + [shape_of(own_i, cross)] * 2,
        (flat_rows(text_stream[0], rows_t), flat_rows(image_stream[0], rows_i), keep),
        far=far,
        scratch=[pltpu.VMEM((all_t, wide_t), LOW), pltpu.VMEM((all_i, wide_i), LOW)] + buffers_for(far),
        flag=info,
        work=6 * cross * (all_t * wide_t + all_i * wide_i),
        name="cross_forward",
    )
    ct_other, ci_other = ct_give, ci_give
    ci_2 = to_other_core(ci_give)
    ct_2 = to_other_core(ct_give)

    def run_first_tail(x, c0, c1, o0, o1, gain, shift, ff, rows, width, hidden, name):
        low_w, low_h = shape_of(rows, width), shape_of(rows, hidden)
        far = (o0, o1) + ff
        return launch(
            first_tail,
            [low_w, low_w, low_h, low_h]
            + [shape_of(rows, hidden, FULL)] * 2
            + [shape_of(rows, width, FULL), shape_of(rows, 128, FULL)] * 2,
            (x, c0, c1, gain, shift),
            far=far,
            scratch=[pltpu.VMEM((rows, width), FULL)] + buffers_for(far),
            flag=info,
            work=4 * rows * width * (o0.shape[0] + 2 * hidden),
            name=name,
        )

    bi, yi, hi0, hi1, si0, si1, ni1, ii1, ni2, ii2 = run_first_tail(
        after(xi_own, (up_t_2, down_t_2, cross_out_2, ct_2)), ci_own, ci_2, image_out, image_out_2, gain_i, shift_i,
        tail_i, own_i, wide_i, ff_i, "tail_i"
    )
    image_in_2, single_in_2, single_out_2 = [
        to_other_core(after(value, bi)) for value in (image_in, single_in, self_text_out)
    ]
    bi_here, bi = bi, to_layer(bi, 1)
    bt, yt, ht0, ht1, st0, st1, nt1, it1, nt2, it2 = run_first_tail(
        after(xt_own, bi_here), ct_own, ct_2, co_text_out, cross_out_2, gain_t, shift_t, tail_t, own_t, wide_t, ff_t, "tail_t"
    )

    def run_self(rows, real, size, width, hidden, x, w0, w1, masked, o0, o1, gain, shift, ff, seed, y, h0, h1, c, name):
        count = half * rows
        inner = w0.shape[2]
        low_w, low_h = shape_of(count, width), shape_of(count, hidden)
        outputs = [low_w, low_w, shape_of(count, cross), shape_of(count, 3 * cross)]
        outputs += [low_w, low_w, low_h, low_h, low_w, low_h] + [shape_of(2, width, FULL)] * 2
        outputs += [shape_of(count, 2 * width + hidden + 4 * cross)]
        scratch = [pltpu.VMEM((count, 3 * inner), LOW)] * 2
        scratch += [pltpu.VMEM((count, hidden), FULL)] * 2
        scratch += [pltpu.VMEM((count, width), FULL), pltpu.VMEM((count, 128), FULL)] * 2
        scratch += [pltpu.VMEM((count, width), FULL)] + [pltpu.VMEM((count, inner), LOW)] * 2
        scratch += [pltpu.VMEM((count, columns), LOW) for columns in (hidden, cross, 3 * cross)]
        weights = (w0, w1, o0, o1) + ff
        return launch(
            functools.partial(self_layer, masked, half, rows, real, size, cross),
            outputs,
            (x, seed, gain, shift, keep),
            far=weights + (y, h0, h1, c),
            scratch=scratch + buffers_for(weights),
            flag=info,
            work=8 * count * width * (4 * inner + 2 * hidden),
            name=name,
        )

    i2 = run_self(
        rows_i, real_i, image_size, wide_i, ff_i, bi, image_in, image_in_2, True, image_out, image_out_2,
        gain_i, shift_i, tail_i, xi_own, yi, hi0, hi1, ci_own, "self_i",
    )
    seed_i = to_layer(i2[1], 0)
    bt = to_layer(bt, 1)
    t2 = run_self(
        rows_t, real_t, text_size, wide_t, ff_t, after(bt, i2[1]), single_in, single_in_2, False,
        self_text_out, single_out_2, gain_t, shift_t, tail_t, xt_own, yt, ht0, ht1, ct_own, "self_t",
    )
    seed_t = to_layer(t2[1], 0)
    (oi, unused, ci_own, pi_own, dai, dfi, dui0, dui1, yi, hi0, dgi, dsi, give_i) = i2
    (ot, unused, ct_own, pt_own, dat, dft, dut0, dut1, yt, ht0, dgt, dst, give_t) = t2
    left_t, left_i = to_other_core(give_t), to_other_core(give_i)

    def run_tail_back(seed, kept, o0, o1, gain, ff, given, rows, width, hidden, name):
        low_w, low_h = shape_of(rows, width), shape_of(rows, hidden)
        outputs = [low_w, low_h, low_w] + [shape_of(2, width, FULL)] * 2
        outputs += [shape_of(rows, width, FULL), shape_of(rows, cross)]
        outputs += [shape_of(rows, 2 * width + hidden + cross)]
        s0, s1, n1, i1, n2, i2 = kept
        u0, d0, u1, d1 = ff
        late = (n2, i2, d0, s0, u0, d1, s1, u1, n1, i1, o0, o1)
        return launch(
            first_tail_back,
            outputs,
            (seed, gain),
            far=late + given,
            scratch=[pltpu.VMEM((rows, hidden), LOW)] + buffers_for(late),
            flag=info,
            work=4 * rows * width * (cross + 2 * hidden),
            name=name,
        )


    def choose(first, second):
        return jnp.where(front, first, second)

    ff_layout = Layout(
        blocks,
        [
            ("down_t", ff_t, wide_t),
            ("up_t", wide_t, ff_t),
            ("up_i", wide_i, ff_i),
            ("down_i", ff_i, wide_i),
        ],
        {"down_t": 1, "up_t": 3, "up_i": 2, "down_i": 1},
    )
    attn_layout = Layout(
        blocks,
        [
            ("in_t", wide_t, 3 * cross),
            ("out_t", cross, wide_t),
            ("in_i", wide_i, 3 * cross),
            ("out_i", cross, wide_i),
            ("small", blocks * 16, UNIT),
        ],
    )
    text_rows = attn_layout.after["out_t"]

    out = run_tail_back(
        seed_i, (si0, si1, ni1, ii1, ni2, ii2), image_out, image_out_2, gain_i, tail_i,
        (dfi, dui0, dui1, dai, dgi, dsi), own_i, wide_i, ff_i, "tail_back_i",
    )
    dfi, dui0, dai, dgi, dsi, dri, dci_own, give_i = out
    right_i = to_other_core(give_i)
    out = run_tail_back(
        after(seed_t, dci_own), (st0, st1, nt1, it1, nt2, it2), co_text_out, cross_out_2, gain_t, tail_t,
        (dft, dut0, dut1, dat, dgt, dst), own_t, wide_t, ff_t, "tail_back_t",
    )
    dft, dut0, dat, dgt, dst, drt, dct_own, give_t = out
    right_t = to_other_core(give_t)
    small = jnp.concatenate([dgt, dst, dgi, dsi], axis=1)
    small = small + to_other_core(small)
    small_rows = round_up(-(-small.size // UNIT), blocks) // blocks
    small = jnp.pad(small.reshape(-1), (0, blocks * small_rows * UNIT - small.size))
    small = small.reshape(blocks, small_rows, UNIT)
    small = jnp.pad(small, ((0, 0), (0, 16 - small_rows), (0, 0))).reshape(blocks * 16, UNIT)
    ff_parts = pack(
        ff_layout,
        {
            "down_t": ((ht0, 0, ff_t), (left_t, wide_t, ff_t), (after(dft, small), 0, wide_t), (right_t, 0, wide_t)),
            "up_t": ((yt, 0, wide_t), (left_t, 0, wide_t), (dut0, 0, ff_t), (right_t, wide_t, ff_t)),
            "up_i": ((yi, 0, wide_i), (left_i, 0, wide_i), (dui0, 0, ff_i), (right_i, wide_i, ff_i)),
            "down_i": ((hi0, 0, ff_i), (left_i, wide_i, ff_i), (dfi, 0, wide_i), (right_i, 0, wide_i)),
        },
        info,
        "pack_ff",
    )
    token = ff_parts[0][1]
    ff = Ring(ff_parts) if in_ring else None
    far = (cross_in, image_in)
    out = launch(
        functools.partial(cross_backward, (wide_t, wide_i), pairs, rows_t, rows_i, real_t),
        [shape_of(own_t, 3 * cross)] * 2
        + [shape_of(own_i, 3 * cross)] * 2
        + [shape_of(own_t, wide_t, FULL)] * 2
        + [shape_of(own_i, wide_i, FULL)] * 2,
        (after(tp, token), ip, dct_own, dci_own, keep),
        far=far + (right_t, right_i, pt_own, left_t, pi_own, left_i),
        scratch=[pltpu.VMEM(v.shape, v.dtype) for v in far]
        + [pltpu.VMEM((own_t, cross), LOW), pltpu.VMEM((own_i, cross), LOW), pltpu.SemaphoreType.DMA((4,))],
        flag=info,
        work=6 * cross * (all_t * wide_t + all_i * wide_i),
        name="cross_backward",
    )
    dtp_own, dtp_other, dip_own, dip_other, dxt_own, dxt_give, dxi_own, dxi_give = out
    token = dtp_own
    if in_ring:
        token, unused = ff.advance(token)

    def columns(part, wide, hidden):
        starts = {"c": wide + hidden, "x": wide + hidden + 4 * cross}
        return starts[part]

    ct_column, xt_column = columns("c", wide_t, ff_t), columns("x", wide_t, ff_t)
    ci_column, xi_column = columns("c", wide_i, ff_i), columns("x", wide_i, ff_i)
    attn_parts = pack(
        attn_layout,
        {
            "in_t": (
                ((xt_own, 0), (bt, 0), wide_t),
                ((xt_other, 0), (left_t, xt_column), wide_t),
                (after(dtp_own, token), 0, 3 * cross),
                (dtp_other, 0, 3 * cross),
            ),
            "out_t": (
                (ct_own, 0, cross),
                ((ct_give, 0), (left_t, ct_column), cross),
                (dat, 0, wide_t),
                (right_t, wide_t + ff_t, wide_t),
            ),
            "in_i": (
                ((xi_own, 0), (bi, 0), wide_i),
                ((xi_other, 0), (left_i, xi_column), wide_i),
                (dip_own, 0, 3 * cross),
                (dip_other, 0, 3 * cross),
            ),
            "out_i": (
                (ci_own, 0, cross),
                ((ci_give, 0), (left_i, ci_column), cross),
                (dai, 0, wide_i),
                (right_i, wide_i + ff_i, wide_i),
            ),
            "small": ((small, 0, UNIT),),
        },
        info,
        "pack_attention",
    )

    def choose(first, second):
        return jnp.where(front, first, second)

    def result(rest, partial, other, output, rows, real, token):
        mine = choose(rest + partial + to_other_core(after(other, token)), output.astype(FULL))
        mine = mine.astype(LOW).reshape(half, rows, -1)[:, :real]
        got = to_other_core(mine)
        return jnp.concatenate(
            [jnp.where(core == 0, mine, got), jnp.where(core == 0, got, mine)], axis=0
        )[None]

    main_shapes = [
        (ff_t, wide_t),
        (wide_t, ff_t),
        (wide_i, ff_i),
        (ff_i, wide_i),
        (3, wide_i, cross),
        (cross, wide_i),
        (blocks * 16, UNIT),
    ]
    text_shapes = [(3, wide_t, cross), (cross, wide_t), (3, wide_t, single), (self_text_out.shape[0], wide_t)]
    main_moves, text_moves = [], []

    def move(target, source, way, row, real, unit, output, shape, mark=0):
        slot, column, columns = None, unit * UNIT, UNIT
        if len(shape) == 3:
            slot, column = column // cross, column % cross
            columns = min(UNIT, shape[2] - column)
        if columns > 0:
            target.append((source, way, row, real, output, slot, column, columns, mark))

    for index, unit, way, row, real in ff_layout.units:
        move(main_moves, way, way, row, real, unit, index, main_shapes[index])
    for index, unit, way, row, real in attn_layout.units:
        if index >= 2:
            move(main_moves, 2 + way, way, row, real, unit, index + 2, main_shapes[index + 2])
        else:
            for mark in (1, 2):
                move(text_moves, way + 2 * (mark - 1), way, row, real, unit, index, text_shapes[index], mark)
                move(text_moves, way + 4 - 2 * mark, way, row, real, unit, index + 2, text_shapes[index + 2], mark)

    main, text = None, None

    def shifted(moves, hop, source_shift, row_shift):
        result = []
        for source, way, row, *rest in moves:
            result.append((source_shift(source), way, hop, row + row_shift(source), *rest))
        return result

    def spread_main(hops, ff, attn, main):
        inputs, moves = [], []
        for number, hop in enumerate(hops):
            inputs += [ff[0][hop], ff[1][hop], attn[0][hop], attn[1][hop]]
            moves += shifted(main_moves, hop, lambda source: source + 4 * number, lambda source: 0)
        return unpack(moves, inputs, main_shapes, main, blocks, info)

    def spread_text(hops, attn, crossed, text):
        inputs, moves, both = [], [], text_rows[0] + text_rows[1]
        for hop in hops:
            inputs += [attn[0][hop], attn[1][hop]]
        places = []
        for array in crossed:
            places += [(len(inputs), row) for row in range(0, array.shape[0], both)]
            inputs.append(array)
        for number, hop in enumerate(hops):
            moves += shifted(
                text_moves,
                hop,
                lambda source: source + 2 * number if source < 2 else places[number][0],
                lambda source: 0 if source < 2 else places[number][1] + (source - 2) * text_rows[0],
            )
        return unpack(moves, inputs, text_shapes, text, blocks, info)

    def cross_over(attn, hops):
        return to_other_section(
            jnp.concatenate([attn[way][hop][: text_rows[way]] for hop in hops for way in range(2)], axis=0)
        )

    if in_ring:
        attn = Ring(attn_parts)
        token = attn_parts[0][1]
        results = (
            result(drt, dxt_own, dxt_give, ot, rows_t, real_t, token),
            result(dri, dxi_own, dxi_give, oi, rows_i, real_i, token),
        )
        token = (token, results)
        groups = [(0, 1), (2, 3), (4, 5), (6,), (7,)]
        crossed = [None] * len(groups)
        while attn.step < attn.last:
            if ff.step < ff.last:
                token, unused = ff.advance(token)
            token, hop = attn.advance(token)
            if hop is None:
                continue
            if hop == 2:
                first = after(crossed[0], token)
                relay = [to_next(first[: text_rows[0]], 1), to_next(first[text_rows[0] : sum(text_rows)], 0)]
            if hop == 4:
                crossed[-1] = jnp.concatenate([after(value, token) for value in relay], axis=0)
                token = (token, crossed[-1])
            for number, group in enumerate(groups):
                if hop == group[-1]:
                    if number < len(groups) - 1:
                        crossed[number] = cross_over(attn.pieces, group)
                    main = spread_main(group, ff.pieces, attn.pieces, main)
                    token = (token, main)
                elif number and hop == group[0] and len(group) > 1:
                    text = spread_text(groups[number - 1], attn.pieces, [crossed[number - 1]], text)
                    token = (token, text)
        text = spread_text(groups[-3], attn.pieces, crossed[-3:-2], text)
        text = spread_text((6, 7), attn.pieces, crossed[-2:], text)
    else:
        results = (
            result(drt, dxt_own, dxt_give, ot, rows_t, real_t, token),
            result(dri, dxi_own, dxi_give, oi, rows_i, real_i, token),
        )
        ff, attn = lax.psum((ff_parts, attn_parts), "dp")
        for hop in range(0, blocks, 2):
            main = spread_main((hop, hop + 1), ff, attn, main)
            text = spread_text((hop, hop + 1), attn, [cross_over(attn, (hop, hop + 1))], text)
    down_t_grad, up_t_grad, up_i_grad, down_i_grad, in_i_grad, out_i_grad, small = main
    co_in_grad, co_out_grad, self_in_grad, self_out_grad = text
    small = small.reshape(blocks, 16, UNIT)[:, :small_rows].reshape(-1)[: 4 * (wide_t + wide_i)]
    small = small.reshape(2, 2 * (wide_t + wide_i))
    small = jnp.split(small, [wide_t, 2 * wide_t, 2 * wide_t + wide_i], axis=1)

    return (
        results[0],
        results[1],
        by_slot(co_in_grad),
        co_out_grad,
        by_slot(self_in_grad),
        self_out_grad,
        by_slot(in_i_grad)[None],
        out_i_grad[None],
        up_t_grad[None],
        down_t_grad[None],
        up_i_grad[None],
        down_i_grad[None],
        small[0][None],
        small[1][None],
        small[2][None],
        small[3][None],
    )


def solution(mesh):
    in_specs = (
        P("section", "dp", None, None),
        P("section", "dp", None, None),
        P("dp", None),
        P(None, None, "tensor"),
        P("tensor", None),
        P(None, None, "tensor"),
        P("tensor", None),
        P("section", None, None, "tensor"),
        P("section", "tensor", None),
        P("section", None, "tensor"),
        P("section", "tensor", None),
        P("section", None, "tensor"),
        P("section", "tensor", None),
        P("section", None, None),
        P("section", None, None),
        P("section", None, None),
        P("section", None, None),
    )
    out_specs = (
        P("section", "dp", None, None),
        P("section", "dp", None, None),
        P(None, None, "tensor"),
        P("tensor", None),
        P(None, None, "tensor"),
        P("tensor", None),
        P("section", None, None, "tensor"),
        P("section", "tensor", None),
        P("section", None, "tensor"),
        P("section", "tensor", None),
        P("section", None, "tensor"),
        P("section", "tensor", None),
        P("section", None, None),
        P("section", None, None),
        P("section", None, None),
        P("section", None, None),
    )
    return jax.shard_map(shards, mesh=mesh, in_specs=in_specs, out_specs=out_specs, check_vma=False)
```

```python
import functools
import math

import jax
import jax.numpy as jnp
from jax import lax
from jax.experimental import pallas as pl
from jax.experimental.pallas import tpu as pltpu
from jax.sharding import PartitionSpec as P

D_TEXT = 768
HEADS_TEXT = 12
D_IMAGE = 1024
HEADS_IMAGE = 8
D_CO = 1024
HEADS_CO = 8

LOW = jnp.bfloat16
FULL = jnp.float32
TILE = 512
UNIT = 256
ROOM = 56 * 1024 * 1024


def times(left, right):
    return jnp.dot(left, right, preferred_element_type=FULL)


def times_back(left, right):
    return lax.dot_general(left, right, (((1,), (1,)), ((), ())), preferred_element_type=FULL)


def back_times(left, right):
    return lax.dot_general(left, right, (((0,), (0,)), ((), ())), preferred_element_type=FULL)


def norm_rows(rows):
    centre = rows - jnp.mean(rows, axis=-1, keepdims=True)
    spread = jnp.mean(centre * centre, axis=-1, keepdims=True)
    inverse = lax.rsqrt(spread + 1e-05)
    return centre * inverse, inverse


def norm_back(unit, inverse, gain, grad):
    scaled = grad * gain
    first = jnp.mean(scaled, axis=-1, keepdims=True)
    second = jnp.mean(scaled * unit, axis=-1, keepdims=True)
    dgain = jnp.sum(grad * unit, axis=0, keepdims=True)
    dshift = jnp.sum(grad, axis=0, keepdims=True)
    return inverse * (scaled - first - unit * second), dgain, dshift


def gelu_both(inputs):
    rate = 0.7978845608028654
    square = inputs * inputs
    bent = jnp.tanh(rate * inputs * (1.0 + 0.044715 * square))
    half = 0.5 * (1.0 + bent)
    slope = half + 0.5 * inputs * (1.0 - bent * bent) * rate * (1.0 + 0.134145 * square)
    return inputs * half, slope


def heads_of(query, size):
    if size == query.shape[1]:
        return [query]
    lower = lax.broadcasted_iota(jnp.int32, (1, query.shape[1]), 1) < size
    low = lower.astype(FULL).astype(LOW)
    return [query * low, query * (1 - low)]


def merged(parts, size):
    if len(parts) == 1:
        return parts[0]
    return jnp.where(lax.broadcasted_iota(jnp.int32, parts[0].shape, 1) < size, parts[0], parts[1])


def softmax_all(pairs, alloweds, size):
    scores = [times_back(query, keys) for query, keys in pairs]
    scores = [
        jnp.where(allowed, score * (1.0 / math.sqrt(size)), -1000000000.0)
        for score, allowed in zip(scores, alloweds)
    ]
    tops = [jnp.max(score, axis=-1, keepdims=True) for score in scores]
    raised = [jnp.exp(score - top) for score, top in zip(scores, tops)]
    shares = [1.0 / jnp.sum(value, axis=-1, keepdims=True) for value in raised]
    return [value * share for value, share in zip(raised, shares)]


def attend_all(units, size):
    singles = [(q, k, v, a) for query, k, v, a in units for q in heads_of(query, size)]
    weights = softmax_all([one[:2] for one in singles], [one[3] for one in singles], size)
    contexts = [times(w.astype(LOW), one[2]) for w, one in zip(weights, singles)]
    heads = len(singles) // len(units)
    return [merged(contexts[n * heads : (n + 1) * heads], size).astype(LOW) for n in range(len(units))]


def attend_back_all(units, size):
    scaling = 1.0 / math.sqrt(size)
    singles = [
        (q, k, v, a, d, query, dcontext)
        for query, k, v, a, dcontext in units
        for q, d in zip(heads_of(query, size), heads_of(dcontext, size))
    ]
    weights = softmax_all([one[:2] for one in singles], [one[3] for one in singles], size)
    dweights = [times_back(one[4], one[2]) for one in singles]
    dvalues = [back_times(w.astype(LOW), one[6]) for w, one in zip(weights, singles)]
    sums = [jnp.sum(dw * w, axis=-1, keepdims=True) for dw, w in zip(dweights, weights)]
    dscores = [(w * (dw - s)).astype(LOW) for w, dw, s in zip(weights, dweights, sums)]
    dqueries = [times(ds, one[1]) * scaling for ds, one in zip(dscores, singles)]
    dkeys = [back_times(ds, one[5]) * scaling for ds, one in zip(dscores, singles)]
    heads = len(singles) // len(units)
    return [
        [merged(grads[n * heads : (n + 1) * heads], size).astype(LOW) for grads in (dqueries, dkeys, dvalues)]
        for n in range(len(units))
    ]


def wide(column):
    return jnp.broadcast_to(column, (column.shape[0], 128))


class Late:
    def __init__(self, source, target, signal):
        self.target = target
        self.copy = pltpu.make_async_copy(source, target, signal)
        self.copy.start()
        self.here = False

    def get(self):
        if not self.here:
            self.copy.wait()
            self.here = True
        return self.target


class Here:
    def __init__(self, target):
        self.target = target

    def get(self):
        return self.target


def fetch(sources, targets, signals):
    return [Late(s, t, signals.at[n]) for n, (s, t) in enumerate(zip(sources, targets))]


def pass_through(sources, targets, signals):
    copies = [
        pltpu.make_async_copy(s, t, signals.at[n]) for n, (s, t) in enumerate(zip(sources, targets))
    ]
    for copy in copies:
        copy.start()
    for copy in copies:
        copy.wait()


def tail_forward(residual, contexts, out_w, gain, shift, up_w, down_w, kept, mixed, leave=None):
    normed_ref, hidden, slopes, unit1, inv1, unit2, inv2 = kept
    branch = times(contexts[0], out_w[0].get()[...]) + times(contexts[1], out_w[1].get()[...])
    unit, inverse = norm_rows(residual.astype(FULL) + branch)
    unit1[...] = unit
    inv1[...] = wide(inverse)
    normed = unit * gain[0:1, :] + shift[0:1, :]
    normed_ref[...] = normed.astype(LOW)
    mixed[...] = normed
    if leave is not None:
        leave.go(normed_ref, unit1, inv1)
    for half in range(2):
        up, down = up_w[half].get(), down_w[half].get()
        for start in range(0, up.shape[1], TILE):
            span = pl.ds(start, TILE)
            value, slope = gelu_both(times(normed_ref[...], up[:, span]))
            hidden[half][:, span] = value.astype(LOW)
            slopes[half][:, span] = slope
            mixed[...] += times(hidden[half][:, span], down[span, :])
        if leave is not None:
            leave.go(hidden[half], slopes[half])
    unit, inverse = norm_rows(mixed[...])
    unit2[...] = unit
    inv2[...] = wide(inverse)
    return unit * gain[1:2, :] + shift[1:2, :]


def tail_backward(seed, kept, out_w, gain, up_w, down_w, grads, total, leave=None):
    slopes, unit1, inv1, unit2, inv2 = kept
    df, du, da, dgain, dshift = grads
    dsecond, dgain1, dshift1 = norm_back(
        unit2.get()[...], inv2.get()[:, 0:1], gain[1:2, :], seed
    )
    total[...] = dsecond
    df[...] = dsecond.astype(LOW)
    for half in range(2):
        up, down, slope = up_w[half].get(), down_w[half].get(), slopes[half].get()
        for start in range(0, up.shape[1], TILE):
            span = pl.ds(start, TILE)
            dhidden = times_back(df[...], down[span, :])
            du[half][:, span] = (dhidden * slope[:, span]).astype(LOW)
            total[...] += times_back(du[half][:, span], up[:, span])
    dfirst, dgain0, dshift0 = norm_back(
        unit1.get()[...], inv1.get()[:, 0:1], gain[0:1, :], total[...]
    )
    dgain[...] = jnp.concatenate([dgain0, dgain1], axis=0)
    dshift[...] = jnp.concatenate([dshift0, dshift1], axis=0)
    total[...] = dfirst
    da[...] = dfirst.astype(LOW)
    if leave is not None:
        leave.go(df, du[0], da, total)
    return [times_back(da[...], w.get()[...]).astype(LOW) for w in out_w]


def shape_of(rows, columns, kind=LOW):
    return jax.ShapeDtypeStruct((rows, columns), kind)


class Leave:
    def __init__(self, buffers, targets, signals):
        self.buffers, self.targets, self.signals = buffers, targets, signals
        self.begun = {}

    def go(self, *buffers):
        for buffer in buffers:
            number = [one is buffer for one in self.buffers].index(True)
            copy = pltpu.make_async_copy(buffer, self.targets[number], self.signals.at[number])
            copy.start()
            self.begun[number] = copy

    def finish(self):
        self.go(*[one for number, one in enumerate(self.buffers) if number not in self.begun])
        for copy in self.begun.values():
            copy.wait()
        self.begun = {}


def launch(body, outputs, args, far=(), scratch=(), flag=None, work=0, name=None):
    whole, anywhere = pl.BlockSpec(memory_space=pltpu.VMEM), pl.BlockSpec(memory_space=pl.ANY)
    moved = sum(
        math.prod(v.shape) * v.dtype.itemsize for v in tuple(args) + tuple(far) + tuple(outputs)
    )
    total, results = len(args) + len(far), len(outputs)

    def whole_body(info, *refs):
        targets, refs = refs[total : total + results], refs[:total] + refs[total + results :]
        outs, signals = refs[total : total + results], refs[total + results]
        body(Leave(outs, targets, signals), info, *refs[:total], *outs, *refs[total + results + 1 :])

    own = [pltpu.VMEM(v.shape, v.dtype) for v in outputs] + [pltpu.SemaphoreType.DMA((results,))]
    return pl.pallas_call(
        whole_body,
        out_shape=tuple(outputs),
        in_specs=[pl.BlockSpec(memory_space=pltpu.SMEM)] + [whole] * len(args) + [anywhere] * len(far),
        out_specs=tuple([anywhere] * results),
        scratch_shapes=own + list(scratch),
        compiler_params=pltpu.CompilerParams(vmem_limit_bytes=ROOM),
        cost_estimate=pl.CostEstimate(flops=work, bytes_accessed=moved, transcendentals=0),
        name=name,
    )(flag, *args, *far)


def buffers_for(far):
    return [pltpu.VMEM(v.shape, v.dtype) for v in far] + [pltpu.SemaphoreType.DMA((len(far),))]


def rows_at(pair, rows):
    return pl.ds(pl.multiple_of(pair * rows, 16), rows)


def slab(index):
    return pl.ds(index * 128, 128)


def cross_forward(
    pairs, rows_t, rows_i, real_t, leave, info, x_t, x_i, keep, far_t, far_i,
    xt_own, xt_other, xi_own, xi_other, tp, ip, ct_own, ct_other, ci_own, ci_other, xt, xi, wt, wi, signals,
):
    half = pairs // 2
    for place in range(pairs):
        pair = lax.rem(place + half * info[1], pairs)
        text, image = x_t[rows_at(pair, rows_t), :], x_i[rows_at(pair, rows_i), :]
        xt[place * rows_t : (place + 1) * rows_t, :] = text
        xi[place * rows_i : (place + 1) * rows_i, :] = image
        inside = place % half
        (xt_own, xt_other)[place // half][inside * rows_t : (inside + 1) * rows_t, :] = text
        (xi_own, xi_other)[place // half][inside * rows_i : (inside + 1) * rows_i, :] = image

    @pl.when(info[0] == 0)
    def idle():
        leave.finish()

    @pl.when(info[0] == 1)
    def work():
        width = ct_own.shape[1]
        weights = fetch((far_t, far_i), (wt, wi), signals)
        leave.go(xt_own, xt_other, xi_own, xi_other)
        for late, x, p in ((weights[0], xt, tp), (weights[1], xi, ip)):
            for slot in range(3):
                p[:, pl.ds(slot * width, width)] = times(x[...], late.get()[slot]).astype(LOW)
            leave.go(p)
        text_keys = lax.broadcasted_iota(jnp.int32, (1, rows_t), 1) < real_t
        slabs = width // 128

        def each(pair, carry):
            at_t, at_i = rows_at(pair, rows_t), rows_at(pair, rows_i)
            for group, ct, ci in ((0, ct_own, ci_own), (half, ct_other, ci_other)):
                from_t, from_i = rows_at(pair + group, rows_t), rows_at(pair + group, rows_i)
                kept = keep[lax.rem(pair + group + half * info[1], pairs)] > 0
                texts, images = [], []
                for n in range(slabs):
                    first, second, third = slab(n), slab(slabs + n), slab(2 * slabs + n)
                    texts.append((tp[from_t, first], ip[from_i, second], ip[from_i, third], kept))
                    images.append((ip[from_i, first], tp[from_t, second], tp[from_t, third], text_keys))
                results = zip(attend_all(texts, 128), attend_all(images, 128))
                for n, (text, image) in enumerate(results):
                    ct[at_t, slab(n)] = text
                    ci[at_i, slab(n)] = image
            return carry

        lax.fori_loop(0, half, each, 0, unroll=True)
        leave.finish()


def first_tail(
    leave, info, x, c0, c1, gain, shift, *refs
):
    far, refs = refs[:6], refs[6:]
    out, y, h0, h1, s0, s1, n1, i1, n2, i2, mixed = refs[:11]
    near, signals = refs[11:17], refs[17]

    @pl.when(info[0] == 1)
    def work():
        o0, o1, u0, d0, u1, d1 = fetch(far, near, signals)
        kept = (y, (h0, h1), (s0, s1), n1, i1, n2, i2)
        out[...] = tail_forward(
            x[...], (c0[...], c1[...]), (o0, o1), gain, shift, (u0, u1), (d0, d1), kept, mixed, leave
        ).astype(LOW)
        leave.finish()


def self_layer(
    masked, half, rows, real, size, stride, leave, info, x, seed, gain, shift, keep, *refs
):
    far, refs = refs[:12], refs[12:]
    (out, dx, c0, p0, da, df, du0, du1, y, h0, dgain, dshift, give) = refs[:13]
    (q0, q1, s0, s1, n1, i1, n2, i2, mixed, dc0, dc1, h1, c1, p1) = refs[13:27]
    near, signals = refs[27:35], refs[35]
    width = q0.shape[1] // 3
    wide_x, wide_h, wide_c = x.shape[1], h1.shape[1], c1.shape[1]
    spans = []
    for columns in (wide_x, wide_h, wide_c, p1.shape[1], wide_x):
        spans.append(pl.ds(sum(span.size for span in spans), columns))

    @pl.when(info[0] == 1)
    def pass_on():
        targets = (y, h0, c0, give.at[:, spans[0]], give.at[:, spans[1]])
        pass_through((far[8], far[9], far[11], far[8], far[10]), targets, signals)
        leave.go(y, h0, c0, give)
        for copy in leave.begun.values():
            copy.wait()
        leave.begun = {}

    @pl.when(info[0] == 0)
    def work():
        w0, w1, o0, o1, u0, d0, u1, d1 = fetch(far[:8], near, signals)
        slabs = width // 128
        if c0.shape[1] != width:
            rest = pl.ds(width, c0.shape[1] - width)
            c0[:, rest] = jnp.zeros((c0.shape[0], c0.shape[1] - width), LOW)
            c1[:, rest] = jnp.zeros((c0.shape[0], c0.shape[1] - width), LOW)
            for slot in range(3):
                rest = pl.ds(slot * stride + width, stride - width)
                p0[:, rest] = jnp.zeros((p0.shape[0], stride - width), LOW)
                p1[:, rest] = jnp.zeros((p0.shape[0], stride - width), LOW)
        for w, q in ((w0, q0), (w1, q1)):
            for slot in range(3):
                q[:, pl.ds(slot * width, width)] = times(x[...], w.get()[slot]).astype(LOW)

        def allowed(pair):
            if not masked:
                return lax.broadcasted_iota(jnp.int32, (1, rows), 1) < real
            return keep[pair + half * info[1]] > 0

        def forward(pair, carry):
            at = rows_at(pair, rows)
            kept = allowed(pair)
            units = [
                (q[at, slab(n)], q[at, slab(slabs + n)], q[at, slab(2 * slabs + n)], kept)
                for q in (q0, q1)
                for n in range(slabs)
            ]
            results = attend_all(units, size)
            for n, value in enumerate(results):
                (c0, c1)[n // slabs][at, slab(n % slabs)] = value
            return carry

        lax.fori_loop(0, half, forward, 0, unroll=True)
        leave.go(c0)
        used = pl.ds(0, width)
        kept = (y, (h0, h1), (s0, s1), n1, i1, n2, i2)
        out[...] = tail_forward(
            x[...], (c0[:, used], c1[:, used]), (o0, o1), gain, shift, (u0, u1), (d0, d1), kept, mixed
        ).astype(LOW)
        leave.go(out, y, h0)
        held = ((Here(s0), Here(s1)), Here(n1), Here(i1), Here(n2), Here(i2))
        dcs = tail_backward(
            seed[...].astype(FULL),
            held,
            (o0, o1),
            gain,
            (u0, u1),
            (d0, d1),
            (df, (du0, du1), da, dgain, dshift),
            mixed,
        )
        leave.go(da, df, du0, du1, dgain, dshift)
        dc0[...] = dcs[0]
        dc1[...] = dcs[1]

        def backward(pair, carry):
            at = rows_at(pair, rows)
            kept = allowed(pair)
            units = [
                (q[at, slab(n)], q[at, slab(slabs + n)], q[at, slab(2 * slabs + n)], kept, dc[at, slab(n)])
                for q, dc in ((q0, dc0), (q1, dc1))
                for n in range(slabs)
            ]
            results = attend_back_all(units, size)
            for n, grads in enumerate(results):
                for slot in range(3):
                    column = slot * stride + (n % slabs) * 128
                    (p0, p1)[n // slabs][at, pl.ds(column, 128)] = grads[slot]
            return carry

        lax.fori_loop(0, half, backward, 0, unroll=True)
        for span, value in zip(spans, (y, h1, c1, p1, x)):
            give[:, span] = value[...]
        leave.go(p0, give)
        for w, p in ((w0, p0), (w1, p1)):
            for slot in range(3):
                mixed[...] += times_back(p[:, pl.ds(slot * stride, width)], w.get()[slot])
        dx[...] = mixed[...].astype(LOW)
        leave.finish()


def first_tail_back(leave, info, seed, gain, *refs):
    far, refs = refs[:18], refs[18:]
    df, du0, da, dgain, dshift, dres, dc0, give = refs[:8]
    du1, near, signals = refs[8], refs[9:21], refs[21]
    spans = []
    for columns in (df.shape[1], du1.shape[1], da.shape[1], dc0.shape[1]):
        spans.append(pl.ds(sum(span.size for span in spans), columns))

    @pl.when(info[0] == 0)
    def pass_on():
        df_in, du0_in, du1_in, da_in, dgain_in, dshift_in = far[12:]
        pass_through(
            (df_in, du0_in, da_in, dgain_in, dshift_in, df_in, du1_in, da_in),
            (df, du0, da, dgain, dshift) + tuple(give.at[:, span] for span in spans[:3]),
            signals,
        )
        leave.finish()

    @pl.when(info[0] == 1)
    def work():
        n2, i2, d0, s0, u0, d1, s1, u1, n1, i1, o0, o1 = fetch(far[:12], near, signals)
        dcs = tail_backward(
            seed[...].astype(FULL),
            ((s0, s1), n1, i1, n2, i2),
            (o0, o1),
            gain,
            (u0, u1),
            (d0, d1),
            (df, (du0, du1), da, dgain, dshift),
            dres,
            leave,
        )
        dc0[...] = dcs[0]
        for span, value in zip(spans, (df[...], du1[...], da[...], dcs[1])):
            give[:, span] = value
        leave.finish()


def cross_backward(
    wides, pairs, rows_t, rows_i, real_t, leave, info,
    tp, ip, dct_own, dci_own, keep, *refs
):
    far, refs = refs[:8], refs[8:]
    dtp_own, dtp_other, dip_own, dip_other, dxt_own, dxt_other, dxi_own, dxi_other = refs[:8]
    wt, wi, dct_other, dci_other, signals = refs[8:]
    width = dct_own.shape[1]
    slabs = width // 128
    half = pairs // 2

    @pl.when(info[0] == 0)
    def pass_on():
        sources = []
        for mine, got in ((far[4], far[5]), (far[6], far[7])):
            start = got.shape[1] - wides[len(sources) // 2] - mine.shape[1]
            sources += [mine, got.at[:, pl.ds(start, mine.shape[1])]]
        pass_through(sources, (dtp_own, dtp_other, dip_own, dip_other), signals)
        leave.finish()

    @pl.when(info[0] == 1)
    def work():
        got = [far[n].at[:, pl.ds(far[n].shape[1] - width, width)] for n in (2, 3)]
        weights = fetch(
            (got[0], got[1], far[0], far[1]), (dct_other, dci_other, wt, wi), signals
        )
        weights[0].get()
        weights[1].get()
        weights = weights[2:]
        text_keys = lax.broadcasted_iota(jnp.int32, (1, rows_t), 1) < real_t

        def each(pair, carry):
            at_t, at_i = rows_at(pair, rows_t), rows_at(pair, rows_i)
            for group, dct, dci, dtp, dip in (
                (0, dct_own, dci_own, dtp_own, dip_own),
                (half, dct_other, dci_other, dtp_other, dip_other),
            ):
                from_t, from_i = rows_at(pair + group, rows_t), rows_at(pair + group, rows_i)
                kept = keep[lax.rem(pair + group + half * info[1], pairs)] > 0
                texts, images = [], []
                for n in range(slabs):
                    first, second, third = slab(n), slab(slabs + n), slab(2 * slabs + n)
                    texts.append((tp[from_t, first], ip[from_i, second], ip[from_i, third], kept, dct[at_t, first]))
                    images.append((ip[from_i, first], tp[from_t, second], tp[from_t, third], text_keys, dci[at_i, first]))
                results = zip(attend_back_all(texts, 128), attend_back_all(images, 128))
                for n, (text, image) in enumerate(results):
                    first, second, third = slab(n), slab(slabs + n), slab(2 * slabs + n)
                    dtp[at_t, first], dip[at_i, second], dip[at_i, third] = text
                    dip[at_i, first], dtp[at_t, second], dtp[at_t, third] = image
            return carry

        lax.fori_loop(0, half, each, 0, unroll=True)
        leave.go(dtp_own, dtp_other, dip_own, dip_other)
        for late, triples in (
            (weights[0], ((dtp_own, dxt_own), (dtp_other, dxt_other))),
            (weights[1], ((dip_own, dxi_own), (dip_other, dxi_other))),
        ):
            for dp, dx in triples:
                total = times_back(dp[:, pl.ds(0, width)], late.get()[0])
                for slot in range(1, 3):
                    total += times_back(dp[:, pl.ds(slot * width, width)], late.get()[slot])
                dx[...] = total
                leave.go(dx)
        leave.finish()


def round_up(value, step):
    return -(-value // step) * step


class Layout:
    def __init__(self, blocks, weights, firsts=None):
        self.blocks, self.weights = blocks, weights
        self.sizes = [0, 0]
        self.units = []
        self.after = {}
        for index, (name, depth, width) in enumerate(weights):
            real = depth // blocks
            for unit in range(width // UNIT):
                way = 0 if self.sizes[0] <= self.sizes[1] else 1
                if firsts:
                    way = 0 if unit < firsts[name] else 1
                self.units.append((index, unit, way, self.sizes[way], real))
                self.sizes[way] += round_up(real, 16)
            self.after[name] = list(self.sizes)


def pack_body(layout, chosen, kinds, later, info, *refs):
    blocks, weights = layout.blocks, layout.weights
    place = info[2]
    arrays = 1 + max(max(k[0], k[2] or 0) for k in kinds)
    sources, refs = refs[:arrays], refs[arrays + later :]
    targets, refs = refs[: 2 * blocks], refs[2 * blocks :]
    buffers, refs = refs[: len(kinds)], refs[len(kinds) :]
    outs, (total, signals, out_signals) = refs[: 2 * blocks], refs[2 * blocks :]
    waits = []
    for number, (first, column, second, other) in enumerate(kinds):
        buffer = buffers[number]

        def copy(source, start):
            view = sources[source].at[:, pl.ds(start, buffer.shape[1])]
            return pltpu.make_async_copy(view, buffer, signals.at[number])

        if second is None:
            copy(first, column).start()
        else:
            pl.when(info[0] == 1)(copy(first, column).start)
            pl.when(info[0] == 0)(copy(second, other).start)
        waits.append(copy(first, column))
    position, copies = 0, []
    for index, (name, depth, width) in enumerate(weights):
        if name not in chosen:
            continue
        mine = buffers[position : position + chosen[name]]
        for wait in waits[position : position + chosen[name]]:
            wait.wait()
        position += chosen[name]
        span = TILE if width % TILE == 0 else UNIT
        units = [unit for unit in layout.units if unit[0] == index]
        for column in range(0, width, span):
            area = pl.ds(column, span)
            if chosen[name] == 1:
                total[0:depth, 0:span] = mine[0][:, area]
            else:
                x0, x1, y0, y1 = mine
                total[0:depth, 0:span] = back_times(x0[...], y0[:, area]) + back_times(
                    x1[...], y1[:, area]
                )
            for unused, unit, way, row, real in units:
                inside = unit * UNIT - column
                if not 0 <= inside < span:
                    continue
                rows = round_up(real, 16)
                for hop in range(blocks):
                    block = lax.rem(place + (blocks - hop if way == 0 else hop), blocks)
                    source = pl.ds(pl.multiple_of(block * real, 8), rows)
                    outs[way * blocks + hop][row : row + rows, :] = total[
                        source, inside : inside + UNIT
                    ].astype(LOW)
        for way in range(2):
            rows = [(unit[3], unit[3] + round_up(unit[4], 16)) for unit in units if unit[2] == way]
            if not rows:
                continue
            part = pl.ds(rows[0][0], rows[-1][1] - rows[0][0])
            for hop in range(blocks):
                number = way * blocks + hop
                out = pltpu.make_async_copy(
                    outs[number].at[part], targets[number].at[part], out_signals.at[len(copies)]
                )
                out.start()
                copies.append(out)
    for out in copies:
        out.wait()


def pack(layout, factors, info, name, former=None):
    blocks = layout.blocks
    outputs = [shape_of(layout.sizes[way], UNIT) for way in range(2) for hop in range(blocks)]
    deepest = max(weight[1] for weight in layout.weights) + 32
    arrays, kinds, buffers, work = [], [], [], 0

    def number_of(array):
        for number, one in enumerate(arrays):
            if one is array:
                return number
        arrays.append(array)
        return len(arrays) - 1

    for weight in layout.weights:
        for first, second, columns in factors.get(weight[0], ()):
            if isinstance(first, tuple):
                kind = (number_of(first[0]), first[1], number_of(second[0]), second[1])
                array = first[0]
            else:
                kind = (number_of(first), second, None, None)
                array = first
            kinds.append(kind)
            buffers.append(pltpu.VMEM((array.shape[0], columns), array.dtype))
        if weight[0] in factors:
            work += 4 * factors[weight[0]][0][0].shape[0] * weight[1] * weight[2] if len(factors[weight[0]]) > 1 and not isinstance(factors[weight[0]][0][0], tuple) else 800 * weight[1] * weight[2]
    chosen = {name: len(value) for name, value in factors.items()}
    former = tuple(former[0]) + tuple(former[1]) if former else ()
    anywhere = pl.BlockSpec(memory_space=pl.ANY)
    moved = sum(math.prod(v.shape) * 2 for v in outputs) * 2
    outs = pl.pallas_call(
        functools.partial(pack_body, layout, chosen, kinds, len(former)),
        out_shape=tuple(outputs),
        in_specs=[pl.BlockSpec(memory_space=pltpu.SMEM)] + [anywhere] * (len(arrays) + len(former)),
        out_specs=tuple([anywhere] * len(outputs)),
        scratch_shapes=buffers
        + [pltpu.VMEM(v.shape, v.dtype) for v in outputs]
        + [
            pltpu.VMEM((deepest, TILE), FULL),
            pltpu.SemaphoreType.DMA((len(buffers),)),
            pltpu.SemaphoreType.DMA((2 * blocks * len(chosen),)),
        ],
        input_output_aliases={1 + len(arrays) + n: n for n in range(len(former))},
        compiler_params=pltpu.CompilerParams(vmem_limit_bytes=ROOM),
        cost_estimate=pl.CostEstimate(flops=work, bytes_accessed=moved, transcendentals=0),
        name=name,
    )(info, *arrays, *former)
    return [list(outs[:blocks]), list(outs[blocks:])]


def unpack_body(moves, shapes, blocks, later, info, *refs):
    sources = len(shapes)
    inputs, refs = refs[:sources], refs[sources:]
    if later:
        refs = refs[later:]
    count = len(refs) - sources - 1
    outs, wide_refs, signals = refs[:count], refs[count : count + sources], refs[-1]
    place = info[2]
    copies = []
    for source, wide_ref in zip(inputs, wide_refs):
        wide_ref[...] = source[...].astype(FULL)
    for number, (source, way, hop, row, real, target, slot, column, columns, mark) in enumerate(moves):
        block = lax.rem(place + (blocks - hop if way == 0 else hop), blocks)
        rows = pl.ds(pl.multiple_of(block * real, 8), real)
        area = pl.ds(column, columns)
        out = outs[target]
        view = out.at[rows, area] if slot is None else out.at[slot, rows, area]
        copy = pltpu.make_async_copy(
            wide_refs[source].at[pl.ds(row, real), pl.ds(0, columns)], view, signals.at[number]
        )
        wanted = None
        if mark:
            wanted = info[0] == (1 if mark == 1 else 0)
        depth = out.shape[-2]
        if depth < blocks * real:
            inside = block * real < depth
            wanted = inside if wanted is None else jnp.logical_and(wanted, inside)
        copies.append((copy, wanted))
    for step in ("start", "wait"):
        for copy, wanted in copies:
            if wanted is None:
                getattr(copy, step)()
            else:
                pl.when(wanted)(getattr(copy, step))


def unpack(moves, inputs, outputs, former, blocks, info):
    spec = pl.BlockSpec(memory_space=pl.ANY)
    whole = pl.BlockSpec(memory_space=pltpu.VMEM)
    former = tuple(former or ())
    inputs = tuple(inputs)
    rows = [value.shape[0] for value in inputs]
    return pl.pallas_call(
        functools.partial(unpack_body, moves, rows, blocks, len(former)),
        out_shape=tuple(jax.ShapeDtypeStruct(shape, FULL) for shape in outputs),
        in_specs=[pl.BlockSpec(memory_space=pltpu.SMEM)] + [whole] * len(inputs) + [spec] * len(former),
        out_specs=tuple([spec] * len(outputs)),
        scratch_shapes=[pltpu.VMEM((count, UNIT), FULL) for count in rows]
        + [pltpu.SemaphoreType.DMA((len(moves),))],
        input_output_aliases={1 + len(inputs) + n: n for n in range(len(former))},
        compiler_params=pltpu.CompilerParams(vmem_limit_bytes=ROOM),
        cost_estimate=pl.CostEstimate(flops=0, bytes_accessed=6 * sum(rows) * UNIT, transcendentals=0),
        name="unpack",
    )(info, *inputs, *former)


CORES = [(0, 1), (1, 0)]


def to_other_core(values):
    return lax.ppermute(values, "tensor", CORES)


def to_other_section(values):
    return lax.ppermute(values, "section", CORES)


def to_layer(values, layer):
    return lax.ppermute(values, "section", [(1 - layer, layer)])


def ring_order():
    places = list(range(lax.axis_size("dp")))
    return places[0::2] + places[1::2][::-1]


def ring_place():
    place, count = lax.axis_index("dp"), lax.axis_size("dp")
    return jnp.where(place % 2 == 0, place // 2, count - 1 - place // 2)


def to_next(values, way):
    order = ring_order()
    route = list(zip(order, order[1:] + order[:1]))
    if way == 1:
        route = [(there, here) for here, there in route]
    return lax.ppermute(values, "dp", route)


def after(values, token):
    if token is None:
        return values
    return lax.optimization_barrier((values, token))[0]


class Ring:
    def __init__(self, parts):
        self.parts = parts
        self.count = len(parts[0])
        self.pieces = [[None] * self.count, [None] * self.count]
        self.step = 0
        self.last = 2 * (self.count - 1)
        self.flying = [to_next(parts[way][1], way) for way in range(2)]

    def advance(self, token):
        got = [after(self.flying[0], token), after(self.flying[1], token)]
        turn, count = self.step, self.count
        self.step += 1
        if turn < count - 1:
            got = [got[way] + self.parts[way][(turn + 2) % count] for way in range(2)]
        hop = max(turn - (count - 2), 0)
        if turn >= count - 2:
            for way in range(2):
                self.pieces[way][hop] = got[way]
        if self.step < self.last:
            self.flying = [to_next(got[way], way) for way in range(2)]
        return tuple(got), (hop if turn >= count - 2 else None)


def shards(
    text_stream,
    image_stream,
    region_mask,
    co_text_in,
    co_text_out,
    self_text_in,
    self_text_out,
    image_attn_in,
    image_attn_out,
    text_up,
    text_down,
    image_up,
    image_down,
    text_gain,
    text_shift,
    image_gain,
    image_shift,
):
    front = lax.axis_index("section") == 0
    core = lax.axis_index("tensor")
    blocks = lax.axis_size("dp")
    in_ring = blocks == 8
    place = ring_place() if in_ring else 0 * core
    info = jnp.stack([front.astype(jnp.int32), core.astype(jnp.int32), place.astype(jnp.int32)])
    pairs = text_stream.shape[1]
    half = pairs // 2
    real_t, real_i = text_stream.shape[2], image_stream.shape[2]
    rows_t, rows_i = round_up(real_t, 16), round_up(real_i, 16)
    wide_t, wide_i = text_stream.shape[3], image_stream.shape[3]
    text_size = D_TEXT // HEADS_TEXT
    image_size = D_IMAGE // HEADS_IMAGE

    def flat_rows(values, rows):
        grown = jnp.pad(values, ((0, 0), (0, rows - values.shape[1]), (0, 0)))
        return grown.reshape(values.shape[0] * rows, values.shape[2])

    def by_slot(weight):
        return jnp.transpose(weight, (1, 0, 2))

    own_t, own_i = half * rows_t, half * rows_i
    all_t, all_i = pairs * rows_t, pairs * rows_i
    keep = jnp.pad(region_mask, ((0, 0), (0, rows_i - real_i))).reshape(pairs, 1, rows_i)
    gain_t, shift_t, gain_i, shift_i = text_gain[0], text_shift[0], image_gain[0], image_shift[0]
    cross_in, image_in, single_in = by_slot(co_text_in), by_slot(image_attn_in[0]), by_slot(self_text_in)
    image_out, up_i, down_i = image_attn_out[0], image_up[0], image_down[0]
    up_t, down_t = text_up[0], text_down[0]
    image_out_2, cross_out_2 = to_other_core(image_out), to_other_core(co_text_out)
    up_i_2, down_i_2 = to_other_core(up_i), to_other_core(down_i)
    up_t_2, down_t_2 = to_other_core(up_t), to_other_core(down_t)
    cross = cross_in.shape[2]
    single = single_in.shape[2]
    ff_t, ff_i = up_t.shape[1], up_i.shape[1]
    tail_t = (up_t, down_t, up_t_2, down_t_2)
    tail_i = (up_i, down_i, up_i_2, down_i_2)

    far = (cross_in, image_in)
    xt_own, xt_other, xi_own, xi_other, tp, ip, ct_own, ct_give, ci_own, ci_give = launch(
        functools.partial(cross_forward, pairs, rows_t, rows_i, real_t),
        [shape_of(own_t, wide_t)] * 2
        + [shape_of(own_i, wide_i)] * 2
        + [shape_of(all_t, 3 * cross), shape_of(all_i, 3 * cross)]
        + [shape_of(own_t, cross)] * 2
        + [shape_of(own_i, cross)] * 2,
        (flat_rows(text_stream[0], rows_t), flat_rows(image_stream[0], rows_i), keep),
        far=far,
        scratch=[pltpu.VMEM((all_t, wide_t), LOW), pltpu.VMEM((all_i, wide_i), LOW)] + buffers_for(far),
        flag=info,
        work=6 * cross * (all_t * wide_t + all_i * wide_i),
        name="cross_forward",
    )
    ct_other, ci_other = ct_give, ci_give
    ci_2 = to_other_core(ci_give)
    ct_2 = to_other_core(ct_give)

    def run_first_tail(x, c0, c1, o0, o1, gain, shift, ff, rows, width, hidden, name):
        low_w, low_h = shape_of(rows, width), shape_of(rows, hidden)
        far = (o0, o1) + ff
        return launch(
            first_tail,
            [low_w, low_w, low_h, low_h]
            + [shape_of(rows, hidden, FULL)] * 2
            + [shape_of(rows, width, FULL), shape_of(rows, 128, FULL)] * 2,
            (x, c0, c1, gain, shift),
            far=far,
            scratch=[pltpu.VMEM((rows, width), FULL)] + buffers_for(far),
            flag=info,
            work=4 * rows * width * (o0.shape[0] + 2 * hidden),
            name=name,
        )

    bi, yi, hi0, hi1, si0, si1, ni1, ii1, ni2, ii2 = run_first_tail(
        after(xi_own, (up_t_2, down_t_2, cross_out_2, ct_2)), ci_own, ci_2, image_out, image_out_2, gain_i, shift_i,
        tail_i, own_i, wide_i, ff_i, "tail_i"
    )
    image_in_2, single_in_2, single_out_2 = [
        to_other_core(after(value, bi)) for value in (image_in, single_in, self_text_out)
    ]
    bi_here, bi = bi, to_layer(bi, 1)
    bt, yt, ht0, ht1, st0, st1, nt1, it1, nt2, it2 = run_first_tail(
        after(xt_own, bi_here), ct_own, ct_2, co_text_out, cross_out_2, gain_t, shift_t, tail_t, own_t, wide_t, ff_t, "tail_t"
    )

    def run_self(rows, real, size, width, hidden, x, w0, w1, masked, o0, o1, gain, shift, ff, seed, y, h0, h1, c, name):
        count = half * rows
        inner = w0.shape[2]
        low_w, low_h = shape_of(count, width), shape_of(count, hidden)
        outputs = [low_w, low_w, shape_of(count, cross), shape_of(count, 3 * cross)]
        outputs += [low_w, low_w, low_h, low_h, low_w, low_h] + [shape_of(2, width, FULL)] * 2
        outputs += [shape_of(count, 2 * width + hidden + 4 * cross)]
        scratch = [pltpu.VMEM((count, 3 * inner), LOW)] * 2
        scratch += [pltpu.VMEM((count, hidden), FULL)] * 2
        scratch += [pltpu.VMEM((count, width), FULL), pltpu.VMEM((count, 128), FULL)] * 2
        scratch += [pltpu.VMEM((count, width), FULL)] + [pltpu.VMEM((count, inner), LOW)] * 2
        scratch += [pltpu.VMEM((count, columns), LOW) for columns in (hidden, cross, 3 * cross)]
        weights = (w0, w1, o0, o1) + ff
        return launch(
            functools.partial(self_layer, masked, half, rows, real, size, cross),
            outputs,
            (x, seed, gain, shift, keep),
            far=weights + (y, h0, h1, c),
            scratch=scratch + buffers_for(weights),
            flag=info,
            work=8 * count * width * (4 * inner + 2 * hidden),
            name=name,
        )

    i2 = run_self(
        rows_i, real_i, image_size, wide_i, ff_i, bi, image_in, image_in_2, True, image_out, image_out_2,
        gain_i, shift_i, tail_i, xi_own, yi, hi0, hi1, ci_own, "self_i",
    )
    seed_i = to_layer(i2[1], 0)
    bt = to_layer(bt, 1)
    t2 = run_self(
        rows_t, real_t, text_size, wide_t, ff_t, after(bt, i2[1]), single_in, single_in_2, False,
        self_text_out, single_out_2, gain_t, shift_t, tail_t, xt_own, yt, ht0, ht1, ct_own, "self_t",
    )
    seed_t = to_layer(t2[1], 0)
    (oi, unused, ci_own, pi_own, dai, dfi, dui0, dui1, yi, hi0, dgi, dsi, give_i) = i2
    (ot, unused, ct_own, pt_own, dat, dft, dut0, dut1, yt, ht0, dgt, dst, give_t) = t2
    left_t, left_i = to_other_core(give_t), to_other_core(give_i)

    def run_tail_back(seed, kept, o0, o1, gain, ff, given, rows, width, hidden, name):
        low_w, low_h = shape_of(rows, width), shape_of(rows, hidden)
        outputs = [low_w, low_h, low_w] + [shape_of(2, width, FULL)] * 2
        outputs += [shape_of(rows, width, FULL), shape_of(rows, cross)]
        outputs += [shape_of(rows, 2 * width + hidden + cross)]
        s0, s1, n1, i1, n2, i2 = kept
        u0, d0, u1, d1 = ff
        late = (n2, i2, d0, s0, u0, d1, s1, u1, n1, i1, o0, o1)
        return launch(
            first_tail_back,
            outputs,
            (seed, gain),
            far=late + given,
            scratch=[pltpu.VMEM((rows, hidden), LOW)] + buffers_for(late),
            flag=info,
            work=4 * rows * width * (cross + 2 * hidden),
            name=name,
        )


    def choose(first, second):
        return jnp.where(front, first, second)

    ff_layout = Layout(
        blocks,
        [
            ("down_t", ff_t, wide_t),
            ("up_t", wide_t, ff_t),
            ("up_i", wide_i, ff_i),
            ("down_i", ff_i, wide_i),
        ],
        {"down_t": 1, "up_t": 3, "up_i": 2, "down_i": 1},
    )
    attn_layout = Layout(
        blocks,
        [
            ("in_t", wide_t, 3 * cross),
            ("out_t", cross, wide_t),
            ("in_i", wide_i, 3 * cross),
            ("out_i", cross, wide_i),
            ("small", blocks * 16, UNIT),
        ],
    )
    text_rows = attn_layout.after["out_t"]

    out = run_tail_back(
        seed_i, (si0, si1, ni1, ii1, ni2, ii2), image_out, image_out_2, gain_i, tail_i,
        (dfi, dui0, dui1, dai, dgi, dsi), own_i, wide_i, ff_i, "tail_back_i",
    )
    dfi, dui0, dai, dgi, dsi, dri, dci_own, give_i = out
    right_i = to_other_core(give_i)
    out = run_tail_back(
        after(seed_t, dci_own), (st0, st1, nt1, it1, nt2, it2), co_text_out, cross_out_2, gain_t, tail_t,
        (dft, dut0, dut1, dat, dgt, dst), own_t, wide_t, ff_t, "tail_back_t",
    )
    dft, dut0, dat, dgt, dst, drt, dct_own, give_t = out
    right_t = to_other_core(give_t)
    small = jnp.concatenate([dgt, dst, dgi, dsi], axis=1)
    small = small + to_other_core(small)
    small_rows = round_up(-(-small.size // UNIT), blocks) // blocks
    small = jnp.pad(small.reshape(-1), (0, blocks * small_rows * UNIT - small.size))
    small = small.reshape(blocks, small_rows, UNIT)
    small = jnp.pad(small, ((0, 0), (0, 16 - small_rows), (0, 0))).reshape(blocks * 16, UNIT)
    ff_parts = pack(
        ff_layout,
        {
            "down_t": ((ht0, 0, ff_t), (left_t, wide_t, ff_t), (after(dft, small), 0, wide_t), (right_t, 0, wide_t)),
            "up_t": ((yt, 0, wide_t), (left_t, 0, wide_t), (dut0, 0, ff_t), (right_t, wide_t, ff_t)),
            "up_i": ((yi, 0, wide_i), (left_i, 0, wide_i), (dui0, 0, ff_i), (right_i, wide_i, ff_i)),
            "down_i": ((hi0, 0, ff_i), (left_i, wide_i, ff_i), (dfi, 0, wide_i), (right_i, 0, wide_i)),
        },
        info,
        "pack_ff",
    )
    token = ff_parts[0][1]
    ff = Ring(ff_parts) if in_ring else None
    far = (cross_in, image_in)
    out = launch(
        functools.partial(cross_backward, (wide_t, wide_i), pairs, rows_t, rows_i, real_t),
        [shape_of(own_t, 3 * cross)] * 2
        + [shape_of(own_i, 3 * cross)] * 2
        + [shape_of(own_t, wide_t, FULL)] * 2
        + [shape_of(own_i, wide_i, FULL)] * 2,
        (after(tp, token), ip, dct_own, dci_own, keep),
        far=far + (right_t, right_i, pt_own, left_t, pi_own, left_i),
        scratch=[pltpu.VMEM(v.shape, v.dtype) for v in far]
        + [pltpu.VMEM((own_t, cross), LOW), pltpu.VMEM((own_i, cross), LOW), pltpu.SemaphoreType.DMA((4,))],
        flag=info,
        work=6 * cross * (all_t * wide_t + all_i * wide_i),
        name="cross_backward",
    )
    dtp_own, dtp_other, dip_own, dip_other, dxt_own, dxt_give, dxi_own, dxi_give = out
    token = dtp_own
    if in_ring:
        token, unused = ff.advance(token)

    def columns(part, wide, hidden):
        starts = {"c": wide + hidden, "x": wide + hidden + 4 * cross}
        return starts[part]

    ct_column, xt_column = columns("c", wide_t, ff_t), columns("x", wide_t, ff_t)
    ci_column, xi_column = columns("c", wide_i, ff_i), columns("x", wide_i, ff_i)
    attn_parts = pack(
        attn_layout,
        {
            "in_t": (
                ((xt_own, 0), (bt, 0), wide_t),
                ((xt_other, 0), (left_t, xt_column), wide_t),
                (after(dtp_own, token), 0, 3 * cross),
                (dtp_other, 0, 3 * cross),
            ),
            "out_t": (
                (ct_own, 0, cross),
                ((ct_give, 0), (left_t, ct_column), cross),
                (dat, 0, wide_t),
                (right_t, wide_t + ff_t, wide_t),
            ),
            "in_i": (
                ((xi_own, 0), (bi, 0), wide_i),
                ((xi_other, 0), (left_i, xi_column), wide_i),
                (dip_own, 0, 3 * cross),
                (dip_other, 0, 3 * cross),
            ),
        },
        info,
        "pack_attention",
    )
    token = attn_parts[0][1]
    if in_ring:
        token, unused = ff.advance(token)
    attn_parts = pack(
        attn_layout,
        {
            "out_i": (
                (ci_own, 0, cross),
                ((ci_give, 0), (left_i, ci_column), cross),
                (after(dai, token), 0, wide_i),
                (right_i, wide_i + ff_i, wide_i),
            ),
            "small": ((small, 0, UNIT),),
        },
        info,
        "pack_rest",
        attn_parts,
    )

    def choose(first, second):
        return jnp.where(front, first, second)

    def result(rest, partial, other, output, rows, real, token):
        mine = choose(rest + partial + after(to_other_core(other), token), output.astype(FULL))
        mine = mine.astype(LOW).reshape(half, rows, -1)[:, :real]
        got = to_other_core(mine)
        return jnp.concatenate(
            [jnp.where(core == 0, mine, got), jnp.where(core == 0, got, mine)], axis=0
        )[None]

    main_shapes = [
        (ff_t, wide_t),
        (wide_t, ff_t),
        (wide_i, ff_i),
        (ff_i, wide_i),
        (3, wide_i, cross),
        (cross, wide_i),
        (blocks * 16, UNIT),
    ]
    text_shapes = [(3, wide_t, cross), (cross, wide_t), (3, wide_t, single), (self_text_out.shape[0], wide_t)]
    main_moves, text_moves = [], []

    def move(target, source, way, row, real, unit, output, shape, mark=0):
        slot, column, columns = None, unit * UNIT, UNIT
        if len(shape) == 3:
            slot, column = column // cross, column % cross
            columns = min(UNIT, shape[2] - column)
        if columns > 0:
            target.append((source, way, row, real, output, slot, column, columns, mark))

    for index, unit, way, row, real in ff_layout.units:
        move(main_moves, way, way, row, real, unit, index, main_shapes[index])
    for index, unit, way, row, real in attn_layout.units:
        if index >= 2:
            move(main_moves, 2 + way, way, row, real, unit, index + 2, main_shapes[index + 2])
        else:
            for mark in (1, 2):
                move(text_moves, way + 2 * (mark - 1), way, row, real, unit, index, text_shapes[index], mark)
                move(text_moves, way + 4 - 2 * mark, way, row, real, unit, index + 2, text_shapes[index + 2], mark)

    main, text = None, None

    def shifted(moves, hop, source_shift, row_shift):
        result = []
        for source, way, row, *rest in moves:
            result.append((source_shift(source), way, hop, row + row_shift(source), *rest))
        return result

    def spread_main(hops, ff, attn, main):
        inputs, moves = [], []
        for number, hop in enumerate(hops):
            inputs += [ff[0][hop], ff[1][hop], attn[0][hop], attn[1][hop]]
            moves += shifted(main_moves, hop, lambda source: source + 4 * number, lambda source: 0)
        return unpack(moves, inputs, main_shapes, main, blocks, info)

    def spread_text(hops, attn, crossed, text):
        inputs, moves, both = [], [], text_rows[0] + text_rows[1]
        for hop in hops:
            inputs += [attn[0][hop], attn[1][hop]]
        places = []
        for array in crossed:
            places += [(len(inputs), row) for row in range(0, array.shape[0], both)]
            inputs.append(array)
        for number, hop in enumerate(hops):
            moves += shifted(
                text_moves,
                hop,
                lambda source: source + 2 * number if source < 2 else places[number][0],
                lambda source: 0 if source < 2 else places[number][1] + (source - 2) * text_rows[0],
            )
        return unpack(moves, inputs, text_shapes, text, blocks, info)

    def cross_over(attn, hops):
        return to_other_section(
            jnp.concatenate([attn[way][hop][: text_rows[way]] for hop in hops for way in range(2)], axis=0)
        )

    if in_ring:
        attn = Ring(attn_parts)
        token = attn_parts[0][1]
        results = (
            result(drt, dxt_own, dxt_give, ot, rows_t, real_t, token),
            result(dri, dxi_own, dxi_give, oi, rows_i, real_i, token),
        )
        token = (token, results)
        groups = [(0, 1), (2, 3), (4, 5), (6,), (7,)]
        crossed = [None] * len(groups)
        while attn.step < attn.last:
            if ff.step < ff.last:
                token, unused = ff.advance(token)
            token, hop = attn.advance(token)
            if hop is None:
                continue
            if hop == 2:
                first = after(crossed[0], token)
                relay = [to_next(first[: text_rows[0]], 1), to_next(first[text_rows[0] : sum(text_rows)], 0)]
            if hop == 4:
                crossed[-1] = jnp.concatenate([after(value, token) for value in relay], axis=0)
                token = (token, crossed[-1])
            for number, group in enumerate(groups):
                if hop == group[-1]:
                    if number < len(groups) - 1:
                        crossed[number] = cross_over(attn.pieces, group)
                    main = spread_main(group, ff.pieces, attn.pieces, main)
                    token = (token, main)
                elif number and hop == group[0] and len(group) > 1:
                    text = spread_text(groups[number - 1], attn.pieces, [crossed[number - 1]], text)
                    token = (token, text)
        text = spread_text(groups[-3], attn.pieces, crossed[-3:-2], text)
        text = spread_text((6, 7), attn.pieces, crossed[-2:], text)
    else:
        results = (
            result(drt, dxt_own, dxt_give, ot, rows_t, real_t, token),
            result(dri, dxi_own, dxi_give, oi, rows_i, real_i, token),
        )
        ff, attn = lax.psum((ff_parts, attn_parts), "dp")
        for hop in range(0, blocks, 2):
            main = spread_main((hop, hop + 1), ff, attn, main)
            text = spread_text((hop, hop + 1), attn, [cross_over(attn, (hop, hop + 1))], text)
    down_t_grad, up_t_grad, up_i_grad, down_i_grad, in_i_grad, out_i_grad, small = main
    co_in_grad, co_out_grad, self_in_grad, self_out_grad = text
    small = small.reshape(blocks, 16, UNIT)[:, :small_rows].reshape(-1)[: 4 * (wide_t + wide_i)]
    small = small.reshape(2, 2 * (wide_t + wide_i))
    small = jnp.split(small, [wide_t, 2 * wide_t, 2 * wide_t + wide_i], axis=1)

    return (
        results[0],
        results[1],
        by_slot(co_in_grad),
        co_out_grad,
        by_slot(self_in_grad),
        self_out_grad,
        by_slot(in_i_grad)[None],
        out_i_grad[None],
        up_t_grad[None],
        down_t_grad[None],
        up_i_grad[None],
        down_i_grad[None],
        small[0][None],
        small[1][None],
        small[2][None],
        small[3][None],
    )


def solution(mesh):
    in_specs = (
        P("section", "dp", None, None),
        P("section", "dp", None, None),
        P("dp", None),
        P(None, None, "tensor"),
        P("tensor", None),
        P(None, None, "tensor"),
        P("tensor", None),
        P("section", None, None, "tensor"),
        P("section", "tensor", None),
        P("section", None, "tensor"),
        P("section", "tensor", None),
        P("section", None, "tensor"),
        P("section", "tensor", None),
        P("section", None, None),
        P("section", None, None),
        P("section", None, None),
        P("section", None, None),
    )
    out_specs = (
        P("section", "dp", None, None),
        P("section", "dp", None, None),
        P(None, None, "tensor"),
        P("tensor", None),
        P(None, None, "tensor"),
        P("tensor", None),
        P("section", None, None, "tensor"),
        P("section", "tensor", None),
        P("section", None, "tensor"),
        P("section", "tensor", None),
        P("section", None, "tensor"),
        P("section", "tensor", None),
        P("section", None, None),
        P("section", None, None),
        P("section", None, None),
        P("section", None, None),
    )
    return jax.shard_map(shards, mesh=mesh, in_specs=in_specs, out_specs=out_specs, check_vma=False)
```

```python
import functools
import math

import jax
import jax.numpy as jnp
from jax import lax
from jax.experimental import pallas as pl
from jax.experimental.pallas import tpu as pltpu
from jax.sharding import PartitionSpec as P

D_TEXT = 768
HEADS_TEXT = 12
D_IMAGE = 1024
HEADS_IMAGE = 8
D_CO = 1024
HEADS_CO = 8

LOW = jnp.bfloat16
FULL = jnp.float32
TILE = 512
UNIT = 256
ROOM = 56 * 1024 * 1024


def times(left, right):
    return jnp.dot(left, right, preferred_element_type=FULL)


def times_back(left, right):
    return lax.dot_general(left, right, (((1,), (1,)), ((), ())), preferred_element_type=FULL)


def back_times(left, right):
    return lax.dot_general(left, right, (((0,), (0,)), ((), ())), preferred_element_type=FULL)


def norm_rows(rows):
    centre = rows - jnp.mean(rows, axis=-1, keepdims=True)
    spread = jnp.mean(centre * centre, axis=-1, keepdims=True)
    inverse = lax.rsqrt(spread + 1e-05)
    return centre * inverse, inverse


def norm_back(unit, inverse, gain, grad):
    scaled = grad * gain
    first = jnp.mean(scaled, axis=-1, keepdims=True)
    second = jnp.mean(scaled * unit, axis=-1, keepdims=True)
    dgain = jnp.sum(grad * unit, axis=0, keepdims=True)
    dshift = jnp.sum(grad, axis=0, keepdims=True)
    return inverse * (scaled - first - unit * second), dgain, dshift


def gelu_both(inputs):
    rate = 0.7978845608028654
    square = inputs * inputs
    bent = jnp.tanh(rate * inputs * (1.0 + 0.044715 * square))
    half = 0.5 * (1.0 + bent)
    slope = half + 0.5 * inputs * (1.0 - bent * bent) * rate * (1.0 + 0.134145 * square)
    return inputs * half, slope


def heads_of(query, size):
    if size == query.shape[1]:
        return [query]
    lower = lax.broadcasted_iota(jnp.int32, (1, query.shape[1]), 1) < size
    low = lower.astype(FULL).astype(LOW)
    return [query * low, query * (1 - low)]


def merged(parts, size):
    if len(parts) == 1:
        return parts[0]
    return jnp.where(lax.broadcasted_iota(jnp.int32, parts[0].shape, 1) < size, parts[0], parts[1])


def softmax_all(pairs, alloweds, size):
    scores = [times_back(query, keys) for query, keys in pairs]
    scores = [
        jnp.where(allowed, score * (1.0 / math.sqrt(size)), -1000000000.0)
        for score, allowed in zip(scores, alloweds)
    ]
    tops = [jnp.max(score, axis=-1, keepdims=True) for score in scores]
    raised = [jnp.exp(score - top) for score, top in zip(scores, tops)]
    shares = [1.0 / jnp.sum(value, axis=-1, keepdims=True) for value in raised]
    return [value * share for value, share in zip(raised, shares)]


def attend_all(units, size):
    singles = [(q, k, v, a) for query, k, v, a in units for q in heads_of(query, size)]
    weights = softmax_all([one[:2] for one in singles], [one[3] for one in singles], size)
    contexts = [times(w.astype(LOW), one[2]) for w, one in zip(weights, singles)]
    heads = len(singles) // len(units)
    return [merged(contexts[n * heads : (n + 1) * heads], size).astype(LOW) for n in range(len(units))]


def attend_back_all(units, size):
    scaling = 1.0 / math.sqrt(size)
    singles = [
        (q, k, v, a, d, query, dcontext)
        for query, k, v, a, dcontext in units
        for q, d in zip(heads_of(query, size), heads_of(dcontext, size))
    ]
    weights = softmax_all([one[:2] for one in singles], [one[3] for one in singles], size)
    dweights = [times_back(one[4], one[2]) for one in singles]
    dvalues = [back_times(w.astype(LOW), one[6]) for w, one in zip(weights, singles)]
    sums = [jnp.sum(dw * w, axis=-1, keepdims=True) for dw, w in zip(dweights, weights)]
    dscores = [(w * (dw - s)).astype(LOW) for w, dw, s in zip(weights, dweights, sums)]
    dqueries = [times(ds, one[1]) * scaling for ds, one in zip(dscores, singles)]
    dkeys = [back_times(ds, one[5]) * scaling for ds, one in zip(dscores, singles)]
    heads = len(singles) // len(units)
    return [
        [merged(grads[n * heads : (n + 1) * heads], size).astype(LOW) for grads in (dqueries, dkeys, dvalues)]
        for n in range(len(units))
    ]


def wide(column):
    return jnp.broadcast_to(column, (column.shape[0], 128))


class Late:
    def __init__(self, source, target, signal):
        self.target = target
        self.copy = pltpu.make_async_copy(source, target, signal)
        self.copy.start()
        self.here = False

    def get(self):
        if not self.here:
            self.copy.wait()
            self.here = True
        return self.target


class Here:
    def __init__(self, target):
        self.target = target

    def get(self):
        return self.target


def fetch(sources, targets, signals):
    return [Late(s, t, signals.at[n]) for n, (s, t) in enumerate(zip(sources, targets))]


def pass_through(sources, targets, signals):
    copies = [
        pltpu.make_async_copy(s, t, signals.at[n]) for n, (s, t) in enumerate(zip(sources, targets))
    ]
    for copy in copies:
        copy.start()
    for copy in copies:
        copy.wait()


def tail_forward(residual, contexts, out_w, gain, shift, up_w, down_w, kept, mixed, leave=None):
    normed_ref, hidden, slopes, unit1, inv1, unit2, inv2 = kept
    branch = times(contexts[0], out_w[0].get()[...]) + times(contexts[1], out_w[1].get()[...])
    unit, inverse = norm_rows(residual.astype(FULL) + branch)
    unit1[...] = unit.astype(unit1.dtype)
    inv1[...] = wide(inverse)
    normed = unit * gain[0:1, :] + shift[0:1, :]
    normed_ref[...] = normed.astype(LOW)
    mixed[...] = normed
    if leave is not None:
        leave.go(normed_ref, unit1, inv1)
    for half in range(2):
        up, down = up_w[half].get(), down_w[half].get()
        for start in range(0, up.shape[1], TILE):
            span = pl.ds(start, TILE)
            value, slope = gelu_both(times(normed_ref[...], up[:, span]))
            hidden[half][:, span] = value.astype(LOW)
            slopes[half][:, span] = slope.astype(slopes[half].dtype)
            mixed[...] += times(hidden[half][:, span], down[span, :])
        if leave is not None:
            leave.go(hidden[half], slopes[half])
    unit, inverse = norm_rows(mixed[...])
    unit2[...] = unit.astype(unit2.dtype)
    inv2[...] = wide(inverse)
    return unit * gain[1:2, :] + shift[1:2, :]


def tail_backward(seed, kept, out_w, gain, up_w, down_w, grads, total, leave=None):
    slopes, unit1, inv1, unit2, inv2 = kept
    df, du, da, dgain, dshift = grads
    dsecond, dgain1, dshift1 = norm_back(
        unit2.get()[...].astype(FULL), inv2.get()[:, 0:1], gain[1:2, :], seed
    )
    total[...] = dsecond
    df[...] = dsecond.astype(LOW)
    for half in range(2):
        up, down, slope = up_w[half].get(), down_w[half].get(), slopes[half].get()
        for start in range(0, up.shape[1], TILE):
            span = pl.ds(start, TILE)
            dhidden = times_back(df[...], down[span, :])
            du[half][:, span] = (dhidden * slope[:, span].astype(FULL)).astype(LOW)
            total[...] += times_back(du[half][:, span], up[:, span])
    dfirst, dgain0, dshift0 = norm_back(
        unit1.get()[...].astype(FULL), inv1.get()[:, 0:1], gain[0:1, :], total[...]
    )
    dgain[...] = jnp.concatenate([dgain0, dgain1], axis=0)
    dshift[...] = jnp.concatenate([dshift0, dshift1], axis=0)
    total[...] = dfirst
    da[...] = dfirst.astype(LOW)
    if leave is not None:
        leave.go(df, du[0], da, total)
    return [times_back(da[...], w.get()[...]).astype(LOW) for w in out_w]


def shape_of(rows, columns, kind=LOW):
    return jax.ShapeDtypeStruct((rows, columns), kind)


class Leave:
    def __init__(self, buffers, targets, signals):
        self.buffers, self.targets, self.signals = buffers, targets, signals
        self.begun = {}

    def go(self, *buffers):
        for buffer in buffers:
            number = [one is buffer for one in self.buffers].index(True)
            copy = pltpu.make_async_copy(buffer, self.targets[number], self.signals.at[number])
            copy.start()
            self.begun[number] = copy

    def finish(self):
        self.go(*[one for number, one in enumerate(self.buffers) if number not in self.begun])
        for copy in self.begun.values():
            copy.wait()
        self.begun = {}


def launch(body, outputs, args, far=(), scratch=(), flag=None, work=0, name=None):
    whole, anywhere = pl.BlockSpec(memory_space=pltpu.VMEM), pl.BlockSpec(memory_space=pl.ANY)
    moved = sum(
        math.prod(v.shape) * v.dtype.itemsize for v in tuple(args) + tuple(far) + tuple(outputs)
    )
    total, results = len(args) + len(far), len(outputs)

    def whole_body(info, *refs):
        targets, refs = refs[total : total + results], refs[:total] + refs[total + results :]
        outs, signals = refs[total : total + results], refs[total + results]
        body(Leave(outs, targets, signals), info, *refs[:total], *outs, *refs[total + results + 1 :])

    own = [pltpu.VMEM(v.shape, v.dtype) for v in outputs] + [pltpu.SemaphoreType.DMA((results,))]
    return pl.pallas_call(
        whole_body,
        out_shape=tuple(outputs),
        in_specs=[pl.BlockSpec(memory_space=pltpu.SMEM)] + [whole] * len(args) + [anywhere] * len(far),
        out_specs=tuple([anywhere] * results),
        scratch_shapes=own + list(scratch),
        compiler_params=pltpu.CompilerParams(vmem_limit_bytes=ROOM),
        cost_estimate=pl.CostEstimate(flops=work, bytes_accessed=moved, transcendentals=0),
        name=name,
    )(flag, *args, *far)


def buffers_for(far):
    return [pltpu.VMEM(v.shape, v.dtype) for v in far] + [pltpu.SemaphoreType.DMA((len(far),))]


def rows_at(pair, rows):
    return pl.ds(pl.multiple_of(pair * rows, 16), rows)


def slab(index):
    return pl.ds(index * 128, 128)


def cross_forward(
    pairs, rows_t, rows_i, real_t, leave, info, x_t, x_i, keep, far_t, far_i,
    xt_own, xt_other, xi_own, xi_other, tp, ip, ct_own, ct_other, ci_own, ci_other, xt, xi, wt, wi, signals,
):
    half = pairs // 2
    for place in range(pairs):
        pair = lax.rem(place + half * info[1], pairs)
        text, image = x_t[rows_at(pair, rows_t), :], x_i[rows_at(pair, rows_i), :]
        xt[place * rows_t : (place + 1) * rows_t, :] = text
        xi[place * rows_i : (place + 1) * rows_i, :] = image
        inside = place % half
        (xt_own, xt_other)[place // half][inside * rows_t : (inside + 1) * rows_t, :] = text
        (xi_own, xi_other)[place // half][inside * rows_i : (inside + 1) * rows_i, :] = image

    @pl.when(info[0] == 0)
    def idle():
        leave.finish()

    @pl.when(info[0] == 1)
    def work():
        width = ct_own.shape[1]
        weights = fetch((far_t, far_i), (wt, wi), signals)
        leave.go(xt_own, xt_other, xi_own, xi_other)
        for late, x, p in ((weights[0], xt, tp), (weights[1], xi, ip)):
            for slot in range(3):
                p[:, pl.ds(slot * width, width)] = times(x[...], late.get()[slot]).astype(LOW)
            leave.go(p)
        text_keys = lax.broadcasted_iota(jnp.int32, (1, rows_t), 1) < real_t
        slabs = width // 128

        def each(pair, carry):
            at_t, at_i = rows_at(pair, rows_t), rows_at(pair, rows_i)
            for group, ct, ci in ((0, ct_own, ci_own), (half, ct_other, ci_other)):
                from_t, from_i = rows_at(pair + group, rows_t), rows_at(pair + group, rows_i)
                kept = keep[lax.rem(pair + group + half * info[1], pairs)] > 0
                texts, images = [], []
                for n in range(slabs):
                    first, second, third = slab(n), slab(slabs + n), slab(2 * slabs + n)
                    texts.append((tp[from_t, first], ip[from_i, second], ip[from_i, third], kept))
                    images.append((ip[from_i, first], tp[from_t, second], tp[from_t, third], text_keys))
                results = zip(attend_all(texts, 128), attend_all(images, 128))
                for n, (text, image) in enumerate(results):
                    ct[at_t, slab(n)] = text
                    ci[at_i, slab(n)] = image
            return carry

        lax.fori_loop(0, half, each, 0, unroll=True)
        leave.finish()


def first_tail(
    leave, info, x, c0, c1, gain, shift, *refs
):
    far, refs = refs[:6], refs[6:]
    out, y, h0, h1, s0, s1, n1, i1, n2, i2, mixed = refs[:11]
    near, signals = refs[11:17], refs[17]

    @pl.when(info[0] == 1)
    def work():
        o0, o1, u0, d0, u1, d1 = fetch(far, near, signals)
        kept = (y, (h0, h1), (s0, s1), n1, i1, n2, i2)
        out[...] = tail_forward(
            x[...], (c0[...], c1[...]), (o0, o1), gain, shift, (u0, u1), (d0, d1), kept, mixed, leave
        ).astype(LOW)
        leave.finish()


def self_layer(
    masked, half, rows, real, size, stride, leave, info, x, seed, gain, shift, keep, *refs
):
    far, refs = refs[:12], refs[12:]
    (out, dx, c0, p0, da, df, du0, du1, y, h0, dgain, dshift, give) = refs[:13]
    (q0, q1, s0, s1, n1, i1, n2, i2, mixed, dc0, dc1, h1, c1, p1) = refs[13:27]
    near, signals = refs[27:35], refs[35]
    width = q0.shape[1] // 3
    wide_x, wide_h, wide_c = x.shape[1], h1.shape[1], c1.shape[1]
    spans = []
    for columns in (wide_x, wide_h, wide_c, p1.shape[1], wide_x):
        spans.append(pl.ds(sum(span.size for span in spans), columns))

    @pl.when(info[0] == 1)
    def pass_on():
        targets = (y, h0, c0, give.at[:, spans[0]], give.at[:, spans[1]])
        pass_through((far[8], far[9], far[11], far[8], far[10]), targets, signals)
        leave.go(y, h0, c0, give)
        for copy in leave.begun.values():
            copy.wait()
        leave.begun = {}

    @pl.when(info[0] == 0)
    def work():
        w0, w1, o0, o1, u0, d0, u1, d1 = fetch(far[:8], near, signals)
        slabs = width // 128
        if c0.shape[1] != width:
            rest = pl.ds(width, c0.shape[1] - width)
            c0[:, rest] = jnp.zeros((c0.shape[0], c0.shape[1] - width), LOW)
            c1[:, rest] = jnp.zeros((c0.shape[0], c0.shape[1] - width), LOW)
            for slot in range(3):
                rest = pl.ds(slot * stride + width, stride - width)
                p0[:, rest] = jnp.zeros((p0.shape[0], stride - width), LOW)
                p1[:, rest] = jnp.zeros((p0.shape[0], stride - width), LOW)
        for w, q in ((w0, q0), (w1, q1)):
            for slot in range(3):
                q[:, pl.ds(slot * width, width)] = times(x[...], w.get()[slot]).astype(LOW)

        def allowed(pair):
            if not masked:
                return lax.broadcasted_iota(jnp.int32, (1, rows), 1) < real
            return keep[pair + half * info[1]] > 0

        def forward(pair, carry):
            at = rows_at(pair, rows)
            kept = allowed(pair)
            units = [
                (q[at, slab(n)], q[at, slab(slabs + n)], q[at, slab(2 * slabs + n)], kept)
                for q in (q0, q1)
                for n in range(slabs)
            ]
            results = attend_all(units, size)
            for n, value in enumerate(results):
                (c0, c1)[n // slabs][at, slab(n % slabs)] = value
            return carry

        lax.fori_loop(0, half, forward, 0, unroll=True)
        leave.go(c0)
        used = pl.ds(0, width)
        kept = (y, (h0, h1), (s0, s1), n1, i1, n2, i2)
        out[...] = tail_forward(
            x[...], (c0[:, used], c1[:, used]), (o0, o1), gain, shift, (u0, u1), (d0, d1), kept, mixed
        ).astype(LOW)
        leave.go(out, y, h0)
        held = ((Here(s0), Here(s1)), Here(n1), Here(i1), Here(n2), Here(i2))
        dcs = tail_backward(
            seed[...].astype(FULL),
            held,
            (o0, o1),
            gain,
            (u0, u1),
            (d0, d1),
            (df, (du0, du1), da, dgain, dshift),
            mixed,
        )
        leave.go(da, df, du0, du1, dgain, dshift)
        dc0[...] = dcs[0]
        dc1[...] = dcs[1]

        def backward(pair, carry):
            at = rows_at(pair, rows)
            kept = allowed(pair)
            units = [
                (q[at, slab(n)], q[at, slab(slabs + n)], q[at, slab(2 * slabs + n)], kept, dc[at, slab(n)])
                for q, dc in ((q0, dc0), (q1, dc1))
                for n in range(slabs)
            ]
            results = attend_back_all(units, size)
            for n, grads in enumerate(results):
                for slot in range(3):
                    column = slot * stride + (n % slabs) * 128
                    (p0, p1)[n // slabs][at, pl.ds(column, 128)] = grads[slot]
            return carry

        lax.fori_loop(0, half, backward, 0, unroll=True)
        for span, value in zip(spans, (y, h1, c1, p1, x)):
            give[:, span] = value[...]
        leave.go(p0, give)
        for w, p in ((w0, p0), (w1, p1)):
            for slot in range(3):
                mixed[...] += times_back(p[:, pl.ds(slot * stride, width)], w.get()[slot])
        dx[...] = mixed[...].astype(LOW)
        leave.finish()


def first_tail_back(leave, info, seed, gain, *refs):
    far, refs = refs[:18], refs[18:]
    df, du0, da, dgain, dshift, dres, dc0, give = refs[:8]
    du1, near, signals = refs[8], refs[9:21], refs[21]
    spans = []
    for columns in (df.shape[1], du1.shape[1], da.shape[1], dc0.shape[1]):
        spans.append(pl.ds(sum(span.size for span in spans), columns))

    @pl.when(info[0] == 0)
    def pass_on():
        df_in, du0_in, du1_in, da_in, dgain_in, dshift_in = far[12:]
        pass_through(
            (df_in, du0_in, da_in, dgain_in, dshift_in, df_in, du1_in, da_in),
            (df, du0, da, dgain, dshift) + tuple(give.at[:, span] for span in spans[:3]),
            signals,
        )
        leave.finish()

    @pl.when(info[0] == 1)
    def work():
        n2, i2, d0, s0, u0, d1, s1, u1, n1, i1, o0, o1 = fetch(far[:12], near, signals)
        dcs = tail_backward(
            seed[...].astype(FULL),
            ((s0, s1), n1, i1, n2, i2),
            (o0, o1),
            gain,
            (u0, u1),
            (d0, d1),
            (df, (du0, du1), da, dgain, dshift),
            dres,
            leave,
        )
        dc0[...] = dcs[0]
        for span, value in zip(spans, (df[...], du1[...], da[...], dcs[1])):
            give[:, span] = value
        leave.finish()


def cross_backward(
    wides, pairs, rows_t, rows_i, real_t, leave, info,
    tp, ip, dct_own, dci_own, keep, *refs
):
    far, refs = refs[:8], refs[8:]
    dtp_own, dtp_other, dip_own, dip_other, dxt_own, dxt_other, dxi_own, dxi_other = refs[:8]
    wt, wi, dct_other, dci_other, signals = refs[8:]
    width = dct_own.shape[1]
    slabs = width // 128
    half = pairs // 2

    @pl.when(info[0] == 0)
    def pass_on():
        sources = []
        for mine, got in ((far[4], far[5]), (far[6], far[7])):
            start = got.shape[1] - wides[len(sources) // 2] - mine.shape[1]
            sources += [mine, got.at[:, pl.ds(start, mine.shape[1])]]
        pass_through(sources, (dtp_own, dtp_other, dip_own, dip_other), signals)
        leave.finish()

    @pl.when(info[0] == 1)
    def work():
        got = [far[n].at[:, pl.ds(far[n].shape[1] - width, width)] for n in (2, 3)]
        weights = fetch(
            (got[0], got[1], far[0], far[1]), (dct_other, dci_other, wt, wi), signals
        )
        weights[0].get()
        weights[1].get()
        weights = weights[2:]
        text_keys = lax.broadcasted_iota(jnp.int32, (1, rows_t), 1) < real_t

        def each(pair, carry):
            at_t, at_i = rows_at(pair, rows_t), rows_at(pair, rows_i)
            for group, dct, dci, dtp, dip in (
                (0, dct_own, dci_own, dtp_own, dip_own),
                (half, dct_other, dci_other, dtp_other, dip_other),
            ):
                from_t, from_i = rows_at(pair + group, rows_t), rows_at(pair + group, rows_i)
                kept = keep[lax.rem(pair + group + half * info[1], pairs)] > 0
                texts, images = [], []
                for n in range(slabs):
                    first, second, third = slab(n), slab(slabs + n), slab(2 * slabs + n)
                    texts.append((tp[from_t, first], ip[from_i, second], ip[from_i, third], kept, dct[at_t, first]))
                    images.append((ip[from_i, first], tp[from_t, second], tp[from_t, third], text_keys, dci[at_i, first]))
                results = zip(attend_back_all(texts, 128), attend_back_all(images, 128))
                for n, (text, image) in enumerate(results):
                    first, second, third = slab(n), slab(slabs + n), slab(2 * slabs + n)
                    dtp[at_t, first], dip[at_i, second], dip[at_i, third] = text
                    dip[at_i, first], dtp[at_t, second], dtp[at_t, third] = image
            return carry

        lax.fori_loop(0, half, each, 0, unroll=True)
        leave.go(dtp_own, dtp_other, dip_own, dip_other)
        for late, triples in (
            (weights[0], ((dtp_own, dxt_own), (dtp_other, dxt_other))),
            (weights[1], ((dip_own, dxi_own), (dip_other, dxi_other))),
        ):
            for dp, dx in triples:
                total = times_back(dp[:, pl.ds(0, width)], late.get()[0])
                for slot in range(1, 3):
                    total += times_back(dp[:, pl.ds(slot * width, width)], late.get()[slot])
                dx[...] = total
                leave.go(dx)
        leave.finish()


def round_up(value, step):
    return -(-value // step) * step


class Layout:
    def __init__(self, blocks, weights, firsts=None):
        self.blocks, self.weights = blocks, weights
        self.sizes = [0, 0]
        self.units = []
        self.after = {}
        for index, (name, depth, width) in enumerate(weights):
            real = depth // blocks
            for unit in range(width // UNIT):
                way = 0 if self.sizes[0] <= self.sizes[1] else 1
                if firsts:
                    way = 0 if unit < firsts[name] else 1
                self.units.append((index, unit, way, self.sizes[way], real))
                self.sizes[way] += round_up(real, 16)
            self.after[name] = list(self.sizes)


def pack_body(layout, chosen, kinds, later, info, *refs):
    blocks, weights = layout.blocks, layout.weights
    place = info[2]
    arrays = 1 + max(max(k[0], k[2] or 0) for k in kinds)
    sources, refs = refs[:arrays], refs[arrays + later :]
    targets, refs = refs[: 2 * blocks], refs[2 * blocks :]
    buffers, refs = refs[: len(kinds)], refs[len(kinds) :]
    outs, (total, signals, out_signals) = refs[: 2 * blocks], refs[2 * blocks :]
    waits = []
    for number, (first, column, second, other) in enumerate(kinds):
        buffer = buffers[number]

        def copy(source, start):
            view = sources[source].at[:, pl.ds(start, buffer.shape[1])]
            return pltpu.make_async_copy(view, buffer, signals.at[number])

        if second is None:
            copy(first, column).start()
        else:
            pl.when(info[0] == 1)(copy(first, column).start)
            pl.when(info[0] == 0)(copy(second, other).start)
        waits.append(copy(first, column))
    position, copies = 0, []
    for index, (name, depth, width) in enumerate(weights):
        if name not in chosen:
            continue
        mine = buffers[position : position + chosen[name]]
        for wait in waits[position : position + chosen[name]]:
            wait.wait()
        position += chosen[name]
        span = TILE if width % TILE == 0 else UNIT
        units = [unit for unit in layout.units if unit[0] == index]
        for column in range(0, width, span):
            area = pl.ds(column, span)
            if chosen[name] == 1:
                total[0:depth, 0:span] = mine[0][:, area].astype(total.dtype)
            else:
                x0, x1, y0, y1 = mine
                product = back_times(x0[...], y0[:, area]) + back_times(x1[...], y1[:, area])
                total[0:depth, 0:span] = product.astype(total.dtype)
            for unused, unit, way, row, real in units:
                inside = unit * UNIT - column
                if not 0 <= inside < span:
                    continue
                rows = round_up(real, 16)
                for hop in range(blocks):
                    block = lax.rem(place + (blocks - hop if way == 0 else hop), blocks)
                    source = pl.ds(pl.multiple_of(block * real, math.gcd(real, 16)), rows)
                    outs[way * blocks + hop][row : row + rows, :] = total[
                        source, inside : inside + UNIT
                    ].astype(LOW)
        for way in range(2):
            rows = [(unit[3], unit[3] + round_up(unit[4], 16)) for unit in units if unit[2] == way]
            if not rows:
                continue
            part = pl.ds(rows[0][0], rows[-1][1] - rows[0][0])
            for hop in range(blocks):
                number = way * blocks + hop
                out = pltpu.make_async_copy(
                    outs[number].at[part], targets[number].at[part], out_signals.at[len(copies)]
                )
                out.start()
                copies.append(out)
    for out in copies:
        out.wait()


def pack(layout, factors, info, name, former=None):
    blocks = layout.blocks
    outputs = [shape_of(layout.sizes[way], UNIT) for way in range(2) for hop in range(blocks)]
    deepest = max(weight[1] for weight in layout.weights) + 32
    arrays, kinds, buffers, work = [], [], [], 0
    even = all(weight[1] // blocks % 16 == 0 for weight in layout.weights)

    def number_of(array):
        for number, one in enumerate(arrays):
            if one is array:
                return number
        arrays.append(array)
        return len(arrays) - 1

    for weight in layout.weights:
        for first, second, columns in factors.get(weight[0], ()):
            if isinstance(first, tuple):
                kind = (number_of(first[0]), first[1], number_of(second[0]), second[1])
                array = first[0]
            else:
                kind = (number_of(first), second, None, None)
                array = first
            kinds.append(kind)
            buffers.append(pltpu.VMEM((array.shape[0], columns), array.dtype))
        if weight[0] in factors:
            work += 4 * factors[weight[0]][0][0].shape[0] * weight[1] * weight[2] if len(factors[weight[0]]) > 1 and not isinstance(factors[weight[0]][0][0], tuple) else 800 * weight[1] * weight[2]
    chosen = {name: len(value) for name, value in factors.items()}
    former = tuple(former[0]) + tuple(former[1]) if former else ()
    anywhere = pl.BlockSpec(memory_space=pl.ANY)
    moved = sum(math.prod(v.shape) * 2 for v in outputs) * 2
    outs = pl.pallas_call(
        functools.partial(pack_body, layout, chosen, kinds, len(former)),
        out_shape=tuple(outputs),
        in_specs=[pl.BlockSpec(memory_space=pltpu.SMEM)] + [anywhere] * (len(arrays) + len(former)),
        out_specs=tuple([anywhere] * len(outputs)),
        scratch_shapes=buffers
        + [pltpu.VMEM(v.shape, v.dtype) for v in outputs]
        + [
            pltpu.VMEM((deepest, TILE), LOW if even else FULL),
            pltpu.SemaphoreType.DMA((len(buffers),)),
            pltpu.SemaphoreType.DMA((2 * blocks * len(chosen),)),
        ],
        input_output_aliases={1 + len(arrays) + n: n for n in range(len(former))},
        compiler_params=pltpu.CompilerParams(vmem_limit_bytes=ROOM),
        cost_estimate=pl.CostEstimate(flops=work, bytes_accessed=moved, transcendentals=0),
        name=name,
    )(info, *arrays, *former)
    return [list(outs[:blocks]), list(outs[blocks:])]


def unpack_body(moves, shapes, blocks, later, info, *refs):
    sources = len(shapes)
    inputs, refs = refs[:sources], refs[sources:]
    if later:
        refs = refs[later:]
    count = len(refs) - sources - 1
    outs, wide_refs, signals = refs[:count], refs[count : count + sources], refs[-1]
    place = info[2]
    copies = []
    for source, wide_ref in zip(inputs, wide_refs):
        wide_ref[...] = source[...].astype(FULL)
    for number, (source, way, hop, row, real, target, slot, column, columns, mark) in enumerate(moves):
        block = lax.rem(place + (blocks - hop if way == 0 else hop), blocks)
        rows = pl.ds(pl.multiple_of(block * real, 8), real)
        area = pl.ds(column, columns)
        out = outs[target]
        view = out.at[rows, area] if slot is None else out.at[slot, rows, area]
        copy = pltpu.make_async_copy(
            wide_refs[source].at[pl.ds(row, real), pl.ds(0, columns)], view, signals.at[number]
        )
        wanted = None
        if mark:
            wanted = info[0] == (1 if mark == 1 else 0)
        depth = out.shape[-2]
        if depth < blocks * real:
            inside = block * real < depth
            wanted = inside if wanted is None else jnp.logical_and(wanted, inside)
        copies.append((copy, wanted))
    for step in ("start", "wait"):
        for copy, wanted in copies:
            if wanted is None:
                getattr(copy, step)()
            else:
                pl.when(wanted)(getattr(copy, step))


def unpack(moves, inputs, outputs, former, blocks, info):
    spec = pl.BlockSpec(memory_space=pl.ANY)
    whole = pl.BlockSpec(memory_space=pltpu.VMEM)
    former = tuple(former or ())
    inputs = tuple(inputs)
    rows = [value.shape[0] for value in inputs]
    return pl.pallas_call(
        functools.partial(unpack_body, moves, rows, blocks, len(former)),
        out_shape=tuple(jax.ShapeDtypeStruct(shape, FULL) for shape in outputs),
        in_specs=[pl.BlockSpec(memory_space=pltpu.SMEM)] + [whole] * len(inputs) + [spec] * len(former),
        out_specs=tuple([spec] * len(outputs)),
        scratch_shapes=[pltpu.VMEM((count, UNIT), FULL) for count in rows]
        + [pltpu.SemaphoreType.DMA((len(moves),))],
        input_output_aliases={1 + len(inputs) + n: n for n in range(len(former))},
        compiler_params=pltpu.CompilerParams(vmem_limit_bytes=ROOM),
        cost_estimate=pl.CostEstimate(flops=0, bytes_accessed=6 * sum(rows) * UNIT, transcendentals=0),
        name="unpack",
    )(info, *inputs, *former)


CORES = [(0, 1), (1, 0)]


def to_other_core(values):
    return lax.ppermute(values, "tensor", CORES)


def to_other_section(values):
    return lax.ppermute(values, "section", CORES)


def to_layer(values, layer):
    return lax.ppermute(values, "section", [(1 - layer, layer)])


def ring_order():
    places = list(range(lax.axis_size("dp")))
    return places[0::2] + places[1::2][::-1]


def ring_place():
    place, count = lax.axis_index("dp"), lax.axis_size("dp")
    return jnp.where(place % 2 == 0, place // 2, count - 1 - place // 2)


def to_next(values, way):
    order = ring_order()
    route = list(zip(order, order[1:] + order[:1]))
    if way == 1:
        route = [(there, here) for here, there in route]
    return lax.ppermute(values, "dp", route)


def after(values, token):
    if token is None:
        return values
    return lax.optimization_barrier((values, token))[0]


class Ring:
    def __init__(self, parts):
        self.parts = parts
        self.count = len(parts[0])
        self.pieces = [[None] * self.count, [None] * self.count]
        self.step = 0
        self.last = 2 * (self.count - 1)
        self.flying = [to_next(parts[way][1], way) for way in range(2)]

    def advance(self, token):
        got = [after(self.flying[0], token), after(self.flying[1], token)]
        turn, count = self.step, self.count
        self.step += 1
        if turn < count - 1:
            got = [got[way] + self.parts[way][(turn + 2) % count] for way in range(2)]
        hop = max(turn - (count - 2), 0)
        if turn >= count - 2:
            for way in range(2):
                self.pieces[way][hop] = got[way]
        if self.step < self.last:
            self.flying = [to_next(got[way], way) for way in range(2)]
        return tuple(got), (hop if turn >= count - 2 else None)


def shards(
    text_stream,
    image_stream,
    region_mask,
    co_text_in,
    co_text_out,
    self_text_in,
    self_text_out,
    image_attn_in,
    image_attn_out,
    text_up,
    text_down,
    image_up,
    image_down,
    text_gain,
    text_shift,
    image_gain,
    image_shift,
):
    front = lax.axis_index("section") == 0
    core = lax.axis_index("tensor")
    blocks = lax.axis_size("dp")
    in_ring = blocks == 8
    place = ring_place() if in_ring else 0 * core
    info = jnp.stack([front.astype(jnp.int32), core.astype(jnp.int32), place.astype(jnp.int32)])
    pairs = text_stream.shape[1]
    half = pairs // 2
    real_t, real_i = text_stream.shape[2], image_stream.shape[2]
    rows_t, rows_i = round_up(real_t, 16), round_up(real_i, 16)
    wide_t, wide_i = text_stream.shape[3], image_stream.shape[3]
    text_size = D_TEXT // HEADS_TEXT
    image_size = D_IMAGE // HEADS_IMAGE

    def flat_rows(values, rows):
        grown = jnp.pad(values, ((0, 0), (0, rows - values.shape[1]), (0, 0)))
        return grown.reshape(values.shape[0] * rows, values.shape[2])

    def by_slot(weight):
        return jnp.transpose(weight, (1, 0, 2))

    own_t, own_i = half * rows_t, half * rows_i
    all_t, all_i = pairs * rows_t, pairs * rows_i
    keep = jnp.pad(region_mask, ((0, 0), (0, rows_i - real_i))).reshape(pairs, 1, rows_i)
    gain_t, shift_t, gain_i, shift_i = text_gain[0], text_shift[0], image_gain[0], image_shift[0]
    cross_in, image_in, single_in = by_slot(co_text_in), by_slot(image_attn_in[0]), by_slot(self_text_in)
    image_out, up_i, down_i = image_attn_out[0], image_up[0], image_down[0]
    up_t, down_t = text_up[0], text_down[0]
    image_out_2, cross_out_2 = to_other_core(image_out), to_other_core(co_text_out)
    up_i_2, down_i_2 = to_other_core(up_i), to_other_core(down_i)
    up_t_2, down_t_2 = to_other_core(up_t), to_other_core(down_t)
    cross = cross_in.shape[2]
    single = single_in.shape[2]
    ff_t, ff_i = up_t.shape[1], up_i.shape[1]
    tail_t = (up_t, down_t, up_t_2, down_t_2)
    tail_i = (up_i, down_i, up_i_2, down_i_2)

    far = (cross_in, image_in)
    xt_own, xt_other, xi_own, xi_other, tp, ip, ct_own, ct_give, ci_own, ci_give = launch(
        functools.partial(cross_forward, pairs, rows_t, rows_i, real_t),
        [shape_of(own_t, wide_t)] * 2
        + [shape_of(own_i, wide_i)] * 2
        + [shape_of(all_t, 3 * cross), shape_of(all_i, 3 * cross)]
        + [shape_of(own_t, cross)] * 2
        + [shape_of(own_i, cross)] * 2,
        (flat_rows(text_stream[0], rows_t), flat_rows(image_stream[0], rows_i), keep),
        far=far,
        scratch=[pltpu.VMEM((all_t, wide_t), LOW), pltpu.VMEM((all_i, wide_i), LOW)] + buffers_for(far),
        flag=info,
        work=6 * cross * (all_t * wide_t + all_i * wide_i),
        name="cross_forward",
    )
    ct_other, ci_other = ct_give, ci_give
    ci_2 = to_other_core(ci_give)
    ct_2 = to_other_core(ct_give)

    def run_first_tail(x, c0, c1, o0, o1, gain, shift, ff, rows, width, hidden, name):
        low_w, low_h = shape_of(rows, width), shape_of(rows, hidden)
        far = (o0, o1) + ff
        return launch(
            first_tail,
            [low_w, low_w, low_h, low_h]
            + [shape_of(rows, hidden)] * 2
            + [shape_of(rows, width), shape_of(rows, 128, FULL)] * 2,
            (x, c0, c1, gain, shift),
            far=far,
            scratch=[pltpu.VMEM((rows, width), FULL)] + buffers_for(far),
            flag=info,
            work=4 * rows * width * (o0.shape[0] + 2 * hidden),
            name=name,
        )

    bi, yi, hi0, hi1, si0, si1, ni1, ii1, ni2, ii2 = run_first_tail(
        after(xi_own, (up_t_2, down_t_2, cross_out_2, ct_2)), ci_own, ci_2, image_out, image_out_2, gain_i, shift_i,
        tail_i, own_i, wide_i, ff_i, "tail_i"
    )
    image_in_2, single_in_2, single_out_2 = [
        to_other_core(after(value, bi)) for value in (image_in, single_in, self_text_out)
    ]
    bi_here, bi = bi, to_layer(bi, 1)
    bt, yt, ht0, ht1, st0, st1, nt1, it1, nt2, it2 = run_first_tail(
        after(xt_own, bi_here), ct_own, ct_2, co_text_out, cross_out_2, gain_t, shift_t, tail_t, own_t, wide_t, ff_t, "tail_t"
    )

    def run_self(rows, real, size, width, hidden, x, w0, w1, masked, o0, o1, gain, shift, ff, seed, y, h0, h1, c, name):
        count = half * rows
        inner = w0.shape[2]
        low_w, low_h = shape_of(count, width), shape_of(count, hidden)
        outputs = [low_w, low_w, shape_of(count, cross), shape_of(count, 3 * cross)]
        outputs += [low_w, low_w, low_h, low_h, low_w, low_h] + [shape_of(2, width, FULL)] * 2
        outputs += [shape_of(count, 2 * width + hidden + 4 * cross)]
        scratch = [pltpu.VMEM((count, 3 * inner), LOW)] * 2
        scratch += [pltpu.VMEM((count, hidden), FULL)] * 2
        scratch += [pltpu.VMEM((count, width), FULL), pltpu.VMEM((count, 128), FULL)] * 2
        scratch += [pltpu.VMEM((count, width), FULL)] + [pltpu.VMEM((count, inner), LOW)] * 2
        scratch += [pltpu.VMEM((count, columns), LOW) for columns in (hidden, cross, 3 * cross)]
        weights = (w0, w1, o0, o1) + ff
        return launch(
            functools.partial(self_layer, masked, half, rows, real, size, cross),
            outputs,
            (x, seed, gain, shift, keep),
            far=weights + (y, h0, h1, c),
            scratch=scratch + buffers_for(weights),
            flag=info,
            work=8 * count * width * (4 * inner + 2 * hidden),
            name=name,
        )

    i2 = run_self(
        rows_i, real_i, image_size, wide_i, ff_i, bi, image_in, image_in_2, True, image_out, image_out_2,
        gain_i, shift_i, tail_i, xi_own, yi, hi0, hi1, ci_own, "self_i",
    )
    seed_i = to_layer(i2[1], 0)
    bt = to_layer(bt, 1)
    t2 = run_self(
        rows_t, real_t, text_size, wide_t, ff_t, after(bt, i2[1]), single_in, single_in_2, False,
        self_text_out, single_out_2, gain_t, shift_t, tail_t, xt_own, yt, ht0, ht1, ct_own, "self_t",
    )
    seed_t = to_layer(t2[1], 0)
    (oi, unused, ci_own, pi_own, dai, dfi, dui0, dui1, yi, hi0, dgi, dsi, give_i) = i2
    (ot, unused, ct_own, pt_own, dat, dft, dut0, dut1, yt, ht0, dgt, dst, give_t) = t2
    left_t, left_i = to_other_core(give_t), to_other_core(give_i)

    def run_tail_back(seed, kept, o0, o1, gain, ff, given, rows, width, hidden, name):
        low_w, low_h = shape_of(rows, width), shape_of(rows, hidden)
        outputs = [low_w, low_h, low_w] + [shape_of(2, width, FULL)] * 2
        outputs += [shape_of(rows, width, FULL), shape_of(rows, cross)]
        outputs += [shape_of(rows, 2 * width + hidden + cross)]
        s0, s1, n1, i1, n2, i2 = kept
        u0, d0, u1, d1 = ff
        late = (n2, i2, d0, s0, u0, d1, s1, u1, n1, i1, o0, o1)
        return launch(
            first_tail_back,
            outputs,
            (seed, gain),
            far=late + given,
            scratch=[pltpu.VMEM((rows, hidden), LOW)] + buffers_for(late),
            flag=info,
            work=4 * rows * width * (cross + 2 * hidden),
            name=name,
        )


    def choose(first, second):
        return jnp.where(front, first, second)

    ff_layout = Layout(
        blocks,
        [
            ("down_t", ff_t, wide_t),
            ("up_t", wide_t, ff_t),
            ("up_i", wide_i, ff_i),
            ("down_i", ff_i, wide_i),
        ],
        {"down_t": 1, "up_t": 3, "up_i": 2, "down_i": 1},
    )
    attn_layout = Layout(
        blocks,
        [
            ("in_t", wide_t, 3 * cross),
            ("out_t", cross, wide_t),
            ("in_i", wide_i, 3 * cross),
            ("out_i", cross, wide_i),
            ("small", blocks * 16, UNIT),
        ],
    )
    text_rows = attn_layout.after["out_t"]

    out = run_tail_back(
        seed_i, (si0, si1, ni1, ii1, ni2, ii2), image_out, image_out_2, gain_i, tail_i,
        (dfi, dui0, dui1, dai, dgi, dsi), own_i, wide_i, ff_i, "tail_back_i",
    )
    dfi, dui0, dai, dgi, dsi, dri, dci_own, give_i = out
    right_i = to_other_core(give_i)
    out = run_tail_back(
        after(seed_t, dci_own), (st0, st1, nt1, it1, nt2, it2), co_text_out, cross_out_2, gain_t, tail_t,
        (dft, dut0, dut1, dat, dgt, dst), own_t, wide_t, ff_t, "tail_back_t",
    )
    dft, dut0, dat, dgt, dst, drt, dct_own, give_t = out
    right_t = to_other_core(give_t)
    small = jnp.concatenate([dgt, dst, dgi, dsi], axis=1)
    small = small + to_other_core(small)
    small_rows = round_up(-(-small.size // UNIT), blocks) // blocks
    small = jnp.pad(small.reshape(-1), (0, blocks * small_rows * UNIT - small.size))
    small = small.reshape(blocks, small_rows, UNIT)
    small = jnp.pad(small, ((0, 0), (0, 16 - small_rows), (0, 0))).reshape(blocks * 16, UNIT)
    ff_parts = pack(
        ff_layout,
        {
            "down_t": ((ht0, 0, ff_t), (left_t, wide_t, ff_t), (after(dft, small), 0, wide_t), (right_t, 0, wide_t)),
            "up_t": ((yt, 0, wide_t), (left_t, 0, wide_t), (dut0, 0, ff_t), (right_t, wide_t, ff_t)),
            "up_i": ((yi, 0, wide_i), (left_i, 0, wide_i), (dui0, 0, ff_i), (right_i, wide_i, ff_i)),
            "down_i": ((hi0, 0, ff_i), (left_i, wide_i, ff_i), (dfi, 0, wide_i), (right_i, 0, wide_i)),
        },
        info,
        "pack_ff",
    )
    token = ff_parts[0][1]
    ff = Ring(ff_parts) if in_ring else None
    far = (cross_in, image_in)
    out = launch(
        functools.partial(cross_backward, (wide_t, wide_i), pairs, rows_t, rows_i, real_t),
        [shape_of(own_t, 3 * cross)] * 2
        + [shape_of(own_i, 3 * cross)] * 2
        + [shape_of(own_t, wide_t, FULL)] * 2
        + [shape_of(own_i, wide_i, FULL)] * 2,
        (after(tp, token), ip, dct_own, dci_own, keep),
        far=far + (right_t, right_i, pt_own, left_t, pi_own, left_i),
        scratch=[pltpu.VMEM(v.shape, v.dtype) for v in far]
        + [pltpu.VMEM((own_t, cross), LOW), pltpu.VMEM((own_i, cross), LOW), pltpu.SemaphoreType.DMA((4,))],
        flag=info,
        work=6 * cross * (all_t * wide_t + all_i * wide_i),
        name="cross_backward",
    )
    dtp_own, dtp_other, dip_own, dip_other, dxt_own, dxt_give, dxi_own, dxi_give = out
    token = dtp_own
    if in_ring:
        token, unused = ff.advance(token)

    def columns(part, wide, hidden):
        starts = {"c": wide + hidden, "x": wide + hidden + 4 * cross}
        return starts[part]

    ct_column, xt_column = columns("c", wide_t, ff_t), columns("x", wide_t, ff_t)
    ci_column, xi_column = columns("c", wide_i, ff_i), columns("x", wide_i, ff_i)
    attn_parts = pack(
        attn_layout,
        {
            "in_t": (
                ((xt_own, 0), (bt, 0), wide_t),
                ((xt_other, 0), (left_t, xt_column), wide_t),
                (after(dtp_own, token), 0, 3 * cross),
                (dtp_other, 0, 3 * cross),
            ),
            "out_t": (
                (ct_own, 0, cross),
                ((ct_give, 0), (left_t, ct_column), cross),
                (dat, 0, wide_t),
                (right_t, wide_t + ff_t, wide_t),
            ),
            "in_i": (
                ((xi_own, 0), (bi, 0), wide_i),
                ((xi_other, 0), (left_i, xi_column), wide_i),
                (dip_own, 0, 3 * cross),
                (dip_other, 0, 3 * cross),
            ),
        },
        info,
        "pack_attention",
    )
    token = attn_parts[0][1]
    if in_ring:
        token, unused = ff.advance(token)
    attn_parts = pack(
        attn_layout,
        {
            "out_i": (
                (ci_own, 0, cross),
                ((ci_give, 0), (left_i, ci_column), cross),
                (after(dai, token), 0, wide_i),
                (right_i, wide_i + ff_i, wide_i),
            ),
            "small": ((small, 0, UNIT),),
        },
        info,
        "pack_rest",
        attn_parts,
    )

    def choose(first, second):
        return jnp.where(front, first, second)

    def result(rest, partial, other, output, rows, real, token):
        mine = choose(rest + partial + after(to_other_core(other), token), output.astype(FULL))
        mine = mine.astype(LOW).reshape(half, rows, -1)[:, :real]
        got = to_other_core(mine)
        return jnp.concatenate(
            [jnp.where(core == 0, mine, got), jnp.where(core == 0, got, mine)], axis=0
        )[None]

    main_shapes = [
        (ff_t, wide_t),
        (wide_t, ff_t),
        (wide_i, ff_i),
        (ff_i, wide_i),
        (3, wide_i, cross),
        (cross, wide_i),
        (blocks * 16, UNIT),
    ]
    text_shapes = [(3, wide_t, cross), (cross, wide_t), (3, wide_t, single), (self_text_out.shape[0], wide_t)]
    main_moves, text_moves = [], []

    def move(target, source, way, row, real, unit, output, shape, mark=0):
        slot, column, columns = None, unit * UNIT, UNIT
        if len(shape) == 3:
            slot, column = column // cross, column % cross
            columns = min(UNIT, shape[2] - column)
        if columns > 0:
            target.append((source, way, row, real, output, slot, column, columns, mark))

    for index, unit, way, row, real in ff_layout.units:
        move(main_moves, way, way, row, real, unit, index, main_shapes[index])
    for index, unit, way, row, real in attn_layout.units:
        if index >= 2:
            move(main_moves, 2 + way, way, row, real, unit, index + 2, main_shapes[index + 2])
        else:
            for mark in (1, 2):
                move(text_moves, way + 2 * (mark - 1), way, row, real, unit, index, text_shapes[index], mark)
                move(text_moves, way + 4 - 2 * mark, way, row, real, unit, index + 2, text_shapes[index + 2], mark)

    main, text = None, None

    def shifted(moves, hop, source_shift, row_shift):
        result = []
        for source, way, row, *rest in moves:
            result.append((source_shift(source), way, hop, row + row_shift(source), *rest))
        return result

    def spread_main(hops, ff, attn, main):
        inputs, moves = [], []
        for number, hop in enumerate(hops):
            inputs += [ff[0][hop], ff[1][hop], attn[0][hop], attn[1][hop]]
            moves += shifted(main_moves, hop, lambda source: source + 4 * number, lambda source: 0)
        return unpack(moves, inputs, main_shapes, main, blocks, info)

    def spread_text(hops, attn, crossed, text):
        inputs, moves, both = [], [], text_rows[0] + text_rows[1]
        for hop in hops:
            inputs += [attn[0][hop], attn[1][hop]]
        places = []
        for array in crossed:
            places += [(len(inputs), row) for row in range(0, array.shape[0], both)]
            inputs.append(array)
        for number, hop in enumerate(hops):
            moves += shifted(
                text_moves,
                hop,
                lambda source: source + 2 * number if source < 2 else places[number][0],
                lambda source: 0 if source < 2 else places[number][1] + (source - 2) * text_rows[0],
            )
        return unpack(moves, inputs, text_shapes, text, blocks, info)

    def cross_over(attn, hops):
        return to_other_section(
            jnp.concatenate([attn[way][hop][: text_rows[way]] for hop in hops for way in range(2)], axis=0)
        )

    if in_ring:
        attn = Ring(attn_parts)
        token = attn_parts[0][1]
        results = (
            result(drt, dxt_own, dxt_give, ot, rows_t, real_t, token),
            result(dri, dxi_own, dxi_give, oi, rows_i, real_i, token),
        )
        token = (token, results)
        groups = [(0, 1), (2, 3), (4, 5), (6,), (7,)]
        crossed = [None] * len(groups)
        while attn.step < attn.last:
            if ff.step < ff.last:
                token, unused = ff.advance(token)
            token, hop = attn.advance(token)
            if hop is None:
                continue
            if hop == 2:
                first = after(crossed[0], token)
                relay = [to_next(first[: text_rows[0]], 1), to_next(first[text_rows[0] : sum(text_rows)], 0)]
            if hop == 4:
                crossed[-1] = jnp.concatenate([after(value, token) for value in relay], axis=0)
                token = (token, crossed[-1])
            for number, group in enumerate(groups):
                if hop == group[-1]:
                    if number < len(groups) - 1:
                        crossed[number] = cross_over(attn.pieces, group)
                    main = spread_main(group, ff.pieces, attn.pieces, main)
                    token = (token, main)
                elif number and hop == group[0] and len(group) > 1:
                    text = spread_text(groups[number - 1], attn.pieces, [crossed[number - 1]], text)
                    token = (token, text)
        text = spread_text(groups[-3], attn.pieces, crossed[-3:-2], text)
        text = spread_text((6, 7), attn.pieces, crossed[-2:], text)
    else:
        results = (
            result(drt, dxt_own, dxt_give, ot, rows_t, real_t, token),
            result(dri, dxi_own, dxi_give, oi, rows_i, real_i, token),
        )
        ff, attn = lax.psum((ff_parts, attn_parts), "dp")
        for hop in range(0, blocks, 2):
            main = spread_main((hop, hop + 1), ff, attn, main)
            text = spread_text((hop, hop + 1), attn, [cross_over(attn, (hop, hop + 1))], text)
    down_t_grad, up_t_grad, up_i_grad, down_i_grad, in_i_grad, out_i_grad, small = main
    co_in_grad, co_out_grad, self_in_grad, self_out_grad = text
    small = small.reshape(blocks, 16, UNIT)[:, :small_rows].reshape(-1)[: 4 * (wide_t + wide_i)]
    small = small.reshape(2, 2 * (wide_t + wide_i))
    small = jnp.split(small, [wide_t, 2 * wide_t, 2 * wide_t + wide_i], axis=1)

    return (
        results[0],
        results[1],
        by_slot(co_in_grad),
        co_out_grad,
        by_slot(self_in_grad),
        self_out_grad,
        by_slot(in_i_grad)[None],
        out_i_grad[None],
        up_t_grad[None],
        down_t_grad[None],
        up_i_grad[None],
        down_i_grad[None],
        small[0][None],
        small[1][None],
        small[2][None],
        small[3][None],
    )


def solution(mesh):
    in_specs = (
        P("section", "dp", None, None),
        P("section", "dp", None, None),
        P("dp", None),
        P(None, None, "tensor"),
        P("tensor", None),
        P(None, None, "tensor"),
        P("tensor", None),
        P("section", None, None, "tensor"),
        P("section", "tensor", None),
        P("section", None, "tensor"),
        P("section", "tensor", None),
        P("section", None, "tensor"),
        P("section", "tensor", None),
        P("section", None, None),
        P("section", None, None),
        P("section", None, None),
        P("section", None, None),
    )
    out_specs = (
        P("section", "dp", None, None),
        P("section", "dp", None, None),
        P(None, None, "tensor"),
        P("tensor", None),
        P(None, None, "tensor"),
        P("tensor", None),
        P("section", None, None, "tensor"),
        P("section", "tensor", None),
        P("section", None, "tensor"),
        P("section", "tensor", None),
        P("section", None, "tensor"),
        P("section", "tensor", None),
        P("section", None, None),
        P("section", None, None),
        P("section", None, None),
        P("section", None, None),
    )
    return jax.shard_map(shards, mesh=mesh, in_specs=in_specs, out_specs=out_specs, check_vma=False)
```
